32 devices in a mesh: cam: 8 (over y, x, core), head: 4 (over z).
Axes of the slice: x: 2, y: 2, z: 4, core: 2. Of those that a mesh axis runs over, the one named last changes fastest.
Arguments:
- queries: bfloat16 [16384, 1024], P('cam', 'head'), may hold values from -24 to 24
- keys: bfloat16 [16384, 1024], P('cam', 'head'), may hold values from -24 to 24
- values: bfloat16 [16384, 1024], P('cam', 'head'), may hold values from -6 to 6
- rates: float32 [16384, 4], P('cam', 'head'), may hold values from 0.1 to 1
- w_one: bfloat16 [4, 256, 256], P('head'), may hold values from -0.375 to 0.375
- w_three: bfloat16 [4, 256, 256], P('head'), may hold values from -0.375 to 0.375
- w_two: bfloat16 [4, 256, 256], P('head'), may hold values from -0.375 to 0.375
- gain: float32 [1024], P('head'), may hold values from 0.5 to 1.5
- order: int32 [8, 2048], P('cam'), may hold values from 0 to 2047, as said below
Outputs:
- mixed: bfloat16 [16384, 1024], P('cam', 'head')
The draws below stay inside these ranges and needn't reach their ends.
Inputs may be any that keep to these rules, and one draw needn't show every extreme that they name: `order`: each row is an ordering of 0 to 2047; every timestamp holds exactly 32 tokens of every camera.
All inputs are finite; a program needn't handle non-finite values.
Results may differ from the reference program's by a relative error of at most 0.0085.
Values may be sent and summed in bfloat16 or wider, within the bound.
No kernel may reach another device: no remote copies, remote signals or barrier semaphores. Data moves between devices by JAX's collectives and lax.ppermute only.
A program may use at most 64 MiB of HBM per device.

```python
import math
import jax
import jax.numpy as jnp
from jax import lax

HD = 256
HID = 256
FRAMES = 64
PATCHES = 32
HEADS = 4
D = 1024
CAMERAS = 8
TOK_DEV = 2048
TOKENS = 16384


def order_table(key):
    keys_all = jax.random.split(jax.random.fold_in(key, 11), CAMERAS)
    table = jax.vmap(lambda single: jax.random.permutation(single, TOK_DEV))(keys_all)
    return table.astype(jnp.int32)


def paired_draw(key, which):
    own_key = jax.random.fold_in(key, 20 + which)
    result = jnp.clip(jax.random.normal(own_key, (CAMERAS, TOK_DEV, D), jnp.float32), -6.0, 6.0)
    return result.reshape(TOKENS, D).astype(jnp.bfloat16)


def draw_queries(key, part):
    return paired_draw(key, 0)


def draw_keys(key, part):
    return paired_draw(key, 1)


def draw_order(key, part):
    return order_table(key)


def block_scale(stream_key, shape, cuts, least, largest):
    def one(axis_at, blocks):
        steps = jax.random.uniform(jax.random.fold_in(jax.random.fold_in(stream_key, 6), axis_at), (blocks,), jnp.float32, least / len(cuts), largest / len(cuts))
        return jnp.repeat(jnp.exp(steps), shape[axis_at] // blocks).reshape((-1,) + (1,) * (len(shape) - axis_at - 1))

    factor_of = one(*cuts[0])
    for cut in cuts[1:]:
        factor_of = factor_of * one(*cut)
    return factor_of


def normal_values(key, shape, width, most, pieces=(), kind=jnp.bfloat16):
    values = jax.random.normal(key, shape, jnp.float32) * width
    if len(pieces) > 0:
        values = block_scale(key, shape, pieces, -0.22, 0.18) * values
    return jnp.clip(values, min=-most, max=most).astype(kind)


def setup_inputs(seed: int = 0) -> dict:
    streams_of = jax.random.split(jax.random.key(seed), 10)
    queries = draw_queries(jax.random.fold_in(streams_of[9], 71), 0)
    keys = draw_keys(jax.random.fold_in(streams_of[9], 71), 0)
    values = normal_values(streams_of[2], (TOKENS, D), 1.0, 6.0, ((0, 8), (1, 4)))
    rates = jnp.clip(jnp.exp(math.log(1.0) - 2.3025851 * jax.random.uniform(streams_of[3], (TOKENS, HEADS), jnp.float32) ** block_scale(streams_of[3], (TOKENS, HEADS), ((0, 8), (1, 4)), -0.2, 0.2)), 0.1, 1.0)
    w_one = normal_values(streams_of[4], (HEADS, HID, HD), HD ** -0.5, 0.375, ((0, 4),))
    w_three = normal_values(streams_of[5], (HEADS, HID, HD), HD ** -0.5, 0.375, ((0, 4),))
    w_two = normal_values(streams_of[6], (HEADS, HD, HID), HID ** -0.5, 0.375, ((0, 4),))
    gain = jnp.clip(1.0 + 0.1 * jax.random.normal(streams_of[7], (D,), jnp.float32), 0.5, 1.5)
    order = draw_order(jax.random.fold_in(streams_of[9], 71), 0)
    return dict(queries=queries, keys=keys, values=values, rates=rates, w_one=w_one, w_three=w_three, w_two=w_two, gain=gain, order=order)


EPSILON = 1e-06

def renew(weight, grad):
    wf = weight.astype(jnp.float32)
    scale = jnp.sqrt(jnp.mean(wf * wf)) / jnp.sqrt(jnp.mean(grad * grad) + EPSILON)
    moved = wf - scale * grad
    ratio = jnp.sqrt(lax.optimization_barrier(jnp.sum(wf * wf, axis=-1, keepdims=True))) / jnp.sqrt(lax.optimization_barrier(jnp.sum(moved * moved, axis=-1, keepdims=True)) + EPSILON)
    return (moved * ratio).astype(jnp.bfloat16)

def reference(queries, keys, values, rates, w_one, w_three, w_two, gain, order):
    inverse = jnp.argsort(order, axis=1).astype(jnp.int32)

    def arrange(data):
        data = data.reshape(CAMERAS, TOK_DEV, HD)
        data = jax.vmap(lambda rows, index: jnp.take(rows, index, axis=0))(data, inverse)
        data = data.reshape(CAMERAS, FRAMES, PATCHES, HD).transpose(1, 0, 2, 3)
        return data.reshape(FRAMES, CAMERAS * PATCHES, HD)

    def restore(data):
        data = data.reshape(FRAMES, CAMERAS, PATCHES, HD).transpose(1, 0, 2, 3).reshape(CAMERAS, TOK_DEV, HD)
        data = jax.vmap(lambda rows, index: jnp.take(rows, index, axis=0))(data, order)
        return data.reshape(TOKENS, HD)

    def attend_frame(block):
        query_rows, key_rows, value_rows = block
        scores = jnp.dot(query_rows, key_rows.T, preferred_element_type=jnp.float32) * HD ** (-0.5)
        scores = scores - lax.optimization_barrier(jnp.max(scores, axis=-1, keepdims=True))
        expo = jnp.exp(scores)
        probs = (expo / lax.optimization_barrier(jnp.sum(expo, axis=-1, keepdims=True))).astype(jnp.bfloat16)
        return jnp.dot(probs, value_rows, preferred_element_type=jnp.float32).astype(jnp.bfloat16)

    def one_head(head):
        start = head * HD
        query = lax.dynamic_slice_in_dim(queries, start, HD, 1)
        key = lax.dynamic_slice_in_dim(keys, start, HD, 1)
        value = lax.dynamic_slice_in_dim(values, start, HD, 1)
        rate = lax.dynamic_slice_in_dim(rates, head, 1, 1)
        first = w_one[head]
        third = w_three[head]
        second = w_two[head]
        h_one = jnp.dot(key, first.T, preferred_element_type=jnp.float32)
        h_three = jnp.dot(key, third.T, preferred_element_type=jnp.float32)
        sigma = jax.nn.sigmoid(h_one)
        active = (h_one * sigma * h_three).astype(jnp.bfloat16)
        error = (-rate * value.astype(jnp.float32)).astype(jnp.bfloat16)
        grad_second = jnp.dot(error.T, active, preferred_element_type=jnp.float32)
        back = jnp.dot(error, second, preferred_element_type=jnp.float32)
        back_one = (back * h_three * sigma * (1.0 + h_one * (1.0 - sigma))).astype(jnp.bfloat16)
        back_three = (back * h_one * sigma).astype(jnp.bfloat16)
        grad_first = jnp.dot(back_one.T, key, preferred_element_type=jnp.float32)
        grad_third = jnp.dot(back_three.T, key, preferred_element_type=jnp.float32)
        new_first = renew(first, grad_first)
        new_third = renew(third, grad_third)
        new_second = renew(second, grad_second)
        q_one = jnp.dot(query, new_first.T, preferred_element_type=jnp.float32)
        q_three = jnp.dot(query, new_third.T, preferred_element_type=jnp.float32)
        q_active = (q_one * jax.nn.sigmoid(q_one) * q_three).astype(jnp.bfloat16)
        readout = jnp.dot(q_active, new_second.T, preferred_element_type=jnp.float32)
        attended = lax.map(attend_frame, (arrange(query), arrange(key), arrange(value)))
        return (readout, restore(attended))
    readouts, attended = lax.map(one_head, jnp.arange(HEADS, dtype=jnp.int32))
    total = lax.optimization_barrier(jnp.sum(readouts * readouts, axis=(0, 2)))
    inv_norm = 1.0 / jnp.sqrt(total / D + EPSILON)
    mixed = readouts * inv_norm[None, :, None] * gain.reshape(HEADS, 1, HD) + attended.astype(jnp.float32)
    return mixed.transpose(1, 0, 2).reshape(TOKENS, D).astype(jnp.bfloat16)
```

```python
import functools

import jax
import jax.numpy as jnp
from jax import lax
from jax.experimental import pallas as pl
from jax.experimental.pallas import tpu as pltpu
from jax.sharding import PartitionSpec as P

PATCHES = 32
EPSILON = 1e-06
LANES = 128
CHUNKS = 2
MIB = 1024 * 1024
F32 = jnp.float32
BF16 = jnp.bfloat16


def dot(a, b):
    return lax.dot_general(a, b, (((1,), (0,)), ((), ())), preferred_element_type=F32)


def dot_bt(a, b):
    return lax.dot_general(a, b, (((1,), (1,)), ((), ())), preferred_element_type=F32)


def dot_at(a, b):
    return lax.dot_general(a, b, (((0,), (0,)), ((), ())), preferred_element_type=F32)


def params():
    return pltpu.CompilerParams(vmem_limit_bytes=40 * MIB)


def full(count):
    return [pl.BlockSpec(memory_space=pltpu.VMEM)] * count


def cost(flops, moved, exps=0):
    return pl.CostEstimate(flops=int(flops), bytes_accessed=int(moved), transcendentals=int(exps))


def power_of_two(n):
    return n & (n - 1) == 0


def peer(me, step, n):
    if power_of_two(n):
        return me ^ step
    ahead = me + step
    return jnp.where(ahead >= n, ahead - n, ahead)


def routes(step, n):
    if power_of_two(n):
        return [(at, at ^ step) for at in range(n)]
    return [(at, (at + step) % n) for at in range(n)]


def column(row):
    return jnp.broadcast_to(row, (LANES, LANES)).T


def sort_kernel(n, start, rows, owned_rows, order_ref, q_ref, k_ref, v_ref, *rest):
    outs, onehot = rest[:n], rest[n]
    me = lax.axis_index("cam")
    count, width = q_ref.shape
    group = onehot.shape[0] // rows
    order = order_ref[...]
    for first in range(0, n, group):
        for at in range(group):
            base = peer(me, first + at, n) * owned_rows + start
            slot = lax.broadcasted_iota(jnp.int32, (rows, count), 0) + base
            onehot[at * rows : (at + 1) * rows, :] = (slot == order).astype(F32).astype(BF16)
        for which, ref in enumerate((q_ref, k_ref, v_ref)):
            picked = dot(onehot[...], ref[...]).astype(BF16)
            for at in range(group):
                outs[first + at][:, which * width : (which + 1) * width] = picked[
                    at * rows : (at + 1) * rows
                ]


def sort_tokens(order, q, k, v, n, start, rows, owned_rows):
    count, width = q.shape
    group = max(1, min(n, 512 // rows))
    while n % group:
        group -= 1
    return pl.pallas_call(
        functools.partial(sort_kernel, n, start, rows, owned_rows),
        out_shape=[jax.ShapeDtypeStruct((rows, 3 * width), BF16)] * n,
        in_specs=full(4),
        out_specs=full(n),
        scratch_shapes=[pltpu.VMEM((group * rows, count), BF16)],
        compiler_params=params(),
        cost_estimate=cost(6 * n * rows * count * width, 6 * count * width),
        name="sort_tokens",
    )(order, q, k, v)


def attend_kernel(n, scale, *refs):
    ins, outs = refs[:n], refs[n : 2 * n]
    q_all, k_all, v_all = refs[2 * n :]
    rows = ins[0].shape[0]
    width = outs[0].shape[1]
    group = n * PATCHES
    block = min(group, 256)
    for stamp in range(rows // PATCHES):
        here = slice(stamp * PATCHES, (stamp + 1) * PATCHES)
        for cam in range(n):
            there = slice(cam * PATCHES, (cam + 1) * PATCHES)
            q_all[there, :] = ins[cam][here, 0:width]
            k_all[there, :] = ins[cam][here, width : 2 * width]
            v_all[there, :] = ins[cam][here, 2 * width : 3 * width]
        for low in range(0, group, block):
            scores = dot_bt(q_all[low : low + block, :], k_all[...]) * scale
            scores = scores - jnp.max(scores, axis=-1, keepdims=True)
            expo = jnp.exp(scores)
            probs = (expo / jnp.sum(expo, axis=-1, keepdims=True)).astype(BF16)
            result = dot(probs, v_all[...]).astype(BF16)
            for cam in range(low // PATCHES, (low + block) // PATCHES):
                at = cam * PATCHES - low
                outs[cam][here, :] = result[at : at + PATCHES]


def attend(blocks, n, width):
    rows = blocks[0].shape[0]
    group = n * PATCHES
    return pl.pallas_call(
        functools.partial(attend_kernel, n, width**-0.5),
        out_shape=[jax.ShapeDtypeStruct((rows, width), BF16)] * n,
        in_specs=full(n),
        out_specs=full(n),
        scratch_shapes=[pltpu.VMEM((group, width), BF16)] * 3,
        compiler_params=params(),
        cost_estimate=cost(
            4 * n * rows * group * width, 8 * n * rows * width, n * rows * group
        ),
        name="attend",
    )(*blocks)


def grads_kernel(n, split, k_ref, v_ref, rate_ref, one_ref, three_ref, two_ref, *rest):
    outs, total = rest[:-1], rest[-1]
    step = pl.program_id(0)
    hid, width = one_ref.shape[1:]

    @pl.when(step == 0)
    def _():
        total[...] = jnp.zeros_like(total)

    k = k_ref[...]
    one, three, two = one_ref[0], three_ref[0], two_ref[0]
    h_one = dot_bt(k, one)
    h_three = dot_bt(k, three)
    sigma = jax.nn.sigmoid(h_one)
    gated = h_one * sigma
    active = (gated * h_three).astype(BF16)
    pieces = []
    for low in range(0, k.shape[0], LANES):
        rate = column(rate_ref[:, low : low + LANES])
        rate = jnp.concatenate([rate] * (width // LANES), axis=1)
        pieces.append((-rate * v_ref[low : low + LANES, :].astype(F32)).astype(BF16))
    error = jnp.concatenate(pieces, axis=0)
    back = dot(error, two)
    back_one = (back * h_three * sigma * (1.0 + h_one * (1.0 - sigma))).astype(BF16)
    back_three = (back * gated).astype(BF16)
    total[0:hid, :] += dot_at(back_one, k)
    total[hid : 2 * hid, :] += dot_at(back_three, k)
    total[2 * hid :, :] += dot_at(error, active)

    @pl.when(step == pl.num_programs(0) - 1)
    def _():
        if split:
            half = total.shape[0] // 2
            core = lax.axis_index("cam") & 1
            outs[0][...] = total[pl.ds(pl.multiple_of(core * half, half), half), :]
            outs[1][...] = total[pl.ds(pl.multiple_of((1 - core) * half, half), half), :]
        else:
            outs[0][...] = total[...]


def gradients(k, v, rate, one, three, two, n):
    count, width = k.shape
    hid = one.shape[1]
    tile = min(count, 512)
    split = n > 1 and power_of_two(n)
    assert hid == width
    rows = 3 * hid
    parts = 2 if split else 1
    weight = pl.BlockSpec((1, hid, width), lambda i: (0, 0, 0))
    return pl.pallas_call(
        functools.partial(grads_kernel, n, split),
        grid=(count // tile,),
        out_shape=[jax.ShapeDtypeStruct((rows // parts, width), F32)] * parts,
        in_specs=[
            pl.BlockSpec((tile, width), lambda i: (i, 0)),
            pl.BlockSpec((tile, width), lambda i: (i, 0)),
            pl.BlockSpec((1, tile), lambda i: (0, i)),
            weight,
            weight,
            weight,
        ],
        out_specs=[pl.BlockSpec((rows // parts, width), lambda i: (0, 0))] * parts,
        scratch_shapes=[pltpu.VMEM((rows, width), F32)],
        compiler_params=params(),
        cost_estimate=cost(12 * count * width * hid, 8 * count * width, count * hid),
        name="gradients",
    )(k, v, rate, one, three, two)


def sum_over_cams(parts, n):
    if len(parts) == 1:
        return [lax.psum(parts[0], "cam")]
    keep, send = parts
    bits = n.bit_length() - 1
    mine = keep + lax.ppermute(send, "cam", routes(1, n))
    span = bits - 1
    for step in range(span):
        pairs = []
        for at in range(n):
            bit = 1 + (step + (at & 1)) % span
            pairs.append((at, at ^ (1 << bit)))
        mine = mine + lax.ppermute(mine, "cam", pairs)
    return [mine, lax.ppermute(mine, "cam", routes(1, n))]


def readout_kernel(parts, q_ref, one_ref, three_ref, two_ref, *rest):
    grads, (y_ref, sq_ref, total, fresh) = rest[:parts], rest[parts:]
    step = pl.program_id(0)
    hid, width = one_ref.shape[1:]

    @pl.when(step == 0)
    def _():
        if parts == 2:
            half = total.shape[0] // 2
            core = lax.axis_index("cam") & 1
            total[pl.ds(pl.multiple_of(core * half, half), half), :] = grads[0][...]
            total[pl.ds(pl.multiple_of((1 - core) * half, half), half), :] = grads[1][...]
        else:
            total[...] = grads[0][...]
        entries = hid * width
        for which, ref in enumerate((one_ref, three_ref, two_ref)):
            grad = total[which * hid : (which + 1) * hid, :]
            weight = ref[0].astype(F32)
            row_sq = jnp.sum(weight * weight, axis=1, keepdims=True)
            weight_sq = jnp.sum(row_sq, axis=0, keepdims=True)
            grad_sq = jnp.sum(
                jnp.sum(grad * grad, axis=1, keepdims=True), axis=0, keepdims=True
            )
            scale = jnp.sqrt(weight_sq / entries) / jnp.sqrt(grad_sq / entries + EPSILON)
            moved = weight - scale * grad
            ratio = jnp.sqrt(row_sq) / jnp.sqrt(
                jnp.sum(moved * moved, axis=1, keepdims=True) + EPSILON
            )
            fresh[which * hid : (which + 1) * hid, :] = (moved * ratio).astype(BF16)

    q = q_ref[...]
    h_one = dot_bt(q, fresh[0:hid, :])
    h_three = dot_bt(q, fresh[hid : 2 * hid, :])
    active = (h_one * jax.nn.sigmoid(h_one) * h_three).astype(BF16)
    y = dot_bt(active, fresh[2 * hid :, :])
    y_ref[...] = y
    square = y * y
    high = square.astype(BF16)
    low = (square - high.astype(F32)).astype(BF16)
    ones = jnp.ones((8, width), BF16)
    sq_ref[...] = (dot_bt(ones, high) + dot_bt(ones, low))[0:1, :]


def read_out(q, one, three, two, grads):
    count, width = q.shape
    hid = one.shape[1]
    tile = min(count, 512)
    weight = pl.BlockSpec((1, hid, width), lambda i: (0, 0, 0))
    parts = len(grads)
    return pl.pallas_call(
        functools.partial(readout_kernel, parts),
        grid=(count // tile,),
        out_shape=[
            jax.ShapeDtypeStruct((count, width), F32),
            jax.ShapeDtypeStruct((1, count), F32),
        ],
        in_specs=[pl.BlockSpec((tile, width), lambda i: (i, 0)), weight, weight, weight]
        + [pl.BlockSpec(grads[0].shape, lambda i: (0, 0))] * parts,
        out_specs=[
            pl.BlockSpec((tile, width), lambda i: (i, 0)),
            pl.BlockSpec((1, tile), lambda i: (0, i)),
        ],
        scratch_shapes=[pltpu.VMEM((3 * hid, width), F32), pltpu.VMEM((3 * hid, width), BF16)],
        compiler_params=params(),
        cost_estimate=cost(6 * count * width * hid, 8 * count * width, count * hid),
        name="read_out",
    )(q, one, three, two, *grads)


def slot_row(n, start, rows, owned_rows):
    me = lax.axis_index("cam")
    at = lax.broadcasted_iota(jnp.int32, (8, n * rows), 1)
    step = jnp.zeros_like(at)
    for cut in range(1, n):
        step = step + (at >= cut * rows).astype(jnp.int32)
    return peer(me, step, n) * owned_rows + start + at - step * rows


def placed(order_ref, low, slots, onehot, joined):
    tile = onehot.shape[0]
    for at in range(0, tile, LANES):
        wanted = column(order_ref[:, low + at : low + at + LANES].astype(F32))
        for lane in range(0, onehot.shape[1], LANES):
            hit = wanted == slots[:, lane : lane + LANES]
            onehot[at : at + LANES, lane : lane + LANES] = hit.astype(F32).astype(BF16)
    return dot(onehot[...], joined[...])


def unsort_kernel(n, start, rows, owned_rows, order_ref, *rest):
    blocks, (out_ref, onehot, joined) = rest[:n], rest[n:]
    for at in range(n):
        joined[at * rows : (at + 1) * rows, :] = blocks[at][...]
    slots = slot_row(n, start, rows, owned_rows)[0:1, :].astype(F32)
    tile = onehot.shape[0]
    for low in range(0, out_ref.shape[0], tile):
        part = placed(order_ref, low, slots, onehot, joined)
        out_ref[low : low + tile, :] = part.astype(BF16)


def unsort(order, blocks, n, start, owned_rows, count):
    rows, width = blocks[0].shape
    tile = min(count, 512)
    return pl.pallas_call(
        functools.partial(unsort_kernel, n, start, rows, owned_rows),
        out_shape=jax.ShapeDtypeStruct((count, width), BF16),
        in_specs=full(1 + n),
        out_specs=pl.BlockSpec(memory_space=pltpu.VMEM),
        scratch_shapes=[
            pltpu.VMEM((tile, n * rows), BF16),
            pltpu.VMEM((n * rows, width), BF16),
        ],
        compiler_params=params(),
        cost_estimate=cost(2 * count * n * rows * width, 4 * count * width),
        name="unsort",
    )(order, *blocks)


def mix_kernel(n, heads, start, rows, owned_rows, order_ref, gain_ref, y_ref, acc_ref, *rest):
    squares, blocks = rest[:heads], rest[heads : heads + n]
    out_ref, onehot, joined = rest[heads + n :]
    count, width = y_ref.shape
    for at in range(n):
        joined[at * rows : (at + 1) * rows, :] = blocks[at][...]
    slots = slot_row(n, start, rows, owned_rows)[0:1, :].astype(F32)
    total = squares[0][...]
    for ref in squares[1:]:
        total = total + ref[...]
    inverse = 1.0 / jnp.sqrt(total / (width * heads) + EPSILON)
    tile = onehot.shape[0]
    gain = gain_ref[...]
    for low in range(0, count, tile):
        part = placed(order_ref, low, slots, onehot, joined)
        for at in range(0, tile, LANES):
            here = slice(low + at, low + at + LANES)
            norm = column(inverse[:, here])
            norm = jnp.concatenate([norm] * (width // LANES), axis=1)
            rest_part = part[at : at + LANES] + acc_ref[here, :].astype(F32)
            out_ref[here, :] = (y_ref[here, :] * norm * gain + rest_part).astype(BF16)


def mix(order, gain, y, acc, squares, blocks, n, start, owned_rows):
    count, width = y.shape
    rows = blocks[0].shape[0]
    tile = min(count, 512)
    heads = len(squares)
    return pl.pallas_call(
        functools.partial(mix_kernel, n, heads, start, rows, owned_rows),
        out_shape=jax.ShapeDtypeStruct((count, width), BF16),
        in_specs=full(4 + heads + n),
        out_specs=pl.BlockSpec(memory_space=pltpu.VMEM),
        scratch_shapes=[
            pltpu.VMEM((tile, n * rows), BF16),
            pltpu.VMEM((n * rows, width), BF16),
        ],
        compiler_params=params(),
        cost_estimate=cost(2 * count * n * rows * width, 8 * count * width),
        name="mix",
    )(order, gain, y, acc, *squares, *blocks)


def exchange(blocks, n):
    return [blocks[0]] + [
        lax.ppermute(blocks[step], "cam", routes(step, n)) for step in range(1, n)
    ]


def give_back(blocks, n):
    moved = [blocks[0]]
    for step in range(1, n):
        pairs = [(target, at) for at, target in routes(step, n)]
        moved.append(lax.ppermute(blocks[step], "cam", pairs))
    return moved


def per_device(queries, keys, values, rates, w_one, w_three, w_two, gain, order):
    count, width = queries.shape
    n = lax.axis_size("cam")
    heads = lax.axis_size("head")
    owned_rows = count // n
    chunks = CHUNKS if (owned_rows // PATCHES) % CHUNKS == 0 else 1
    rows = owned_rows // chunks
    arrived = []
    for at in range(chunks):
        blocks = sort_tokens(order, queries, keys, values, n, at * rows, rows, owned_rows)
        arrived.append(exchange(blocks, n))
    parts = gradients(keys, values, rates.reshape(1, count), w_one, w_three, w_two, n)
    summed = sum_over_cams(parts, n)
    y, square = read_out(queries, w_one, w_three, w_two, summed)
    squares = [square] + [
        lax.ppermute(square, "head", [(at, (at + step) % heads) for at in range(heads)])
        for step in range(1, heads)
    ]
    acc = jnp.zeros((count, width), BF16) if chunks == 1 else None
    for at in range(chunks):
        returned = give_back(attend(arrived[at], n, width), n)
        if at == chunks - 1:
            gain_row = gain.reshape(1, width)
            return mix(order, gain_row, y, acc, squares, returned, n, at * rows, owned_rows)
        part = unsort(order, returned, n, at * rows, owned_rows, count)
        acc = part if acc is None else acc + part


def solution(mesh):
    in_specs = (
        P("cam", "head"),
        P("cam", "head"),
        P("cam", "head"),
        P("cam", "head"),
        P("head", None, None),
        P("head", None, None),
        P("head", None, None),
        P("head"),
        P("cam", None),
    )
    out_specs = P("cam", "head")
    return jax.shard_map(
        per_device, mesh=mesh, in_specs=in_specs, out_specs=out_specs, check_vma=False
    )
```

```python
import functools

import jax
import jax.numpy as jnp
from jax import lax
from jax.experimental import pallas as pl
from jax.experimental.pallas import tpu as pltpu
from jax.sharding import PartitionSpec as P

PATCHES = 32
EPSILON = 1e-06
LANES = 128
CHUNKS = 2
TILE = 512
MIB = 1024 * 1024
F32 = jnp.float32
BF16 = jnp.bfloat16


def dot(a, b):
    return lax.dot_general(a, b, (((1,), (0,)), ((), ())), preferred_element_type=F32)


def dot_bt(a, b):
    return lax.dot_general(a, b, (((1,), (1,)), ((), ())), preferred_element_type=F32)


def dot_at(a, b):
    return lax.dot_general(a, b, (((0,), (0,)), ((), ())), preferred_element_type=F32)


def params():
    return pltpu.CompilerParams(vmem_limit_bytes=40 * MIB)


def full(count):
    return [pl.BlockSpec(memory_space=pltpu.VMEM)] * count


def cost(flops, moved, exps=0):
    return pl.CostEstimate(flops=int(flops), bytes_accessed=int(moved), transcendentals=int(exps))


def power_of_two(n):
    return n & (n - 1) == 0


def crossed(step):
    return (step & ~6) | ((step & 2) << 1) | ((step & 4) >> 1)


def peer(me, step, n):
    if power_of_two(n):
        if n < 8:
            return me ^ step
        odd = me & 1
        return me ^ (step * (1 - odd) + crossed(step) * odd)
    ahead = me + step
    wrap = ahead - n
    return wrap * (wrap >= 0) + ahead * (wrap < 0)


def routes(step, n):
    return [(at, int(peer(at, step, n))) for at in range(n)]


def column(row):
    return jnp.broadcast_to(row, (LANES, LANES)).T


def sort_into(n, start, rows, owned_rows, order, sources, outs, onehot):
    me = lax.axis_index("cam")
    group = onehot.shape[0] // rows
    count = onehot.shape[1]
    for first in range(0, n, group):
        for at in range(group):
            base = peer(me, first + at, n) * owned_rows + start
            slot = lax.broadcasted_iota(jnp.int32, (rows, count), 0) + base
            onehot[at * rows : (at + 1) * rows, :] = (slot == order).astype(F32).astype(BF16)
        for which, source in sources:
            ref = source(first == 0)
            width = ref.shape[1]
            picked = dot(onehot[...], ref[...]).astype(BF16)
            for at in range(group):
                outs[first + at][:, which * width : (which + 1) * width] = picked[
                    at * rows : (at + 1) * rows
                ]


def first_sort_kernel(n, start, rows, owned_rows, order_in, q_in, k_in, v_in, *rest):
    outs, (order_ref, q_ref, k_ref, v_ref, onehot, sems) = rest[:n], rest[n:]
    copies = [
        pltpu.make_async_copy(source, target, sems.at[at])
        for at, (source, target) in enumerate(
            ((order_in, order_ref), (k_in, k_ref), (v_in, v_ref), (q_in, q_ref))
        )
    ]
    for copy in copies:
        copy.start()
    copies[0].wait()

    def arrives(ref, copy):
        def get(first):
            if first:
                copy.wait()
            return ref

        return get

    sources = (
        (1, arrives(k_ref, copies[1])),
        (2, arrives(v_ref, copies[2])),
        (0, arrives(q_ref, copies[3])),
    )
    sort_into(n, start, rows, owned_rows, order_ref[...], sources, outs, onehot)


def sort_kernel(n, start, rows, owned_rows, order_ref, q_ref, k_ref, v_ref, *rest):
    outs, onehot = rest[:n], rest[n]
    sources = ((0, lambda _: q_ref), (1, lambda _: k_ref), (2, lambda _: v_ref))
    sort_into(n, start, rows, owned_rows, order_ref[...], sources, outs, onehot)


def sort_tokens(order, q, k, v, n, start, rows, owned_rows, first):
    count, width = q.shape
    group = max(1, min(n, 512 // rows))
    while n % group:
        group -= 1
    shapes = [jax.ShapeDtypeStruct((rows, 3 * width), BF16)] * n
    scratch = [pltpu.VMEM((group * rows, count), BF16)]
    if first:
        shapes = shapes + [
            jax.ShapeDtypeStruct(array.shape, array.dtype) for array in (order, q, k, v)
        ]
        scratch = scratch + [pltpu.SemaphoreType.DMA((4,))]
    return pl.pallas_call(
        functools.partial(
            first_sort_kernel if first else sort_kernel, n, start, rows, owned_rows
        ),
        out_shape=shapes,
        in_specs=[pl.BlockSpec(memory_space=pltpu.HBM)] * 4 if first else full(4),
        out_specs=full(len(shapes)),
        scratch_shapes=scratch,
        compiler_params=params(),
        cost_estimate=cost(6 * n * rows * count * width, 6 * count * width),
        name="sort_tokens",
    )(order, q, k, v)


def attend_kernel(n, scale, *refs):
    ins, outs = refs[:n], refs[-3 - n : -3]
    q_all, k_all, v_all = refs[-3:]
    rows = ins[0].shape[0]
    width = outs[0].shape[1]
    group = n * PATCHES
    block = min(group, 256)
    for stamp in range(rows // PATCHES):
        here = slice(stamp * PATCHES, (stamp + 1) * PATCHES)
        for cam in range(n):
            there = slice(cam * PATCHES, (cam + 1) * PATCHES)
            q_all[there, :] = ins[cam][here, 0:width]
            k_all[there, :] = ins[cam][here, width : 2 * width]
            v_all[there, :] = ins[cam][here, 2 * width : 3 * width]
        for low in range(0, group, block):
            scores = dot_bt(q_all[low : low + block, :], k_all[...]) * scale
            scores = scores - jnp.max(scores, axis=-1, keepdims=True)
            expo = jnp.exp(scores)
            probs = (expo / jnp.sum(expo, axis=-1, keepdims=True)).astype(BF16)
            result = dot(probs, v_all[...]).astype(BF16)
            for cam in range(low // PATCHES, (low + block) // PATCHES):
                at = cam * PATCHES - low
                outs[cam][here, :] = result[at : at + PATCHES]


def attend(blocks, after, n, width):
    rows = blocks[0].shape[0]
    group = n * PATCHES
    return pl.pallas_call(
        functools.partial(attend_kernel, n, width**-0.5),
        out_shape=[jax.ShapeDtypeStruct((rows, width), BF16)] * n,
        in_specs=full(n) + [pl.BlockSpec(memory_space=pl.ANY)] * len(after),
        out_specs=full(n),
        scratch_shapes=[pltpu.VMEM((group, width), BF16)] * 3,
        compiler_params=params(),
        cost_estimate=cost(
            4 * n * rows * group * width, 8 * n * rows * width, n * rows * group
        ),
        name="attend",
    )(*blocks, *after)


def grads_kernel(n, split, k_ref, v_ref, rate_ref, one_ref, three_ref, two_ref, *rest):
    outs, total = rest[:-1], rest[-1]
    count, width = k_ref.shape
    hid = one_ref.shape[1]
    one, three, two = one_ref[0], three_ref[0], two_ref[0]
    tile = min(count, TILE)
    for start in range(0, count, tile):
        k = k_ref[start : start + tile, :]
        h_one = dot_bt(k, one)
        h_three = dot_bt(k, three)
        sigma = jax.nn.sigmoid(h_one)
        gated = h_one * sigma
        active = (gated * h_three).astype(BF16)
        pieces = []
        for low in range(start, start + tile, LANES):
            rate = column(rate_ref[:, low : low + LANES])
            rate = jnp.concatenate([rate] * (width // LANES), axis=1)
            pieces.append((-rate * v_ref[low : low + LANES, :].astype(F32)).astype(BF16))
        error = jnp.concatenate(pieces, axis=0)
        back = dot(error, two)
        back_one = (back * h_three * sigma * (1.0 + h_one * (1.0 - sigma))).astype(BF16)
        back_three = (back * gated).astype(BF16)
        sums = (dot_at(back_one, k), dot_at(back_three, k), dot_at(error, active))
        for which, term in enumerate(sums):
            here = slice(which * hid, (which + 1) * hid)
            total[here, :] = term if start == 0 else total[here, :] + term
    if split:
        half = total.shape[0] // 2
        core = lax.axis_index("cam") & 1
        outs[0][...] = total[pl.ds(pl.multiple_of(core * half, half), half), :]
        outs[1][...] = total[pl.ds(pl.multiple_of((1 - core) * half, half), half), :]
    else:
        outs[0][...] = total[...]


def gradients(k, v, rate, one, three, two, n):
    count, width = k.shape
    hid = one.shape[1]
    split = n > 1 and power_of_two(n)
    assert hid == width
    rows = 3 * hid
    parts = 2 if split else 1
    return pl.pallas_call(
        functools.partial(grads_kernel, n, split),
        out_shape=[jax.ShapeDtypeStruct((rows // parts, width), F32)] * parts,
        in_specs=full(6),
        out_specs=full(parts),
        scratch_shapes=[pltpu.VMEM((rows, width), F32)],
        compiler_params=params(),
        cost_estimate=cost(12 * count * width * hid, 8 * count * width, count * hid),
        name="gradients",
    )(k, v, rate, one, three, two)


def sum_over_cams(parts, n):
    if len(parts) == 1:
        return [lax.psum(parts[0], "cam")]
    keep, send = parts
    bits = n.bit_length() - 1
    pair = [(at, at ^ 1) for at in range(n)]
    mine = keep + lax.ppermute(send, "cam", pair)
    span = bits - 1
    for step in range(span):
        pairs = []
        for at in range(n):
            bit = 1 + (step + (at & 1)) % span
            pairs.append((at, at ^ (1 << bit)))
        mine = mine + lax.ppermute(mine.astype(BF16), "cam", pairs).astype(F32)
    return [mine, lax.ppermute(mine, "cam", pair)]


def readout_kernel(parts, q_ref, one_ref, three_ref, two_ref, *rest):
    grads, (y_ref, sq_ref, total, fresh) = rest[:parts], rest[parts:]
    hid, width = one_ref.shape[1:]
    if parts == 2:
        half = total.shape[0] // 2
        core = lax.axis_index("cam") & 1
        total[pl.ds(pl.multiple_of(core * half, half), half), :] = grads[0][...]
        total[pl.ds(pl.multiple_of((1 - core) * half, half), half), :] = grads[1][...]
    else:
        total[...] = grads[0][...]
    entries = hid * width
    for which, ref in enumerate((one_ref, three_ref, two_ref)):
        grad = total[which * hid : (which + 1) * hid, :]
        weight = ref[0].astype(F32)
        row_sq = jnp.sum(weight * weight, axis=1, keepdims=True)
        weight_sq = jnp.sum(row_sq, axis=0, keepdims=True)
        grad_sq = jnp.sum(jnp.sum(grad * grad, axis=1, keepdims=True), axis=0, keepdims=True)
        scale = jnp.sqrt(weight_sq / entries) / jnp.sqrt(grad_sq / entries + EPSILON)
        moved = weight - scale * grad
        ratio = jnp.sqrt(row_sq) / jnp.sqrt(
            jnp.sum(moved * moved, axis=1, keepdims=True) + EPSILON
        )
        fresh[which * hid : (which + 1) * hid, :] = (moved * ratio).astype(BF16)
    count = q_ref.shape[0]
    tile = min(count, TILE)
    ones = jnp.ones((8, width), BF16)
    for start in range(0, count, tile):
        here = slice(start, start + tile)
        q = q_ref[here, :]
        h_one = dot_bt(q, fresh[0:hid, :])
        h_three = dot_bt(q, fresh[hid : 2 * hid, :])
        active = (h_one * jax.nn.sigmoid(h_one) * h_three).astype(BF16)
        y = dot_bt(active, fresh[2 * hid :, :])
        y_ref[here, :] = y
        square = y * y
        high = square.astype(BF16)
        low = (square - high.astype(F32)).astype(BF16)
        sq_ref[:, here] = (dot_bt(ones, high) + dot_bt(ones, low))[0:1, :]


def read_out(q, one, three, two, grads):
    count, width = q.shape
    hid = one.shape[1]
    parts = len(grads)
    return pl.pallas_call(
        functools.partial(readout_kernel, parts),
        out_shape=[
            jax.ShapeDtypeStruct((count, width), F32),
            jax.ShapeDtypeStruct((1, count), F32),
        ],
        in_specs=full(4 + parts),
        out_specs=full(2),
        scratch_shapes=[pltpu.VMEM((3 * hid, width), F32), pltpu.VMEM((3 * hid, width), BF16)],
        compiler_params=params(),
        cost_estimate=cost(6 * count * width * hid, 8 * count * width, count * hid),
        name="read_out",
    )(q, one, three, two, *grads)


def slot_row(n, start, rows, owned_rows):
    me = lax.axis_index("cam")
    at = lax.broadcasted_iota(jnp.int32, (8, n * rows), 1)
    step = jnp.zeros_like(at)
    for cut in range(1, n):
        step = step + (at >= cut * rows).astype(jnp.int32)
    return peer(me, step, n) * owned_rows + start + at - step * rows


def placed(order_ref, low, slots, onehot, joined):
    tile = onehot.shape[0]
    for at in range(0, tile, LANES):
        wanted = column(order_ref[:, low + at : low + at + LANES].astype(F32))
        for lane in range(0, onehot.shape[1], LANES):
            hit = wanted == slots[:, lane : lane + LANES]
            onehot[at : at + LANES, lane : lane + LANES] = hit.astype(F32).astype(BF16)
    return dot(onehot[...], joined[...])


def base_kernel(heads, shapes, order_ref, gain_ref, y_ref, *rest):
    squares, rest = rest[:heads], rest[heads:]
    count, width = y_ref.shape
    n, given = shapes
    groups = [rest[at * n : (at + 1) * n] for at in range(len(given))]
    out_ref = rest[len(given) * n]
    scratch = rest[len(given) * n + 1 :]
    total = squares[0][...]
    for ref in squares[1:]:
        total = total + ref[...]
    inverse = 1.0 / jnp.sqrt(total / (width * heads) + EPSILON)
    gain = gain_ref[...]
    owned_rows = count // n
    tile = min(count, TILE)
    laid = []
    for at, (start, rows) in enumerate(given):
        onehot, joined = scratch[2 * at : 2 * at + 2]
        for cam in range(n):
            joined[cam * rows : (cam + 1) * rows, :] = groups[at][cam][...]
        laid.append((slot_row(n, start, rows, owned_rows)[0:1, :].astype(F32), onehot, joined))
    for low in range(0, count, tile):
        parts = [placed(order_ref, low, *entry) for entry in laid]
        for at in range(0, tile, LANES):
            here = slice(low + at, low + at + LANES)
            norm = column(inverse[:, here])
            norm = jnp.concatenate([norm] * (width // LANES), axis=1)
            value = y_ref[here, :] * norm * gain
            for part in parts:
                value = value + part[at : at + LANES]
            out_ref[here, :] = value


def base(order, gain, y, squares, groups, starts, n):
    count, width = y.shape
    heads = len(squares)
    tile = min(count, TILE)
    scratch = []
    for _, rows in starts:
        scratch.append(pltpu.VMEM((tile, n * rows), BF16))
        scratch.append(pltpu.VMEM((n * rows, width), BF16))
    blocks = [block for group in groups for block in group]
    moved = sum(n * rows for _, rows in starts)
    return pl.pallas_call(
        functools.partial(base_kernel, heads, (n, tuple(starts))),
        out_shape=jax.ShapeDtypeStruct((count, width), F32),
        in_specs=full(3 + heads + len(blocks)),
        out_specs=pl.BlockSpec(memory_space=pltpu.VMEM),
        scratch_shapes=scratch,
        compiler_params=params(),
        cost_estimate=cost(2 * count * moved * width, 8 * count * width),
        name="base",
    )(order, gain, y, *squares, *blocks)


def mix_kernel(n, start, rows, owned_rows, order_ref, base_ref, *rest):
    blocks, (out_ref, onehot, joined) = rest[:n], rest[n:]
    step = pl.program_id(0)

    @pl.when(step == 0)
    def _():
        for at in range(n):
            joined[at * rows : (at + 1) * rows, :] = blocks[at][...]

    slots = slot_row(n, start, rows, owned_rows)[0:1, :].astype(F32)
    part = placed(order_ref, 0, slots, onehot, joined)
    out_ref[...] = (base_ref[...] + part).astype(BF16)


def mix(order, given, blocks, n, start, owned_rows):
    count, width = given.shape
    rows = blocks[0].shape[0]
    tile = min(count, TILE)
    return pl.pallas_call(
        functools.partial(mix_kernel, n, start, rows, owned_rows),
        grid=(count // tile,),
        out_shape=jax.ShapeDtypeStruct((count, width), BF16),
        in_specs=[
            pl.BlockSpec((1, tile), lambda i: (0, i)),
            pl.BlockSpec((tile, width), lambda i: (i, 0)),
        ]
        + full(n),
        out_specs=pl.BlockSpec((tile, width), lambda i: (i, 0)),
        scratch_shapes=[
            pltpu.VMEM((tile, n * rows), BF16),
            pltpu.VMEM((n * rows, width), BF16),
        ],
        compiler_params=params(),
        cost_estimate=cost(2 * count * n * rows * width, 8 * count * width),
        name="mix",
    )(order, given, *blocks)


def exchange(blocks, n):
    return [blocks[0]] + [
        lax.ppermute(blocks[step], "cam", routes(step, n)) for step in range(1, n)
    ]


def give_back(blocks, n):
    moved = [blocks[0]]
    for step in range(1, n):
        pairs = [(target, at) for at, target in routes(step, n)]
        moved.append(lax.ppermute(blocks[step], "cam", pairs))
    return moved


def per_device(queries, keys, values, rates, w_one, w_three, w_two, gain, order):
    count, width = queries.shape
    n = lax.axis_size("cam")
    heads = lax.axis_size("head")
    owned_rows = count // n
    chunks = CHUNKS if (owned_rows // PATCHES) % CHUNKS == 0 else 1
    rows = owned_rows // chunks
    arrived = []
    for at in range(chunks):
        blocks = sort_tokens(
            order, queries, keys, values, n, at * rows, rows, owned_rows, at == 0
        )
        if at == 0:
            order, queries, keys, values = blocks[n:]
            blocks = blocks[:n]
        arrived.append(exchange(blocks, n))
    parts = gradients(keys, values, rates.reshape(1, count), w_one, w_three, w_two, n)
    summed = sum_over_cams(parts, n)
    y, square = read_out(queries, w_one, w_three, w_two, summed)
    squares = [square] + [
        lax.ppermute(square, "head", [(at, (at + step) % heads) for at in range(heads)])
        for step in range(1, heads)
    ]
    returned = []
    for at in range(chunks):
        after = [square] if at == chunks - 1 else []
        returned.append(give_back(attend(arrived[at], after, n, width), n))
    starts = [(at * rows, rows) for at in range(chunks)]
    given = base(order, gain.reshape(1, width), y, squares, returned[:-1], starts[:-1], n)
    return mix(order, given, returned[-1], n, starts[-1][0], owned_rows)


def solution(mesh):
    in_specs = (
        P("cam", "head"),
        P("cam", "head"),
        P("cam", "head"),
        P("cam", "head"),
        P("head", None, None),
        P("head", None, None),
        P("head", None, None),
        P("head"),
        P("cam", None),
    )
    out_specs = P("cam", "head")
    return jax.shard_map(
        per_device, mesh=mesh, in_specs=in_specs, out_specs=out_specs, check_vma=False
    )
```

```python
import functools

import jax
import jax.numpy as jnp
from jax import lax
from jax.experimental import pallas as pl
from jax.experimental.pallas import tpu as pltpu
from jax.sharding import PartitionSpec as P

PATCHES = 32
EPSILON = 1e-06
LANES = 128
TILE = 512
LIMIT = 24
FIRST_LIMIT = 54
COST = 8
MIB = 1024 * 1024
F32 = jnp.float32
BF16 = jnp.bfloat16
TOKEN = jax.ShapeDtypeStruct((8, LANES), F32)


def dot(a, b):
    return lax.dot_general(a, b, (((1,), (0,)), ((), ())), preferred_element_type=F32)


def dot_bt(a, b):
    return lax.dot_general(a, b, (((1,), (1,)), ((), ())), preferred_element_type=F32)


def dot_at(a, b):
    return lax.dot_general(a, b, (((0,), (0,)), ((), ())), preferred_element_type=F32)


def params(limit=LIMIT):
    return pltpu.CompilerParams(vmem_limit_bytes=limit * MIB)


def full(count):
    return [pl.BlockSpec(memory_space=pltpu.VMEM)] * count


def cost(flops, moved, exps=0):
    return pl.CostEstimate(
        flops=int(flops) // COST,
        bytes_accessed=int(moved) // COST,
        transcendentals=int(exps) // COST,
    )


def power_of_two(n):
    return n & (n - 1) == 0


def crossed(step):
    return (step & ~6) | ((step & 2) << 1) | ((step & 4) >> 1)


def peer(me, step, n):
    if power_of_two(n):
        if n < 8:
            return me ^ step
        odd = me & 1
        return me ^ (step * (1 - odd) + crossed(step) * odd)
    ahead = me + step
    wrap = ahead - n
    return wrap * (wrap >= 0) + ahead * (wrap < 0)


def routes(step, n):
    return [(at, int(peer(at, step, n))) for at in range(n)]


def column(row):
    return jnp.broadcast_to(row, (LANES, LANES)).T


def far_first(n):
    return sorted(range(n), key=lambda step: (-(step >> 1).bit_count(), -step))


def fetch(pairs, sems):
    copies = []
    for at, (source, target) in enumerate(pairs):
        copies.append(pltpu.make_async_copy(source, target, sems.at[at]))
        copies[-1].start()
    return copies


def sort_into(n, steps, order, sources, outs, onehot):
    me = lax.axis_index("cam")
    count = onehot.shape[1]
    rows = count // n
    group = onehot.shape[0] // rows
    for first in range(0, len(steps), group):
        for at in range(group):
            base = peer(me, steps[first + at], n) * rows
            slot = lax.broadcasted_iota(jnp.int32, (rows, count), 0) + base
            onehot[at * rows : (at + 1) * rows, :] = (slot == order).astype(F32).astype(BF16)
        for which, source in sources:
            ref = source(first == 0)
            width = ref.shape[1]
            picked = dot(onehot[...], ref[...]).astype(BF16)
            for at in range(group):
                outs[first + at][:, which * width : (which + 1) * width] = picked[
                    at * rows : (at + 1) * rows
                ]


def first_sort_kernel(n, steps, order_in, q_in, k_in, v_in, *rest):
    outs, rest = rest[: len(steps)], rest[len(steps) :]
    token, onehot, order_ref, k_ref, v_ref, q_ref, sems = rest
    token[...] = jnp.zeros_like(token)
    copies = fetch(
        ((order_in, order_ref), (k_in, k_ref), (v_in, v_ref), (q_in, q_ref)), sems
    )
    copies[0].wait()

    def arrives(ref, copy):
        def get(first):
            if first:
                copy.wait()
            return ref

        return get

    sources = (
        (1, arrives(k_ref, copies[1])),
        (2, arrives(v_ref, copies[2])),
        (0, arrives(q_ref, copies[3])),
    )
    sort_into(n, steps, order_ref[...], sources, outs, onehot)


def sort_kernel(n, steps, order_ref, q_ref, k_ref, v_ref, *rest):
    outs, (token, onehot) = rest[: len(steps)], rest[len(steps) :]
    token[...] = jnp.zeros_like(token)
    sources = ((0, lambda _: q_ref), (1, lambda _: k_ref), (2, lambda _: v_ref))
    sort_into(n, steps, order_ref[...], sources, outs, onehot)


def sort_tokens(order, q, k, v, n, steps, first):
    count, width = q.shape
    rows = count // n
    size = len(steps)
    group = max(1, min(size, TILE // rows))
    while size % group:
        group -= 1
    shapes = [jax.ShapeDtypeStruct((rows, 3 * width), BF16)] * size + [TOKEN]
    scratch = [pltpu.VMEM((group * rows, count), BF16)]
    if first:
        scratch = scratch + [pltpu.VMEM(array.shape, array.dtype) for array in (order, k, v, q)]
        scratch = scratch + [pltpu.SemaphoreType.DMA((4,))]
    return pl.pallas_call(
        functools.partial(first_sort_kernel if first else sort_kernel, n, tuple(steps)),
        out_shape=shapes,
        in_specs=[pl.BlockSpec(memory_space=pltpu.HBM)] * 4 if first else full(4),
        out_specs=full(len(shapes)),
        scratch_shapes=scratch,
        compiler_params=params(FIRST_LIMIT if first else LIMIT),
        cost_estimate=cost(6 * size * rows * count * width, 6 * count * width),
        name="sort_tokens",
    )(order, q, k, v)


def attend_kernel(n, scale, *refs):
    ins, outs = refs[:n], refs[-3 - n : -3]
    q_all, k_all, v_all = refs[-3:]
    rows = ins[0].shape[0]
    width = outs[0].shape[1]
    group = n * PATCHES
    block = min(group, 256)
    for stamp in range(rows // PATCHES):
        here = slice(stamp * PATCHES, (stamp + 1) * PATCHES)
        for cam in range(n):
            there = slice(cam * PATCHES, (cam + 1) * PATCHES)
            q_all[there, :] = ins[cam][here, 0:width]
            k_all[there, :] = ins[cam][here, width : 2 * width]
            v_all[there, :] = ins[cam][here, 2 * width : 3 * width]
        for low in range(0, group, block):
            scores = dot_bt(q_all[low : low + block, :], k_all[...]) * scale
            scores = scores - jnp.max(scores, axis=-1, keepdims=True)
            expo = jnp.exp(scores)
            probs = (expo / jnp.sum(expo, axis=-1, keepdims=True)).astype(BF16)
            result = dot(probs, v_all[...]).astype(BF16)
            for cam in range(low // PATCHES, (low + block) // PATCHES):
                at = cam * PATCHES - low
                outs[cam][here, :] = result[at : at + PATCHES]


def attend(blocks, after, n, width):
    rows = blocks[0].shape[0]
    group = n * PATCHES
    return pl.pallas_call(
        functools.partial(attend_kernel, n, width**-0.5),
        out_shape=[jax.ShapeDtypeStruct((rows, width), BF16)] * n,
        in_specs=full(n) + [pl.BlockSpec(memory_space=pl.ANY)] * len(after),
        out_specs=full(n),
        scratch_shapes=[pltpu.VMEM((group, width), BF16)] * 3,
        compiler_params=params(),
        cost_estimate=cost(
            4 * n * rows * group * width, 8 * n * rows * width, n * rows * group
        ),
        name="attend",
    )(*blocks, *after)


def grads_kernel(n, split, parts, k_in, v_in, rate_in, one_in, three_in, two_in, *rest):
    outs, rest = rest[:parts], rest[parts:]
    total, one_ref, three_ref, two_ref, rate_ref, k_ref, v_ref, sems = rest
    count, width = k_ref.shape
    hid = one_ref.shape[1]
    tile = min(count, TILE)
    tiles = [slice(start, start + tile) for start in range(0, count, tile)]
    pairs = [(one_in, one_ref), (three_in, three_ref), (k_in.at[tiles[0]], k_ref.at[tiles[0]])]
    pairs += [(rate_in, rate_ref), (v_in.at[tiles[0]], v_ref.at[tiles[0]]), (two_in, two_ref)]
    for here in tiles[1:]:
        pairs += [(k_in.at[here], k_ref.at[here]), (v_in.at[here], v_ref.at[here])]
    copies = fetch(pairs, sems)
    for copy in copies[:6]:
        copy.wait()
    one, three, two = one_ref[0], three_ref[0], two_ref[0]
    for start in range(0, count, tile):
        if start:
            copies[4 + 2 * (start // tile)].wait()
            copies[5 + 2 * (start // tile)].wait()
        k = k_ref[start : start + tile, :]
        h_one = dot_bt(k, one)
        h_three = dot_bt(k, three)
        sigma = jax.nn.sigmoid(h_one)
        gated = h_one * sigma
        active = (gated * h_three).astype(BF16)
        pieces = []
        for low in range(start, start + tile, LANES):
            rate = column(rate_ref[:, low : low + LANES])
            rate = jnp.concatenate([rate] * (width // LANES), axis=1)
            pieces.append((-rate * v_ref[low : low + LANES, :].astype(F32)).astype(BF16))
        error = jnp.concatenate(pieces, axis=0)
        back = dot(error, two)
        back_one = (back * h_three * sigma * (1.0 + h_one * (1.0 - sigma))).astype(BF16)
        back_three = (back * gated).astype(BF16)
        sums = (dot_at(back_one, k), dot_at(back_three, k), dot_at(error, active))
        for which, term in enumerate(sums):
            here = slice(which * hid, (which + 1) * hid)
            total[here, :] = term if start == 0 else total[here, :] + term
    if split:
        half = total.shape[0] // 2
        core = lax.axis_index("cam") & 1
        outs[0][...] = total[pl.ds(pl.multiple_of(core * half, half), half), :]
        outs[1][...] = total[pl.ds(pl.multiple_of((1 - core) * half, half), half), :]
    else:
        outs[0][...] = total[...]


def gradients(k, v, rate, one, three, two, n):
    count, width = k.shape
    hid = one.shape[1]
    split = n > 1 and power_of_two(n)
    assert hid == width
    rows = 3 * hid
    parts = 2 if split else 1
    tiles = count // min(count, TILE)
    held = (one, three, two, rate, k, v)
    return pl.pallas_call(
        functools.partial(grads_kernel, n, split, parts),
        out_shape=[jax.ShapeDtypeStruct((rows // parts, width), F32)] * parts,
        in_specs=[pl.BlockSpec(memory_space=pltpu.HBM)] * 6,
        out_specs=full(parts),
        scratch_shapes=[pltpu.VMEM((rows, width), F32)]
        + [pltpu.VMEM(array.shape, array.dtype) for array in held]
        + [pltpu.SemaphoreType.DMA((4 + 2 * tiles,))],
        compiler_params=params(58),
        cost_estimate=cost(12 * count * width * hid, 8 * count * width, count * hid),
        name="gradients",
    )(k, v, rate, one, three, two)


def merge_kernel(keep_ref, got_ref, *rest):
    rest[-1][...] = keep_ref[...] + got_ref[...].astype(F32)


def merge(keep, got, after):
    return pl.pallas_call(
        merge_kernel,
        out_shape=jax.ShapeDtypeStruct(keep.shape, F32),
        in_specs=full(2) + [pl.BlockSpec(memory_space=pl.ANY)] * len(after),
        out_specs=pl.BlockSpec(memory_space=pltpu.VMEM),
        compiler_params=params(),
        cost_estimate=cost(keep.size, 12 * keep.size),
        name="merge",
    )(keep, got, *after)


def sum_over_cams(parts, after, n):
    if len(parts) == 1:
        return [lax.psum(parts[0], "cam")]
    keep, send = parts
    bits = n.bit_length() - 1
    pair = [(at, at ^ 1) for at in range(n)]
    mine = merge(keep, lax.ppermute(send, "cam", pair), after[0])
    span = bits - 1
    for step in range(span):
        pairs = []
        for at in range(n):
            bit = 1 + (step + (at & 1)) % span
            pairs.append((at, at ^ (1 << bit)))
        got = lax.ppermute(mine.astype(BF16), "cam", pairs)
        if step + 1 < len(after):
            mine = merge(mine, got, after[step + 1])
        else:
            mine = mine + got.astype(F32)
    return [mine, lax.ppermute(mine, "cam", pair)]


def readout_kernel(parts, q_ref, one_ref, three_ref, two_ref, *rest):
    grads, (y_ref, sq_ref, total, fresh) = rest[:parts], rest[parts:]
    hid, width = one_ref.shape[1:]
    if parts == 2:
        half = total.shape[0] // 2
        core = lax.axis_index("cam") & 1
        total[pl.ds(pl.multiple_of(core * half, half), half), :] = grads[0][...]
        total[pl.ds(pl.multiple_of((1 - core) * half, half), half), :] = grads[1][...]
    else:
        total[...] = grads[0][...]
    entries = hid * width
    for which, ref in enumerate((one_ref, three_ref, two_ref)):
        grad = total[which * hid : (which + 1) * hid, :]
        weight = ref[0].astype(F32)
        row_sq = jnp.sum(weight * weight, axis=1, keepdims=True)
        weight_sq = jnp.sum(row_sq, axis=0, keepdims=True)
        grad_sq = jnp.sum(jnp.sum(grad * grad, axis=1, keepdims=True), axis=0, keepdims=True)
        scale = jnp.sqrt(weight_sq / entries) / jnp.sqrt(grad_sq / entries + EPSILON)
        moved = weight - scale * grad
        ratio = jnp.sqrt(row_sq) / jnp.sqrt(
            jnp.sum(moved * moved, axis=1, keepdims=True) + EPSILON
        )
        fresh[which * hid : (which + 1) * hid, :] = (moved * ratio).astype(BF16)
    count = q_ref.shape[0]
    tile = min(count, TILE)
    ones = jnp.ones((8, width), BF16)
    for start in range(0, count, tile):
        here = slice(start, start + tile)
        q = q_ref[here, :]
        h_one = dot_bt(q, fresh[0:hid, :])
        h_three = dot_bt(q, fresh[hid : 2 * hid, :])
        active = (h_one * jax.nn.sigmoid(h_one) * h_three).astype(BF16)
        y = dot_bt(active, fresh[2 * hid :, :])
        y_ref[here, :] = y
        square = y * y
        high = square.astype(BF16)
        low = (square - high.astype(F32)).astype(BF16)
        sq_ref[:, here] = (dot_bt(ones, high) + dot_bt(ones, low))[0:1, :]


def read_out(q, one, three, two, grads):
    count, width = q.shape
    hid = one.shape[1]
    parts = len(grads)
    return pl.pallas_call(
        functools.partial(readout_kernel, parts),
        out_shape=[
            jax.ShapeDtypeStruct((count, width), F32),
            jax.ShapeDtypeStruct((1, count), F32),
        ],
        in_specs=full(4 + parts),
        out_specs=full(2),
        scratch_shapes=[pltpu.VMEM((3 * hid, width), F32), pltpu.VMEM((3 * hid, width), BF16)],
        compiler_params=params(),
        cost_estimate=cost(6 * count * width * hid, 8 * count * width, count * hid),
        name="read_out",
    )(q, one, three, two, *grads)


def place_kernel(n, steps, order_ref, *outs):
    me = lax.axis_index("cam")
    count = order_ref.shape[1]
    rows = count // n
    size = len(steps) * rows
    at = lax.broadcasted_iota(jnp.int32, (8, size), 1)
    slots = at * 0
    for which, step in enumerate(steps):
        inside = jnp.logical_and(at >= which * rows, at < (which + 1) * rows)
        slots = jnp.where(inside, peer(me, step, n) * rows + at - which * rows, slots)
    slots = slots[0:1, :].astype(F32)
    each = outs[0].shape[1]
    for low in range(0, count, LANES):
        wanted = column(order_ref[:, low : low + LANES].astype(F32))
        for lane in range(0, size, LANES):
            hit = wanted == slots[:, lane : lane + LANES]
            out = outs[lane // each]
            start = lane % each
            out[low : low + LANES, start : start + LANES] = hit.astype(F32).astype(BF16)


def place(order, n, steps):
    count = order.shape[1]
    shape = jax.ShapeDtypeStruct((count, count // 2), BF16)
    return pl.pallas_call(
        functools.partial(place_kernel, n, tuple(steps)),
        out_shape=[shape, shape],
        in_specs=full(1),
        out_specs=full(2),
        compiler_params=params(),
        cost_estimate=cost(count * count, 2 * count * count),
        name="place",
    )(order)


def gathered(onehot, here, blocks):
    rows = blocks[0].shape[0]
    total = None
    for at, block in enumerate(blocks):
        part = dot(onehot[here, at * rows : (at + 1) * rows], block[...])
        total = part if total is None else total + part
    return total


def base_kernel(heads, gain_ref, y_ref, onehot, *rest):
    squares, blocks, out_ref = rest[:heads], rest[heads:-1], rest[-1]
    count, width = y_ref.shape
    total = squares[0][...]
    for ref in squares[1:]:
        total = total + ref[...]
    inverse = 1.0 / jnp.sqrt(total / (width * heads) + EPSILON)
    gain = gain_ref[...]
    tile = min(count, TILE)
    for low in range(0, count, tile):
        part = gathered(onehot, slice(low, low + tile), blocks)
        for at in range(0, tile, LANES):
            here = slice(low + at, low + at + LANES)
            norm = column(inverse[:, here])
            norm = jnp.concatenate([norm] * (width // LANES), axis=1)
            out_ref[here, :] = y_ref[here, :] * norm * gain + part[at : at + LANES]


def base(gain, y, onehot, squares, blocks):
    count, width = y.shape
    heads = len(squares)
    moved = len(blocks) * blocks[0].shape[0]
    return pl.pallas_call(
        functools.partial(base_kernel, heads),
        out_shape=jax.ShapeDtypeStruct((count, width), F32),
        in_specs=full(3 + heads + len(blocks)),
        out_specs=pl.BlockSpec(memory_space=pltpu.VMEM),
        compiler_params=params(),
        cost_estimate=cost(2 * count * moved * width, 8 * count * width),
        name="base",
    )(gain, y, onehot, *squares, *blocks)


def mix_kernel(base_ref, onehot, *rest):
    blocks, (out_ref, held, sems) = rest[:-3], rest[-3:]
    count = base_ref.shape[0]
    tile = min(count, TILE)
    copies = []
    for at in range(count // tile):
        here = slice(at * tile, (at + 1) * tile)
        held[here, :] = (base_ref[here, :] + gathered(onehot, here, blocks)).astype(BF16)
        copies += fetch([(held.at[here], out_ref.at[here])], sems.at[at : at + 1])
    for copy in copies:
        copy.wait()


def mix(given, onehot, blocks):
    count, width = given.shape
    moved = len(blocks) * blocks[0].shape[0]
    tile = min(count, TILE)
    return pl.pallas_call(
        mix_kernel,
        out_shape=jax.ShapeDtypeStruct((count, width), BF16),
        in_specs=full(2 + len(blocks)),
        out_specs=pl.BlockSpec(memory_space=pltpu.HBM),
        scratch_shapes=[
            pltpu.VMEM((count, width), BF16),
            pltpu.SemaphoreType.DMA((count // tile,)),
        ],
        compiler_params=params(),
        cost_estimate=cost(2 * count * moved * width, 8 * count * width),
        name="mix",
    )(given, onehot, *blocks)


def exchange(block, step, n):
    return lax.ppermute(block, "cam", routes(step, n)) if step else block


def give_back(block, step, n):
    pairs = [(target, at) for at, target in routes(step, n)]
    return lax.ppermute(block, "cam", pairs) if step else block


def per_device(queries, keys, values, rates, w_one, w_three, w_two, gain, order):
    count, width = queries.shape
    n = lax.axis_size("cam")
    heads = lax.axis_size("head")
    steps = far_first(n)
    few = max(1, n // 4)
    parts = gradients(keys, values, rates.reshape(1, count), w_one, w_three, w_two, n)
    arrived = {}
    after = []
    for at, group in enumerate((steps[:few], steps[few:])):
        blocks = sort_tokens(order, queries, keys, values, n, group, True)
        after.append(blocks[-1])
        for step, block in zip(group, blocks):
            arrived[step] = exchange(block, step, n)
    summed = sum_over_cams(parts, [after[:1], after[1:], [arrived[step] for step in steps[: 2 * few]]], n)
    y, square = read_out(queries, w_one, w_three, w_two, summed)
    squares = [square] + [
        lax.ppermute(square, "head", [(at, (at + step) % heads) for at in range(heads)])
        for step in range(1, heads)
    ]
    early = steps[:few] + steps[n - few :]
    late = steps[few : n - few]
    early_places, late_places = place(order, n, early + late)
    attended = attend(
        [arrived[step] for step in range(n)], squares + [late_places], n, width
    )
    returned = {step: give_back(attended[step], step, n) for step in early + late}
    given = base(
        gain.reshape(1, width), y, early_places, squares, [returned[step] for step in early]
    )
    return mix(given, late_places, [returned[step] for step in late])


def solution(mesh):
    in_specs = (
        P("cam", "head"),
        P("cam", "head"),
        P("cam", "head"),
        P("cam", "head"),
        P("head", None, None),
        P("head", None, None),
        P("head", None, None),
        P("head"),
        P("cam", None),
    )
    out_specs = P("cam", "head")
    return jax.shard_map(
        per_device, mesh=mesh, in_specs=in_specs, out_specs=out_specs, check_vma=False
    )
```

```python
import functools

import jax
import jax.numpy as jnp
from jax import lax
from jax.experimental import pallas as pl
from jax.experimental.pallas import tpu as pltpu
from jax.sharding import PartitionSpec as P

PATCHES = 32
EPSILON = 1e-06
LANES = 128
TILE = 512
LIMIT = 24
COST = 1
FIRST_COST = pl.CostEstimate(flops=10**12, bytes_accessed=1024, transcendentals=0)
MIB = 1024 * 1024
F32 = jnp.float32
BF16 = jnp.bfloat16
TOKEN = jax.ShapeDtypeStruct((8, LANES), F32)


def dot(a, b):
    return lax.dot_general(a, b, (((1,), (0,)), ((), ())), preferred_element_type=F32)


def dot_bt(a, b):
    return lax.dot_general(a, b, (((1,), (1,)), ((), ())), preferred_element_type=F32)


def dot_at(a, b):
    return lax.dot_general(a, b, (((0,), (0,)), ((), ())), preferred_element_type=F32)


def params(limit=LIMIT):
    return pltpu.CompilerParams(vmem_limit_bytes=int(limit * MIB))


def full(count):
    return [pl.BlockSpec(memory_space=pltpu.VMEM)] * count


def cost(flops, moved, exps=0):
    return pl.CostEstimate(
        flops=int(flops) // COST,
        bytes_accessed=int(moved) // COST,
        transcendentals=int(exps) // COST,
    )


def power_of_two(n):
    return n & (n - 1) == 0


def crossed(step):
    return (step & ~6) | ((step & 2) << 1) | ((step & 4) >> 1)


def peer(me, step, n):
    if power_of_two(n):
        if n < 8:
            return me ^ step
        odd = me & 1
        return me ^ (step * (1 - odd) + crossed(step) * odd)
    ahead = me + step
    wrap = ahead - n
    return wrap * (wrap >= 0) + ahead * (wrap < 0)


def routes(step, n):
    return [(at, int(peer(at, step, n))) for at in range(n)]


def column(row):
    return jnp.broadcast_to(row, (LANES, LANES)).T


def far_first(n):
    return sorted(range(n), key=lambda step: (-(step >> 1).bit_count(), -step))


def fetch(pairs, sems):
    copies = []
    for at, (source, target) in enumerate(pairs):
        copies.append(pltpu.make_async_copy(source, target, sems.at[at]))
        copies[-1].start()
    return copies


def mark_kernel(n, steps, order_ref, *rest):
    outs, token = rest[:-1], rest[-1]
    token[...] = jnp.zeros_like(token)
    me = lax.axis_index("cam")
    count = order_ref.shape[1]
    rows = count // n
    order = order_ref[...]
    slot = lax.broadcasted_iota(jnp.int32, (rows, count), 0)
    for group, out in zip(steps, outs):
        for at, step in enumerate(group):
            hit = slot + peer(me, step, n) * rows == order
            out[at * rows : (at + 1) * rows, :] = hit.astype(F32).astype(BF16)


def mark(order, n, steps):
    count = order.shape[1]
    rows = count // n
    return pl.pallas_call(
        functools.partial(mark_kernel, n, steps),
        out_shape=[jax.ShapeDtypeStruct((len(group) * rows, count), BF16) for group in steps]
        + [TOKEN],
        in_specs=full(1),
        out_specs=full(len(steps) + 1),
        compiler_params=params(),
        cost_estimate=FIRST_COST,
        name="mark",
    )(order)


def sort_kernel(onehot, q_ref, k_ref, v_ref, *rest):
    outs, token = rest[:-1], rest[-1]
    token[...] = jnp.zeros_like(token)
    rows, width = outs[0].shape[0], q_ref.shape[1]
    group = max(1, min(len(outs), TILE // rows))
    while len(outs) % group:
        group -= 1
    for first in range(0, len(outs), group):
        marks = onehot[first * rows : (first + group) * rows, :]
        for which, ref in enumerate((q_ref, k_ref, v_ref)):
            picked = dot(marks, ref[...]).astype(BF16)
            for at in range(group):
                outs[first + at][:, which * width : (which + 1) * width] = picked[
                    at * rows : (at + 1) * rows
                ]


def sort_tokens(onehot, q, k, v, n):
    count, width = q.shape
    rows = count // n
    size = onehot.shape[0] // rows
    return pl.pallas_call(
        sort_kernel,
        out_shape=[jax.ShapeDtypeStruct((rows, 3 * width), BF16)] * size + [TOKEN],
        in_specs=full(4),
        out_specs=full(size + 1),
        compiler_params=params(),
        cost_estimate=cost(6 * size * rows * count * width, 6 * count * width),
        name="sort_tokens",
    )(onehot, q, k, v)


def attend_kernel(n, scale, *refs):
    ins, outs = refs[:n], refs[-3 - n : -3]
    q_all, k_all, v_all = refs[-3:]
    rows = ins[0].shape[0]
    width = outs[0].shape[1]
    group = n * PATCHES
    block = min(group, 256)
    for stamp in range(rows // PATCHES):
        here = slice(stamp * PATCHES, (stamp + 1) * PATCHES)
        for cam in range(n):
            there = slice(cam * PATCHES, (cam + 1) * PATCHES)
            q_all[there, :] = ins[cam][here, 0:width]
            k_all[there, :] = ins[cam][here, width : 2 * width]
            v_all[there, :] = ins[cam][here, 2 * width : 3 * width]
        for low in range(0, group, block):
            scores = dot_bt(q_all[low : low + block, :], k_all[...]) * scale
            scores = scores - jnp.max(scores, axis=-1, keepdims=True)
            expo = jnp.exp(scores)
            probs = (expo / jnp.sum(expo, axis=-1, keepdims=True)).astype(BF16)
            result = dot(probs, v_all[...]).astype(BF16)
            for cam in range(low // PATCHES, (low + block) // PATCHES):
                at = cam * PATCHES - low
                outs[cam][here, :] = result[at : at + PATCHES]


def attend(blocks, after, n, width):
    rows = blocks[0].shape[0]
    group = n * PATCHES
    return pl.pallas_call(
        functools.partial(attend_kernel, n, width**-0.5),
        out_shape=[jax.ShapeDtypeStruct((rows, width), BF16)] * n,
        in_specs=full(n) + [pl.BlockSpec(memory_space=pl.ANY)] * len(after),
        out_specs=full(n),
        scratch_shapes=[pltpu.VMEM((group, width), BF16)] * 3,
        compiler_params=params(),
        cost_estimate=cost(
            4 * n * rows * group * width, 8 * n * rows * width, n * rows * group
        ),
        name="attend",
    )(*blocks, *after)


def grads_kernel(n, split, k_ref, v_ref, rate_ref, one_ref, three_ref, two_ref, *rest):
    outs, total = rest[1:-1], rest[-1]
    count, width = k_ref.shape
    hid = one_ref.shape[1]
    one, three, two = one_ref[0], three_ref[0], two_ref[0]
    tile = min(count, TILE)
    for start in range(0, count, tile):
        k = k_ref[start : start + tile, :]
        h_one = dot_bt(k, one)
        h_three = dot_bt(k, three)
        sigma = jax.nn.sigmoid(h_one)
        gated = h_one * sigma
        active = (gated * h_three).astype(BF16)
        pieces = []
        for low in range(start, start + tile, LANES):
            rate = column(rate_ref[:, low : low + LANES])
            rate = jnp.concatenate([rate] * (width // LANES), axis=1)
            pieces.append((-rate * v_ref[low : low + LANES, :].astype(F32)).astype(BF16))
        error = jnp.concatenate(pieces, axis=0)
        back = dot(error, two)
        back_one = (back * h_three * sigma * (1.0 + h_one * (1.0 - sigma))).astype(BF16)
        back_three = (back * gated).astype(BF16)
        sums = (dot_at(back_one, k), dot_at(back_three, k), dot_at(error, active))
        for which, term in enumerate(sums):
            here = slice(which * hid, (which + 1) * hid)
            total[here, :] = term if start == 0 else total[here, :] + term
    if split:
        half = total.shape[0] // 2
        core = lax.axis_index("cam") & 1
        outs[0][...] = total[pl.ds(pl.multiple_of(core * half, half), half), :]
        outs[1][...] = total[pl.ds(pl.multiple_of((1 - core) * half, half), half), :]
    else:
        outs[0][...] = total[...]


def gradients(k, v, rate, one, three, two, after, n):
    count, width = k.shape
    hid = one.shape[1]
    split = n > 1 and power_of_two(n)
    assert hid == width
    rows = 3 * hid
    parts = 2 if split else 1
    return pl.pallas_call(
        functools.partial(grads_kernel, n, split),
        out_shape=[jax.ShapeDtypeStruct((rows // parts, width), F32)] * parts,
        in_specs=full(6) + [pl.BlockSpec(memory_space=pl.ANY)],
        out_specs=full(parts),
        scratch_shapes=[pltpu.VMEM((rows, width), F32)],
        compiler_params=params(),
        cost_estimate=cost(12 * count * width * hid, 8 * count * width, count * hid),
        name="gradients",
    )(k, v, rate, one, three, two, after)


def merge_kernel(keep_ref, got_ref, *rest):
    rest[-1][...] = keep_ref[...] + got_ref[...].astype(F32)


def merge(keep, got, after):
    return pl.pallas_call(
        merge_kernel,
        out_shape=jax.ShapeDtypeStruct(keep.shape, F32),
        in_specs=full(2) + [pl.BlockSpec(memory_space=pl.ANY)] * len(after),
        out_specs=pl.BlockSpec(memory_space=pltpu.VMEM),
        compiler_params=params(),
        cost_estimate=cost(keep.size, 12 * keep.size),
        name="merge",
    )(keep, got, *after)


def sum_over_cams(parts, after, n):
    if len(parts) == 1:
        return [lax.psum(parts[0], "cam")]
    keep, send = parts
    bits = n.bit_length() - 1
    pair = [(at, at ^ 1) for at in range(n)]
    mine = merge(keep, lax.ppermute(send, "cam", pair), after[0])
    span = bits - 1
    for step in range(span):
        pairs = []
        for at in range(n):
            bit = 1 + (step + (at & 1)) % span
            pairs.append((at, at ^ (1 << bit)))
        got = lax.ppermute(mine.astype(BF16), "cam", pairs)
        if step + 1 < len(after):
            mine = merge(mine, got, after[step + 1])
        else:
            mine = mine + got.astype(F32)
    return [mine, lax.ppermute(mine, "cam", pair)]


def readout_kernel(parts, q_ref, one_ref, three_ref, two_ref, *rest):
    grads, (y_ref, sq_ref, total, fresh) = rest[:parts], rest[parts:]
    hid, width = one_ref.shape[1:]
    if parts == 2:
        half = total.shape[0] // 2
        core = lax.axis_index("cam") & 1
        total[pl.ds(pl.multiple_of(core * half, half), half), :] = grads[0][...]
        total[pl.ds(pl.multiple_of((1 - core) * half, half), half), :] = grads[1][...]
    else:
        total[...] = grads[0][...]
    entries = hid * width
    for which, ref in enumerate((one_ref, three_ref, two_ref)):
        grad = total[which * hid : (which + 1) * hid, :]
        weight = ref[0].astype(F32)
        row_sq = jnp.sum(weight * weight, axis=1, keepdims=True)
        weight_sq = jnp.sum(row_sq, axis=0, keepdims=True)
        grad_sq = jnp.sum(jnp.sum(grad * grad, axis=1, keepdims=True), axis=0, keepdims=True)
        scale = jnp.sqrt(weight_sq / entries) / jnp.sqrt(grad_sq / entries + EPSILON)
        moved = weight - scale * grad
        ratio = jnp.sqrt(row_sq) / jnp.sqrt(
            jnp.sum(moved * moved, axis=1, keepdims=True) + EPSILON
        )
        fresh[which * hid : (which + 1) * hid, :] = (moved * ratio).astype(BF16)
    count = q_ref.shape[0]
    tile = min(count, TILE)
    ones = jnp.ones((8, width), BF16)
    for start in range(0, count, tile):
        here = slice(start, start + tile)
        q = q_ref[here, :]
        h_one = dot_bt(q, fresh[0:hid, :])
        h_three = dot_bt(q, fresh[hid : 2 * hid, :])
        active = (h_one * jax.nn.sigmoid(h_one) * h_three).astype(BF16)
        y = dot_bt(active, fresh[2 * hid :, :])
        y_ref[here, :] = y
        square = y * y
        high = square.astype(BF16)
        low = (square - high.astype(F32)).astype(BF16)
        sq_ref[:, here] = (dot_bt(ones, high) + dot_bt(ones, low))[0:1, :]


def read_out(q, one, three, two, grads):
    count, width = q.shape
    hid = one.shape[1]
    parts = len(grads)
    return pl.pallas_call(
        functools.partial(readout_kernel, parts),
        out_shape=[
            jax.ShapeDtypeStruct((count, width), F32),
            jax.ShapeDtypeStruct((1, count), F32),
        ],
        in_specs=full(4 + parts),
        out_specs=full(2),
        scratch_shapes=[pltpu.VMEM((3 * hid, width), F32), pltpu.VMEM((3 * hid, width), BF16)],
        compiler_params=params(),
        cost_estimate=cost(6 * count * width * hid, 8 * count * width, count * hid),
        name="read_out",
    )(q, one, three, two, *grads)


def place_kernel(n, steps, order_ref, *outs):
    me = lax.axis_index("cam")
    count = order_ref.shape[1]
    rows = count // n
    size = len(steps) * rows
    at = lax.broadcasted_iota(jnp.int32, (8, size), 1)
    slots = at * 0
    for which, step in enumerate(steps):
        inside = jnp.logical_and(at >= which * rows, at < (which + 1) * rows)
        slots = jnp.where(inside, peer(me, step, n) * rows + at - which * rows, slots)
    slots = slots[0:1, :].astype(F32)
    each = outs[0].shape[1]
    for low in range(0, count, LANES):
        wanted = column(order_ref[:, low : low + LANES].astype(F32))
        for lane in range(0, size, LANES):
            hit = wanted == slots[:, lane : lane + LANES]
            out = outs[lane // each]
            start = lane % each
            out[low : low + LANES, start : start + LANES] = hit.astype(F32).astype(BF16)


def place(order, n, steps):
    count = order.shape[1]
    shape = jax.ShapeDtypeStruct((count, count // 2), BF16)
    return pl.pallas_call(
        functools.partial(place_kernel, n, tuple(steps)),
        out_shape=[shape, shape],
        in_specs=full(1),
        out_specs=full(2),
        compiler_params=params(),
        cost_estimate=cost(count * count, 2 * count * count),
        name="place",
    )(order)


def gathered(onehot, here, blocks):
    rows = blocks[0].shape[0]
    total = None
    for at, block in enumerate(blocks):
        part = dot(onehot[here, at * rows : (at + 1) * rows], block[...])
        total = part if total is None else total + part
    return total


def base_kernel(heads, gain_ref, y_ref, onehot, *rest):
    squares, blocks, out_ref = rest[:heads], rest[heads:-1], rest[-1]
    count, width = y_ref.shape
    total = squares[0][...]
    for ref in squares[1:]:
        total = total + ref[...]
    inverse = 1.0 / jnp.sqrt(total / (width * heads) + EPSILON)
    gain = gain_ref[...]
    tile = min(count, TILE)
    for low in range(0, count, tile):
        part = gathered(onehot, slice(low, low + tile), blocks)
        for at in range(0, tile, LANES):
            here = slice(low + at, low + at + LANES)
            norm = column(inverse[:, here])
            norm = jnp.concatenate([norm] * (width // LANES), axis=1)
            out_ref[here, :] = y_ref[here, :] * norm * gain + part[at : at + LANES]


def base(gain, y, onehot, squares, blocks):
    count, width = y.shape
    heads = len(squares)
    moved = len(blocks) * blocks[0].shape[0]
    return pl.pallas_call(
        functools.partial(base_kernel, heads),
        out_shape=jax.ShapeDtypeStruct((count, width), F32),
        in_specs=full(3 + heads + len(blocks)),
        out_specs=pl.BlockSpec(memory_space=pltpu.VMEM),
        compiler_params=params(),
        cost_estimate=cost(2 * count * moved * width, 8 * count * width),
        name="base",
    )(gain, y, onehot, *squares, *blocks)


def mix_kernel(base_ref, onehot, *rest):
    blocks, (out_ref, held, sems) = rest[:-3], rest[-3:]
    count = base_ref.shape[0]
    tile = min(count, TILE)
    copies = []
    for at in range(count // tile):
        here = slice(at * tile, (at + 1) * tile)
        held[here, :] = (base_ref[here, :] + gathered(onehot, here, blocks)).astype(BF16)
        copies += fetch([(held.at[here], out_ref.at[here])], sems.at[at : at + 1])
    for copy in copies:
        copy.wait()


def mix(given, onehot, blocks):
    count, width = given.shape
    moved = len(blocks) * blocks[0].shape[0]
    tile = min(count, TILE)
    return pl.pallas_call(
        mix_kernel,
        out_shape=jax.ShapeDtypeStruct((count, width), BF16),
        in_specs=full(2 + len(blocks)),
        out_specs=pl.BlockSpec(memory_space=pltpu.HBM),
        scratch_shapes=[
            pltpu.VMEM((count, width), BF16),
            pltpu.SemaphoreType.DMA((count // tile,)),
        ],
        compiler_params=params(),
        cost_estimate=cost(2 * count * moved * width, 8 * count * width),
        name="mix",
    )(given, onehot, *blocks)


def exchange(block, step, n):
    return lax.ppermute(block, "cam", routes(step, n)) if step else block


def give_back(block, step, n):
    pairs = [(target, at) for at, target in routes(step, n)]
    return lax.ppermute(block, "cam", pairs) if step else block


def per_device(queries, keys, values, rates, w_one, w_three, w_two, gain, order):
    count, width = queries.shape
    n = lax.axis_size("cam")
    heads = lax.axis_size("head")
    steps = far_first(n)
    few = max(1, n // 4)
    weights = (w_one, w_three, w_two)
    groups = (tuple(steps[:few]), tuple(steps[few:]))
    marks = mark(order, n, groups)
    parts = gradients(keys, values, rates.reshape(1, count), *weights, marks[-1], n)
    arrived = {}
    after = []
    for group, onehot in zip(groups, marks):
        blocks = sort_tokens(onehot, queries, keys, values, n)
        after.append(blocks[-1])
        for step, block in zip(group, blocks):
            arrived[step] = exchange(block, step, n)
    summed = sum_over_cams(parts, [after[:1], after[1:], [arrived[step] for step in steps[:few+1]]], n)
    y, square = read_out(queries, *weights, summed)
    squares = [square] + [
        lax.ppermute(square, "head", [(at, (at + step) % heads) for at in range(heads)])
        for step in range(1, heads)
    ]
    early = steps[:few] + steps[n - few :]
    late = steps[few : n - few]
    early_places, late_places = place(order, n, early + late)
    attended = attend(
        [arrived[step] for step in range(n)], squares + [late_places], n, width
    )
    returned = {step: give_back(attended[step], step, n) for step in early + late}
    given = base(
        gain.reshape(1, width), y, early_places, squares, [returned[step] for step in early]
    )
    return mix(given, late_places, [returned[step] for step in late])


def solution(mesh):
    in_specs = (
        P("cam", "head"),
        P("cam", "head"),
        P("cam", "head"),
        P("cam", "head"),
        P("head", None, None),
        P("head", None, None),
        P("head", None, None),
        P("head"),
        P("cam", None),
    )
    out_specs = P("cam", "head")
    return jax.shard_map(
        per_device, mesh=mesh, in_specs=in_specs, out_specs=out_specs, check_vma=False
    )
```

```python
import functools

import jax
import jax.numpy as jnp
from jax import lax
from jax.experimental import pallas as pl
from jax.experimental.pallas import tpu as pltpu
from jax.sharding import PartitionSpec as P

PATCHES = 32
EPSILON = 1e-06
LANES = 128
TILE = 512
LIMIT = 24
COST = 1
FIRST_COST = pl.CostEstimate(flops=10**12, bytes_accessed=1024, transcendentals=0)
MIB = 1024 * 1024
F32 = jnp.float32
BF16 = jnp.bfloat16
TOKEN = jax.ShapeDtypeStruct((8, LANES), F32)


def dot(a, b):
    return lax.dot_general(a, b, (((1,), (0,)), ((), ())), preferred_element_type=F32)


def dot_bt(a, b):
    return lax.dot_general(a, b, (((1,), (1,)), ((), ())), preferred_element_type=F32)


def dot_at(a, b):
    return lax.dot_general(a, b, (((0,), (0,)), ((), ())), preferred_element_type=F32)


def params(limit=LIMIT):
    return pltpu.CompilerParams(vmem_limit_bytes=int(limit * MIB))


def full(count):
    return [pl.BlockSpec(memory_space=pltpu.VMEM)] * count


def cost(flops, moved, exps=0):
    return pl.CostEstimate(
        flops=int(flops) // COST,
        bytes_accessed=int(moved) // COST,
        transcendentals=int(exps) // COST,
    )


def power_of_two(n):
    return n & (n - 1) == 0


def crossed(step):
    return (step & ~6) | ((step & 2) << 1) | ((step & 4) >> 1)


def peer(me, step, n):
    if power_of_two(n):
        if n < 8:
            return me ^ step
        odd = me & 1
        return me ^ (step * (1 - odd) + crossed(step) * odd)
    ahead = me + step
    wrap = ahead - n
    return wrap * (wrap >= 0) + ahead * (wrap < 0)


def routes(step, n):
    return [(at, int(peer(at, step, n))) for at in range(n)]


def column(row):
    return jnp.broadcast_to(row, (LANES, LANES)).T


def far_first(n):
    return sorted(range(n), key=lambda step: (-(step >> 1).bit_count(), -step))


def fetch(pairs, sems):
    copies = []
    for at, (source, target) in enumerate(pairs):
        copies.append(pltpu.make_async_copy(source, target, sems.at[at]))
        copies[-1].start()
    return copies


def mark_kernel(n, steps, order_ref, *rest):
    outs, token = rest[:-1], rest[-1]
    token[...] = jnp.zeros_like(token)
    me = lax.axis_index("cam")
    count = order_ref.shape[1]
    rows = count // n
    order = order_ref[...]
    slot = lax.broadcasted_iota(jnp.int32, (rows, count), 0)
    for group, out in zip(steps, outs):
        for at, step in enumerate(group):
            hit = slot + peer(me, step, n) * rows == order
            out[at * rows : (at + 1) * rows, :] = hit.astype(F32).astype(BF16)


def mark(order, n, steps):
    count = order.shape[1]
    rows = count // n
    return pl.pallas_call(
        functools.partial(mark_kernel, n, steps),
        out_shape=[jax.ShapeDtypeStruct((len(group) * rows, count), BF16) for group in steps]
        + [TOKEN],
        in_specs=full(1),
        out_specs=full(len(steps) + 1),
        compiler_params=params(),
        cost_estimate=FIRST_COST,
        name="mark",
    )(order)


def sort_kernel(size, onehot, q_ref, k_ref, v_ref, *rest):
    outs, token = rest[-1 - size : -1], rest[-1]
    token[...] = jnp.zeros_like(token)
    rows, width = outs[0].shape[0], q_ref.shape[1]
    group = max(1, min(len(outs), TILE // rows))
    while len(outs) % group:
        group -= 1
    for first in range(0, len(outs), group):
        marks = onehot[first * rows : (first + group) * rows, :]
        for which, ref in enumerate((q_ref, k_ref, v_ref)):
            picked = dot(marks, ref[...]).astype(BF16)
            for at in range(group):
                outs[first + at][:, which * width : (which + 1) * width] = picked[
                    at * rows : (at + 1) * rows
                ]


def sort_tokens(onehot, q, k, v, after, n):
    count, width = q.shape
    rows = count // n
    size = onehot.shape[0] // rows
    return pl.pallas_call(
        functools.partial(sort_kernel, size),
        out_shape=[jax.ShapeDtypeStruct((rows, 3 * width), BF16)] * size + [TOKEN],
        in_specs=full(4) + [pl.BlockSpec(memory_space=pl.ANY)] * len(after),
        out_specs=full(size + 1),
        compiler_params=params(),
        cost_estimate=cost(6 * size * rows * count * width, 6 * count * width),
        name="sort_tokens",
    )(onehot, q, k, v, *after)


def attend_kernel(n, scale, *refs):
    ins, outs = refs[:n], refs[-3 - n : -3]
    q_all, k_all, v_all = refs[-3:]
    rows = ins[0].shape[0]
    width = outs[0].shape[1]
    group = n * PATCHES
    block = min(group, 256)
    for stamp in range(rows // PATCHES):
        here = slice(stamp * PATCHES, (stamp + 1) * PATCHES)
        for cam in range(n):
            there = slice(cam * PATCHES, (cam + 1) * PATCHES)
            q_all[there, :] = ins[cam][here, 0:width]
            k_all[there, :] = ins[cam][here, width : 2 * width]
            v_all[there, :] = ins[cam][here, 2 * width : 3 * width]
        for low in range(0, group, block):
            scores = dot_bt(q_all[low : low + block, :], k_all[...]) * scale
            scores = scores - jnp.max(scores, axis=-1, keepdims=True)
            expo = jnp.exp(scores)
            probs = (expo / jnp.sum(expo, axis=-1, keepdims=True)).astype(BF16)
            result = dot(probs, v_all[...]).astype(BF16)
            for cam in range(low // PATCHES, (low + block) // PATCHES):
                at = cam * PATCHES - low
                outs[cam][here, :] = result[at : at + PATCHES]


def attend(blocks, after, n, width):
    rows = blocks[0].shape[0]
    group = n * PATCHES
    return pl.pallas_call(
        functools.partial(attend_kernel, n, width**-0.5),
        out_shape=[jax.ShapeDtypeStruct((rows, width), BF16)] * n,
        in_specs=full(n) + [pl.BlockSpec(memory_space=pl.ANY)] * len(after),
        out_specs=full(n),
        scratch_shapes=[pltpu.VMEM((group, width), BF16)] * 3,
        compiler_params=params(),
        cost_estimate=cost(
            4 * n * rows * group * width, 8 * n * rows * width, n * rows * group
        ),
        name="attend",
    )(*blocks, *after)


def grads_kernel(n, split, k_ref, v_ref, rate_ref, one_ref, three_ref, two_ref, *rest):
    outs, total = rest[1:-1], rest[-1]
    count, width = k_ref.shape
    hid = one_ref.shape[1]
    one, three, two = one_ref[0], three_ref[0], two_ref[0]
    tile = min(count, TILE)
    for start in range(0, count, tile):
        k = k_ref[start : start + tile, :]
        h_one = dot_bt(k, one)
        h_three = dot_bt(k, three)
        sigma = jax.nn.sigmoid(h_one)
        gated = h_one * sigma
        active = (gated * h_three).astype(BF16)
        pieces = []
        for low in range(start, start + tile, LANES):
            rate = column(rate_ref[:, low : low + LANES])
            rate = jnp.concatenate([rate] * (width // LANES), axis=1)
            pieces.append((-rate * v_ref[low : low + LANES, :].astype(F32)).astype(BF16))
        error = jnp.concatenate(pieces, axis=0)
        back = dot(error, two)
        back_one = (back * h_three * sigma * (1.0 + h_one * (1.0 - sigma))).astype(BF16)
        back_three = (back * gated).astype(BF16)
        sums = (dot_at(back_one, k), dot_at(back_three, k), dot_at(error, active))
        for which, term in enumerate(sums):
            here = slice(which * hid, (which + 1) * hid)
            total[here, :] = term if start == 0 else total[here, :] + term
    if split:
        half = total.shape[0] // 2
        core = lax.axis_index("cam") & 1
        outs[0][...] = total[pl.ds(pl.multiple_of(core * half, half), half), :]
        outs[1][...] = total[pl.ds(pl.multiple_of((1 - core) * half, half), half), :]
    else:
        outs[0][...] = total[...]


def gradients(k, v, rate, one, three, two, after, n):
    count, width = k.shape
    hid = one.shape[1]
    split = n > 1 and power_of_two(n)
    assert hid == width
    rows = 3 * hid
    parts = 2 if split else 1
    return pl.pallas_call(
        functools.partial(grads_kernel, n, split),
        out_shape=[jax.ShapeDtypeStruct((rows // parts, width), F32)] * parts,
        in_specs=full(6) + [pl.BlockSpec(memory_space=pl.ANY)],
        out_specs=full(parts),
        scratch_shapes=[pltpu.VMEM((rows, width), F32)],
        compiler_params=params(),
        cost_estimate=cost(12 * count * width * hid, 8 * count * width, count * hid),
        name="gradients",
    )(k, v, rate, one, three, two, after)


def merge_kernel(keep_ref, got_ref, *rest):
    rest[-1][...] = keep_ref[...] + got_ref[...].astype(F32)


def merge(keep, got, after):
    return pl.pallas_call(
        merge_kernel,
        out_shape=jax.ShapeDtypeStruct(keep.shape, F32),
        in_specs=full(2) + [pl.BlockSpec(memory_space=pl.ANY)] * len(after),
        out_specs=pl.BlockSpec(memory_space=pltpu.VMEM),
        compiler_params=params(),
        cost_estimate=cost(keep.size, 12 * keep.size),
        name="merge",
    )(keep, got, *after)


def core_step(parts, after, n):
    if len(parts) == 1:
        return parts[0]
    pair = [(at, at ^ 1) for at in range(n)]
    return merge(parts[0], lax.ppermute(parts[1], "cam", pair), after)


def sum_over_chips(mine, split, after, n):
    if not split:
        return [lax.psum(mine, "cam")]
    span = n.bit_length() - 2
    for step in range(span):
        pairs = []
        for at in range(n):
            bit = 1 + (step + (at & 1)) % span
            pairs.append((at, at ^ (1 << bit)))
        got = lax.ppermute(mine.astype(BF16), "cam", pairs)
        if step < len(after):
            mine = merge(mine, got, after[step])
        else:
            mine = mine + got.astype(F32)
    return [mine, lax.ppermute(mine, "cam", [(at, at ^ 1) for at in range(n)])]


def readout_kernel(parts, q_ref, one_ref, three_ref, two_ref, *rest):
    grads, (y_ref, sq_ref, total, fresh) = rest[:parts], rest[parts:]
    hid, width = one_ref.shape[1:]
    if parts == 2:
        half = total.shape[0] // 2
        core = lax.axis_index("cam") & 1
        total[pl.ds(pl.multiple_of(core * half, half), half), :] = grads[0][...]
        total[pl.ds(pl.multiple_of((1 - core) * half, half), half), :] = grads[1][...]
    else:
        total[...] = grads[0][...]
    entries = hid * width
    for which, ref in enumerate((one_ref, three_ref, two_ref)):
        grad = total[which * hid : (which + 1) * hid, :]
        weight = ref[0].astype(F32)
        row_sq = jnp.sum(weight * weight, axis=1, keepdims=True)
        weight_sq = jnp.sum(row_sq, axis=0, keepdims=True)
        grad_sq = jnp.sum(jnp.sum(grad * grad, axis=1, keepdims=True), axis=0, keepdims=True)
        scale = jnp.sqrt(weight_sq / entries) / jnp.sqrt(grad_sq / entries + EPSILON)
        moved = weight - scale * grad
        ratio = jnp.sqrt(row_sq) / jnp.sqrt(
            jnp.sum(moved * moved, axis=1, keepdims=True) + EPSILON
        )
        fresh[which * hid : (which + 1) * hid, :] = (moved * ratio).astype(BF16)
    count = q_ref.shape[0]
    tile = min(count, TILE)
    ones = jnp.ones((8, width), BF16)
    for start in range(0, count, tile):
        here = slice(start, start + tile)
        q = q_ref[here, :]
        h_one = dot_bt(q, fresh[0:hid, :])
        h_three = dot_bt(q, fresh[hid : 2 * hid, :])
        active = (h_one * jax.nn.sigmoid(h_one) * h_three).astype(BF16)
        y = dot_bt(active, fresh[2 * hid :, :])
        y_ref[here, :] = y
        square = y * y
        high = square.astype(BF16)
        low = (square - high.astype(F32)).astype(BF16)
        sq_ref[:, here] = (dot_bt(ones, high) + dot_bt(ones, low))[0:1, :]


def read_out(q, one, three, two, grads):
    count, width = q.shape
    hid = one.shape[1]
    parts = len(grads)
    return pl.pallas_call(
        functools.partial(readout_kernel, parts),
        out_shape=[
            jax.ShapeDtypeStruct((count, width), F32),
            jax.ShapeDtypeStruct((1, count), F32),
        ],
        in_specs=full(4 + parts),
        out_specs=full(2),
        scratch_shapes=[pltpu.VMEM((3 * hid, width), F32), pltpu.VMEM((3 * hid, width), BF16)],
        compiler_params=params(),
        cost_estimate=cost(6 * count * width * hid, 8 * count * width, count * hid),
        name="read_out",
    )(q, one, three, two, *grads)


def place_kernel(n, steps, order_ref, *outs):
    me = lax.axis_index("cam")
    count = order_ref.shape[1]
    rows = count // n
    size = len(steps) * rows
    at = lax.broadcasted_iota(jnp.int32, (8, size), 1)
    slots = at * 0
    for which, step in enumerate(steps):
        inside = jnp.logical_and(at >= which * rows, at < (which + 1) * rows)
        slots = jnp.where(inside, peer(me, step, n) * rows + at - which * rows, slots)
    slots = slots[0:1, :].astype(F32)
    each = outs[0].shape[1]
    for low in range(0, count, LANES):
        wanted = column(order_ref[:, low : low + LANES].astype(F32))
        for lane in range(0, size, LANES):
            hit = wanted == slots[:, lane : lane + LANES]
            out = outs[lane // each]
            start = lane % each
            out[low : low + LANES, start : start + LANES] = hit.astype(F32).astype(BF16)


def place(order, n, steps):
    count = order.shape[1]
    shape = jax.ShapeDtypeStruct((count, count // 2), BF16)
    return pl.pallas_call(
        functools.partial(place_kernel, n, tuple(steps)),
        out_shape=[shape, shape],
        in_specs=full(1),
        out_specs=full(2),
        compiler_params=params(),
        cost_estimate=cost(count * count, 2 * count * count),
        name="place",
    )(order)


def gathered(onehot, here, blocks):
    rows = blocks[0].shape[0]
    total = None
    for at, block in enumerate(blocks):
        part = dot(onehot[here, at * rows : (at + 1) * rows], block[...])
        total = part if total is None else total + part
    return total


def base_kernel(heads, gain_ref, y_ref, onehot, *rest):
    squares, blocks, out_ref = rest[:heads], rest[heads:-1], rest[-1]
    count, width = y_ref.shape
    total = squares[0][...]
    for ref in squares[1:]:
        total = total + ref[...]
    inverse = 1.0 / jnp.sqrt(total / (width * heads) + EPSILON)
    gain = gain_ref[...]
    tile = min(count, TILE)
    for low in range(0, count, tile):
        part = gathered(onehot, slice(low, low + tile), blocks)
        for at in range(0, tile, LANES):
            here = slice(low + at, low + at + LANES)
            norm = column(inverse[:, here])
            norm = jnp.concatenate([norm] * (width // LANES), axis=1)
            out_ref[here, :] = y_ref[here, :] * norm * gain + part[at : at + LANES]


def base(gain, y, onehot, squares, blocks):
    count, width = y.shape
    heads = len(squares)
    moved = len(blocks) * blocks[0].shape[0]
    return pl.pallas_call(
        functools.partial(base_kernel, heads),
        out_shape=jax.ShapeDtypeStruct((count, width), F32),
        in_specs=full(3 + heads + len(blocks)),
        out_specs=pl.BlockSpec(memory_space=pltpu.VMEM),
        compiler_params=params(),
        cost_estimate=cost(2 * count * moved * width, 8 * count * width),
        name="base",
    )(gain, y, onehot, *squares, *blocks)


def mix_kernel(base_ref, onehot, *rest):
    blocks, (out_ref, held, sems) = rest[:-3], rest[-3:]
    count = base_ref.shape[0]
    tile = min(count, TILE)
    copies = []
    for at in range(count // tile):
        here = slice(at * tile, (at + 1) * tile)
        held[here, :] = (base_ref[here, :] + gathered(onehot, here, blocks)).astype(BF16)
        copies += fetch([(held.at[here], out_ref.at[here])], sems.at[at : at + 1])
    for copy in copies:
        copy.wait()


def mix(given, onehot, blocks):
    count, width = given.shape
    moved = len(blocks) * blocks[0].shape[0]
    tile = min(count, TILE)
    return pl.pallas_call(
        mix_kernel,
        out_shape=jax.ShapeDtypeStruct((count, width), BF16),
        in_specs=full(2 + len(blocks)),
        out_specs=pl.BlockSpec(memory_space=pltpu.HBM),
        scratch_shapes=[
            pltpu.VMEM((count, width), BF16),
            pltpu.SemaphoreType.DMA((count // tile,)),
        ],
        compiler_params=params(),
        cost_estimate=cost(2 * count * moved * width, 8 * count * width),
        name="mix",
    )(given, onehot, *blocks)


def exchange(block, step, n):
    return lax.ppermute(block, "cam", routes(step, n)) if step else block


def give_back(block, step, n):
    pairs = [(target, at) for at, target in routes(step, n)]
    return lax.ppermute(block, "cam", pairs) if step else block


def per_device(queries, keys, values, rates, w_one, w_three, w_two, gain, order):
    count, width = queries.shape
    n = lax.axis_size("cam")
    heads = lax.axis_size("head")
    steps = far_first(n)
    few = max(1, n // 4)
    weights = (w_one, w_three, w_two)
    groups = (tuple(steps[:few]), tuple(steps[few:]))
    marks = mark(order, n, groups)
    parts = gradients(keys, values, rates.reshape(1, count), *weights, marks[-1], n)
    early = steps[:few] + steps[n - few :]
    late = steps[few : n - few]
    early_places, late_places = place(order, n, early + late)
    mine = core_step(parts, [late_places], n)
    arrived = {}
    tokens = []
    for group, onehot, after in zip(groups, marks, ([mine], [])):
        blocks = sort_tokens(onehot, queries, keys, values, after + tokens, n)
        tokens.append(blocks[-1])
        for step, block in zip(group, blocks):
            arrived[step] = exchange(block, step, n)
    summed = sum_over_chips(mine, len(parts) == 2, [tokens[1:] + [arrived[steps[0]], arrived[steps[1]]], [arrived[step] for step in steps[: 2 * few + 1]]], n)
    y, square = read_out(queries, *weights, summed)
    squares = [square] + [
        lax.ppermute(square, "head", [(at, (at + step) % heads) for at in range(heads)])
        for step in range(1, heads)
    ]
    attended = attend([arrived[step] for step in range(n)], [square], n, width)
    returned = {step: give_back(attended[step], step, n) for step in early + late}
    given = base(
        gain.reshape(1, width), y, early_places, squares, [returned[step] for step in early]
    )
    return mix(given, late_places, [returned[step] for step in late])


def solution(mesh):
    in_specs = (
        P("cam", "head"),
        P("cam", "head"),
        P("cam", "head"),
        P("cam", "head"),
        P("head", None, None),
        P("head", None, None),
        P("head", None, None),
        P("head"),
        P("cam", None),
    )
    out_specs = P("cam", "head")
    return jax.shard_map(
        per_device, mesh=mesh, in_specs=in_specs, out_specs=out_specs, check_vma=False
    )
```

```python
import functools

import jax
import jax.numpy as jnp
from jax import lax
from jax.experimental import pallas as pl
from jax.experimental.pallas import tpu as pltpu
from jax.sharding import PartitionSpec as P

PATCHES = 32
EPSILON = 1e-06
LANES = 128
TILE = 512
LIMIT = 24
COST = 1
FIRST_COST = pl.CostEstimate(flops=10**12, bytes_accessed=1024, transcendentals=0)
MIB = 1024 * 1024
F32 = jnp.float32
BF16 = jnp.bfloat16
TOKEN = jax.ShapeDtypeStruct((8, LANES), F32)


def dot(a, b):
    return lax.dot_general(a, b, (((1,), (0,)), ((), ())), preferred_element_type=F32)


def dot_bt(a, b):
    return lax.dot_general(a, b, (((1,), (1,)), ((), ())), preferred_element_type=F32)


def dot_at(a, b):
    return lax.dot_general(a, b, (((0,), (0,)), ((), ())), preferred_element_type=F32)


def params(limit=LIMIT):
    return pltpu.CompilerParams(vmem_limit_bytes=int(limit * MIB))


def full(count):
    return [pl.BlockSpec(memory_space=pltpu.VMEM)] * count


def cost(flops, moved, exps=0):
    return pl.CostEstimate(
        flops=int(flops) // COST,
        bytes_accessed=int(moved) // COST,
        transcendentals=int(exps) // COST,
    )


def power_of_two(n):
    return n & (n - 1) == 0


def crossed(step):
    return (step & ~6) | ((step & 2) << 1) | ((step & 4) >> 1)


def peer(me, step, n):
    if power_of_two(n):
        if n < 8:
            return me ^ step
        odd = me & 1
        return me ^ (step * (1 - odd) + crossed(step) * odd)
    ahead = me + step
    wrap = ahead - n
    return wrap * (wrap >= 0) + ahead * (wrap < 0)


def routes(step, n):
    return [(at, int(peer(at, step, n))) for at in range(n)]


def column(row):
    return jnp.broadcast_to(row, (LANES, LANES)).T


def far_first(n):
    return sorted(range(n), key=lambda step: (-(step >> 1).bit_count(), -step))


def fetch(pairs, sems):
    copies = []
    for at, (source, target) in enumerate(pairs):
        copies.append(pltpu.make_async_copy(source, target, sems.at[at]))
        copies[-1].start()
    return copies


def mark_kernel(n, steps, order_ref, *rest):
    outs, token = rest[:-1], rest[-1]
    token[...] = jnp.zeros_like(token)
    me = lax.axis_index("cam")
    count = order_ref.shape[1]
    rows = count // n
    order = order_ref[...]
    slot = lax.broadcasted_iota(jnp.int32, (rows, count), 0)
    for group, out in zip(steps, outs):
        for at, step in enumerate(group):
            hit = slot + peer(me, step, n) * rows == order
            out[at * rows : (at + 1) * rows, :] = hit.astype(F32).astype(BF16)


def mark(order, n, steps):
    count = order.shape[1]
    rows = count // n
    return pl.pallas_call(
        functools.partial(mark_kernel, n, steps),
        out_shape=[jax.ShapeDtypeStruct((len(group) * rows, count), BF16) for group in steps]
        + [TOKEN],
        in_specs=full(1),
        out_specs=full(len(steps) + 1),
        compiler_params=params(),
        cost_estimate=FIRST_COST,
        name="mark",
    )(order)


def sort_kernel(size, onehot, q_ref, k_ref, v_ref, *rest):
    outs, token = rest[-1 - size : -1], rest[-1]
    token[...] = jnp.zeros_like(token)
    rows, width = outs[0].shape[0], q_ref.shape[1]
    group = max(1, min(len(outs), TILE // rows))
    while len(outs) % group:
        group -= 1
    for first in range(0, len(outs), group):
        marks = onehot[first * rows : (first + group) * rows, :]
        for which, ref in enumerate((q_ref, k_ref, v_ref)):
            picked = dot(marks, ref[...]).astype(BF16)
            for at in range(group):
                outs[first + at][:, which * width : (which + 1) * width] = picked[
                    at * rows : (at + 1) * rows
                ]


def sort_tokens(onehot, q, k, v, after, n):
    count, width = q.shape
    rows = count // n
    size = onehot.shape[0] // rows
    return pl.pallas_call(
        functools.partial(sort_kernel, size),
        out_shape=[jax.ShapeDtypeStruct((rows, 3 * width), BF16)] * size + [TOKEN],
        in_specs=full(4) + [pl.BlockSpec(memory_space=pl.ANY)] * len(after),
        out_specs=full(size + 1),
        compiler_params=params(),
        cost_estimate=cost(6 * size * rows * count * width, 6 * count * width),
        name="sort_tokens",
    )(onehot, q, k, v, *after)


def attend_kernel(n, scale, *refs):
    ins, outs = refs[:n], refs[-3 - n : -3]
    q_all, k_all, v_all = refs[-3:]
    rows = ins[0].shape[0]
    width = outs[0].shape[1]
    group = n * PATCHES
    block = min(group, 256)
    for stamp in range(rows // PATCHES):
        here = slice(stamp * PATCHES, (stamp + 1) * PATCHES)
        for cam in range(n):
            there = slice(cam * PATCHES, (cam + 1) * PATCHES)
            q_all[there, :] = ins[cam][here, 0:width]
            k_all[there, :] = ins[cam][here, width : 2 * width]
            v_all[there, :] = ins[cam][here, 2 * width : 3 * width]
        for low in range(0, group, block):
            scores = dot_bt(q_all[low : low + block, :], k_all[...]) * scale
            scores = scores - jnp.max(scores, axis=-1, keepdims=True)
            expo = jnp.exp(scores)
            probs = (expo / jnp.sum(expo, axis=-1, keepdims=True)).astype(BF16)
            result = dot(probs, v_all[...]).astype(BF16)
            for cam in range(low // PATCHES, (low + block) // PATCHES):
                at = cam * PATCHES - low
                outs[cam][here, :] = result[at : at + PATCHES]


def attend(blocks, after, n, width):
    rows = blocks[0].shape[0]
    group = n * PATCHES
    return pl.pallas_call(
        functools.partial(attend_kernel, n, width**-0.5),
        out_shape=[jax.ShapeDtypeStruct((rows, width), BF16)] * n,
        in_specs=full(n) + [pl.BlockSpec(memory_space=pl.ANY)] * len(after),
        out_specs=full(n),
        scratch_shapes=[pltpu.VMEM((group, width), BF16)] * 3,
        compiler_params=params(),
        cost_estimate=cost(
            4 * n * rows * group * width, 8 * n * rows * width, n * rows * group
        ),
        name="attend",
    )(*blocks, *after)


def grads_kernel(n, split, k_ref, v_ref, rate_ref, one_ref, three_ref, two_ref, *rest):
    outs, total = rest[1:-1], rest[-1]
    count, width = k_ref.shape
    hid = one_ref.shape[1]
    one, three, two = one_ref[0], three_ref[0], two_ref[0]
    tile = min(count, TILE)
    for start in range(0, count, tile):
        k = k_ref[start : start + tile, :]
        h_one = dot_bt(k, one)
        h_three = dot_bt(k, three)
        sigma = jax.nn.sigmoid(h_one)
        gated = h_one * sigma
        active = (gated * h_three).astype(BF16)
        pieces = []
        for low in range(start, start + tile, LANES):
            rate = column(rate_ref[:, low : low + LANES])
            rate = jnp.concatenate([rate] * (width // LANES), axis=1)
            pieces.append((-rate * v_ref[low : low + LANES, :].astype(F32)).astype(BF16))
        error = jnp.concatenate(pieces, axis=0)
        back = dot(error, two)
        back_one = (back * h_three * sigma * (1.0 + h_one * (1.0 - sigma))).astype(BF16)
        back_three = (back * gated).astype(BF16)
        sums = (dot_at(back_one, k), dot_at(back_three, k), dot_at(error, active))
        for which, term in enumerate(sums):
            here = slice(which * hid, (which + 1) * hid)
            total[here, :] = term if start == 0 else total[here, :] + term
    if split:
        half = total.shape[0] // 2
        core = lax.axis_index("cam") & 1
        outs[0][...] = total[pl.ds(pl.multiple_of(core * half, half), half), :]
        outs[1][...] = total[pl.ds(pl.multiple_of((1 - core) * half, half), half), :]
    else:
        outs[0][...] = total[...]


def gradients(k, v, rate, one, three, two, after, n):
    count, width = k.shape
    hid = one.shape[1]
    split = n > 1 and power_of_two(n)
    assert hid == width
    rows = 3 * hid
    parts = 2 if split else 1
    return pl.pallas_call(
        functools.partial(grads_kernel, n, split),
        out_shape=[jax.ShapeDtypeStruct((rows // parts, width), F32)] * parts,
        in_specs=full(6) + [pl.BlockSpec(memory_space=pl.ANY)],
        out_specs=full(parts),
        scratch_shapes=[pltpu.VMEM((rows, width), F32)],
        compiler_params=params(),
        cost_estimate=cost(12 * count * width * hid, 8 * count * width, count * hid),
        name="gradients",
    )(k, v, rate, one, three, two, after)


def merge_kernel(keep_ref, got_ref, *rest):
    rest[-1][...] = keep_ref[...] + got_ref[...].astype(F32)


def merge(keep, got, after):
    return pl.pallas_call(
        merge_kernel,
        out_shape=jax.ShapeDtypeStruct(keep.shape, F32),
        in_specs=full(2) + [pl.BlockSpec(memory_space=pl.ANY)] * len(after),
        out_specs=pl.BlockSpec(memory_space=pltpu.VMEM),
        compiler_params=params(),
        cost_estimate=cost(keep.size, 12 * keep.size),
        name="merge",
    )(keep, got, *after)


def core_step(parts, after, n):
    if len(parts) == 1:
        return parts[0]
    pair = [(at, at ^ 1) for at in range(n)]
    return merge(parts[0], lax.ppermute(parts[1], "cam", pair), after)


def sum_over_chips(mine, split, after, n):
    if not split:
        return [lax.psum(mine, "cam")]
    span = n.bit_length() - 2
    for step in range(span):
        pairs = []
        for at in range(n):
            bit = 1 + (step + (at & 1)) % span
            pairs.append((at, at ^ (1 << bit)))
        got = lax.ppermute(mine.astype(BF16), "cam", pairs)
        if step < len(after):
            mine = merge(mine, got, after[step])
        else:
            mine = mine + got.astype(F32)
    return [mine, lax.ppermute(mine, "cam", [(at, at ^ 1) for at in range(n)])]


def readout_kernel(parts, q_ref, one_ref, three_ref, two_ref, *rest):
    grads, (y_ref, sq_ref, total, fresh) = rest[:parts], rest[-4:]
    hid, width = one_ref.shape[1:]
    if parts == 2:
        half = total.shape[0] // 2
        core = lax.axis_index("cam") & 1
        total[pl.ds(pl.multiple_of(core * half, half), half), :] = grads[0][...]
        total[pl.ds(pl.multiple_of((1 - core) * half, half), half), :] = grads[1][...]
    else:
        total[...] = grads[0][...]
    entries = hid * width
    for which, ref in enumerate((one_ref, three_ref, two_ref)):
        grad = total[which * hid : (which + 1) * hid, :]
        weight = ref[0].astype(F32)
        row_sq = jnp.sum(weight * weight, axis=1, keepdims=True)
        weight_sq = jnp.sum(row_sq, axis=0, keepdims=True)
        grad_sq = jnp.sum(jnp.sum(grad * grad, axis=1, keepdims=True), axis=0, keepdims=True)
        scale = jnp.sqrt(weight_sq / entries) / jnp.sqrt(grad_sq / entries + EPSILON)
        moved = weight - scale * grad
        ratio = jnp.sqrt(row_sq) / jnp.sqrt(
            jnp.sum(moved * moved, axis=1, keepdims=True) + EPSILON
        )
        fresh[which * hid : (which + 1) * hid, :] = (moved * ratio).astype(BF16)
    count = q_ref.shape[0]
    tile = min(count, TILE)
    ones = jnp.ones((8, width), BF16)
    for start in range(0, count, tile):
        here = slice(start, start + tile)
        q = q_ref[here, :]
        h_one = dot_bt(q, fresh[0:hid, :])
        h_three = dot_bt(q, fresh[hid : 2 * hid, :])
        active = (h_one * jax.nn.sigmoid(h_one) * h_three).astype(BF16)
        y = dot_bt(active, fresh[2 * hid :, :])
        y_ref[here, :] = y
        square = y * y
        high = square.astype(BF16)
        low = (square - high.astype(F32)).astype(BF16)
        sq_ref[:, here] = (dot_bt(ones, high) + dot_bt(ones, low))[0:1, :]


def read_out(q, one, three, two, grads, after):
    count, width = q.shape
    hid = one.shape[1]
    parts = len(grads)
    return pl.pallas_call(
        functools.partial(readout_kernel, parts),
        out_shape=[
            jax.ShapeDtypeStruct((count, width), F32),
            jax.ShapeDtypeStruct((1, count), F32),
        ],
        in_specs=full(4 + parts) + [pl.BlockSpec(memory_space=pl.ANY)] * len(after),
        out_specs=full(2),
        scratch_shapes=[pltpu.VMEM((3 * hid, width), F32), pltpu.VMEM((3 * hid, width), BF16)],
        compiler_params=params(),
        cost_estimate=cost(6 * count * width * hid, 8 * count * width, count * hid),
        name="read_out",
    )(q, one, three, two, *grads, *after)


def place_kernel(n, steps, order_ref, *outs):
    me = lax.axis_index("cam")
    count = order_ref.shape[1]
    rows = count // n
    size = len(steps) * rows
    at = lax.broadcasted_iota(jnp.int32, (8, size), 1)
    slots = at * 0
    for which, step in enumerate(steps):
        inside = jnp.logical_and(at >= which * rows, at < (which + 1) * rows)
        slots = jnp.where(inside, peer(me, step, n) * rows + at - which * rows, slots)
    slots = slots[0:1, :].astype(F32)
    each = outs[0].shape[1]
    for low in range(0, count, LANES):
        wanted = column(order_ref[:, low : low + LANES].astype(F32))
        for lane in range(0, size, LANES):
            hit = wanted == slots[:, lane : lane + LANES]
            out = outs[lane // each]
            start = lane % each
            out[low : low + LANES, start : start + LANES] = hit.astype(F32).astype(BF16)


def place(order, n, steps):
    count = order.shape[1]
    shape = jax.ShapeDtypeStruct((count, count // 2), BF16)
    return pl.pallas_call(
        functools.partial(place_kernel, n, tuple(steps)),
        out_shape=[shape, shape],
        in_specs=full(1),
        out_specs=full(2),
        compiler_params=params(),
        cost_estimate=cost(count * count, 2 * count * count),
        name="place",
    )(order)


def gathered(onehot, here, blocks):
    rows = blocks[0].shape[0]
    total = None
    for at, block in enumerate(blocks):
        part = dot(onehot[here, at * rows : (at + 1) * rows], block[...])
        total = part if total is None else total + part
    return total


def base_kernel(heads, gain_ref, y_ref, onehot, *rest):
    squares, blocks, out_ref = rest[:heads], rest[heads:-1], rest[-1]
    count, width = y_ref.shape
    total = squares[0][...]
    for ref in squares[1:]:
        total = total + ref[...]
    inverse = 1.0 / jnp.sqrt(total / (width * heads) + EPSILON)
    gain = gain_ref[...]
    tile = min(count, TILE)
    for low in range(0, count, tile):
        part = gathered(onehot, slice(low, low + tile), blocks)
        for at in range(0, tile, LANES):
            here = slice(low + at, low + at + LANES)
            norm = column(inverse[:, here])
            norm = jnp.concatenate([norm] * (width // LANES), axis=1)
            out_ref[here, :] = y_ref[here, :] * norm * gain + part[at : at + LANES]


def base(gain, y, onehot, squares, blocks):
    count, width = y.shape
    heads = len(squares)
    moved = len(blocks) * blocks[0].shape[0]
    return pl.pallas_call(
        functools.partial(base_kernel, heads),
        out_shape=jax.ShapeDtypeStruct((count, width), F32),
        in_specs=full(3 + heads + len(blocks)),
        out_specs=pl.BlockSpec(memory_space=pltpu.VMEM),
        compiler_params=params(),
        cost_estimate=cost(2 * count * moved * width, 8 * count * width),
        name="base",
    )(gain, y, onehot, *squares, *blocks)


def mix_kernel(base_ref, onehot, *rest):
    blocks, (out_ref, held, sems) = rest[:-3], rest[-3:]
    count = base_ref.shape[0]
    tile = min(count, TILE)
    copies = []
    for at in range(count // tile):
        here = slice(at * tile, (at + 1) * tile)
        held[here, :] = (base_ref[here, :] + gathered(onehot, here, blocks)).astype(BF16)
        copies += fetch([(held.at[here], out_ref.at[here])], sems.at[at : at + 1])
    for copy in copies:
        copy.wait()


def mix(given, onehot, blocks):
    count, width = given.shape
    moved = len(blocks) * blocks[0].shape[0]
    tile = min(count, TILE)
    return pl.pallas_call(
        mix_kernel,
        out_shape=jax.ShapeDtypeStruct((count, width), BF16),
        in_specs=full(2 + len(blocks)),
        out_specs=pl.BlockSpec(memory_space=pltpu.HBM),
        scratch_shapes=[
            pltpu.VMEM((count, width), BF16),
            pltpu.SemaphoreType.DMA((count // tile,)),
        ],
        compiler_params=params(),
        cost_estimate=cost(2 * count * moved * width, 8 * count * width),
        name="mix",
    )(given, onehot, *blocks)


def exchange(block, step, n):
    return lax.ppermute(block, "cam", routes(step, n)) if step else block


def give_back(block, step, n):
    pairs = [(target, at) for at, target in routes(step, n)]
    return lax.ppermute(block, "cam", pairs) if step else block


def per_device(queries, keys, values, rates, w_one, w_three, w_two, gain, order):
    count, width = queries.shape
    n = lax.axis_size("cam")
    heads = lax.axis_size("head")
    steps = far_first(n)
    few = max(1, n // 4)
    weights = (w_one, w_three, w_two)
    groups = (tuple(steps[:few]), tuple(steps[few : 2 * few]), tuple(steps[2 * few :]))
    marks = mark(order, n, groups)
    parts = gradients(keys, values, rates.reshape(1, count), *weights, marks[-1], n)
    arrived = {}
    tokens = []
    for group, onehot in zip(groups, marks):
        blocks = sort_tokens(onehot, queries, keys, values, [], n)
        tokens.append(blocks[-1])
        for step, block in zip(group, blocks):
            arrived[step] = exchange(block, step, n)
    mine = core_step(parts, tokens[:1], n)
    summed = sum_over_chips(mine, len(parts) == 2, [tokens[1:2], [arrived[s] for s in steps[:2]] + tokens[2:]], n)
    early = steps[:few] + steps[n - few :]
    late = steps[few : n - few]
    early_places, late_places = place(order, n, early + late)
    y, square = read_out(queries, *weights, summed, [late_places])
    squares = [square] + [
        lax.ppermute(square, "head", [(at, (at + step) % heads) for at in range(heads)])
        for step in range(1, heads)
    ]
    attended = attend([arrived[step] for step in range(n)], squares, n, width)
    returned = {step: give_back(attended[step], step, n) for step in early + late}
    given = base(
        gain.reshape(1, width), y, early_places, squares, [returned[step] for step in early]
    )
    return mix(given, late_places, [returned[step] for step in late])


def solution(mesh):
    in_specs = (
        P("cam", "head"),
        P("cam", "head"),
        P("cam", "head"),
        P("cam", "head"),
        P("head", None, None),
        P("head", None, None),
        P("head", None, None),
        P("head"),
        P("cam", None),
    )
    out_specs = P("cam", "head")
    return jax.shard_map(
        per_device, mesh=mesh, in_specs=in_specs, out_specs=out_specs, check_vma=False
    )
```

```python
import functools

import jax
import jax.numpy as jnp
from jax import lax
from jax.experimental import pallas as pl
from jax.experimental.pallas import tpu as pltpu
from jax.sharding import PartitionSpec as P

PATCHES = 32
EPSILON = 1e-06
LANES = 128
TILE = 512
LIMIT = 24
COST = 1
FIRST_COST = pl.CostEstimate(flops=10**12, bytes_accessed=1024, transcendentals=0)
MIB = 1024 * 1024
F32 = jnp.float32
BF16 = jnp.bfloat16
TOKEN = jax.ShapeDtypeStruct((8, LANES), F32)


def dot(a, b):
    return lax.dot_general(a, b, (((1,), (0,)), ((), ())), preferred_element_type=F32)


def dot_bt(a, b):
    return lax.dot_general(a, b, (((1,), (1,)), ((), ())), preferred_element_type=F32)


def dot_at(a, b):
    return lax.dot_general(a, b, (((0,), (0,)), ((), ())), preferred_element_type=F32)


def params(limit=LIMIT):
    return pltpu.CompilerParams(vmem_limit_bytes=int(limit * MIB))


def full(count):
    return [pl.BlockSpec(memory_space=pltpu.VMEM)] * count


def cost(flops, moved, exps=0):
    return pl.CostEstimate(
        flops=int(flops) // COST,
        bytes_accessed=int(moved) // COST,
        transcendentals=int(exps) // COST,
    )


def power_of_two(n):
    return n & (n - 1) == 0


def crossed(step):
    return (step & ~6) | ((step & 2) << 1) | ((step & 4) >> 1)


def peer(me, step, n):
    if power_of_two(n):
        if n < 8:
            return me ^ step
        odd = me & 1
        return me ^ (step * (1 - odd) + crossed(step) * odd)
    ahead = me + step
    wrap = ahead - n
    return wrap * (wrap >= 0) + ahead * (wrap < 0)


def routes(step, n):
    return [(at, int(peer(at, step, n))) for at in range(n)]


def column(row):
    return jnp.broadcast_to(row, (LANES, LANES)).T


def far_first(n):
    return sorted(range(n), key=lambda step: (-(step >> 1).bit_count(), -step))


def fetch(pairs, sems):
    copies = []
    for at, (source, target) in enumerate(pairs):
        copies.append(pltpu.make_async_copy(source, target, sems.at[at]))
        copies[-1].start()
    return copies


def mark_kernel(n, steps, order_ref, *rest):
    outs, token = rest[:-1], rest[-1]
    token[...] = jnp.zeros_like(token)
    me = lax.axis_index("cam")
    count = order_ref.shape[1]
    rows = count // n
    order = order_ref[...]
    slot = lax.broadcasted_iota(jnp.int32, (rows, count), 0)
    for group, out in zip(steps, outs):
        for at, step in enumerate(group):
            hit = slot + peer(me, step, n) * rows == order
            out[at * rows : (at + 1) * rows, :] = hit.astype(F32).astype(BF16)


def mark(order, n, steps):
    count = order.shape[1]
    rows = count // n
    return pl.pallas_call(
        functools.partial(mark_kernel, n, steps),
        out_shape=[jax.ShapeDtypeStruct((len(group) * rows, count), BF16) for group in steps]
        + [TOKEN],
        in_specs=full(1),
        out_specs=full(len(steps) + 1),
        compiler_params=params(),
        cost_estimate=FIRST_COST,
        name="mark",
    )(order)


def sort_kernel(size, onehot, q_ref, k_ref, v_ref, *rest):
    outs, token = rest[-1 - size : -1], rest[-1]
    token[...] = jnp.zeros_like(token)
    rows, width = outs[0].shape[0], q_ref.shape[1]
    group = max(1, min(len(outs), TILE // rows))
    while len(outs) % group:
        group -= 1
    for first in range(0, len(outs), group):
        marks = onehot[first * rows : (first + group) * rows, :]
        for which, ref in enumerate((q_ref, k_ref, v_ref)):
            picked = dot(marks, ref[...]).astype(BF16)
            for at in range(group):
                outs[first + at][:, which * width : (which + 1) * width] = picked[
                    at * rows : (at + 1) * rows
                ]


def sort_tokens(onehot, q, k, v, after, n):
    count, width = q.shape
    rows = count // n
    size = onehot.shape[0] // rows
    return pl.pallas_call(
        functools.partial(sort_kernel, size),
        out_shape=[jax.ShapeDtypeStruct((rows, 3 * width), BF16)] * size + [TOKEN],
        in_specs=full(4) + [pl.BlockSpec(memory_space=pl.ANY)] * len(after),
        out_specs=full(size + 1),
        compiler_params=params(),
        cost_estimate=cost(6 * size * rows * count * width, 6 * count * width),
        name="sort_tokens",
    )(onehot, q, k, v, *after)


def attend_kernel(n, scale, *refs):
    ins, outs = refs[:n], refs[-3 - n : -3]
    q_all, k_all, v_all = refs[-3:]
    rows = ins[0].shape[0]
    width = outs[0].shape[1]
    group = n * PATCHES
    block = min(group, 256)
    for stamp in range(rows // PATCHES):
        here = slice(stamp * PATCHES, (stamp + 1) * PATCHES)
        for cam in range(n):
            there = slice(cam * PATCHES, (cam + 1) * PATCHES)
            q_all[there, :] = ins[cam][here, 0:width]
            k_all[there, :] = ins[cam][here, width : 2 * width]
            v_all[there, :] = ins[cam][here, 2 * width : 3 * width]
        for low in range(0, group, block):
            scores = dot_bt(q_all[low : low + block, :], k_all[...]) * scale
            scores = scores - jnp.max(scores, axis=-1, keepdims=True)
            expo = jnp.exp(scores)
            probs = (expo / jnp.sum(expo, axis=-1, keepdims=True)).astype(BF16)
            result = dot(probs, v_all[...]).astype(BF16)
            for cam in range(low // PATCHES, (low + block) // PATCHES):
                at = cam * PATCHES - low
                outs[cam][here, :] = result[at : at + PATCHES]


def attend(blocks, after, n, width):
    rows = blocks[0].shape[0]
    group = n * PATCHES
    return pl.pallas_call(
        functools.partial(attend_kernel, n, width**-0.5),
        out_shape=[jax.ShapeDtypeStruct((rows, width), BF16)] * n,
        in_specs=full(n) + [pl.BlockSpec(memory_space=pl.ANY)] * len(after),
        out_specs=full(n),
        scratch_shapes=[pltpu.VMEM((group, width), BF16)] * 3,
        compiler_params=params(),
        cost_estimate=cost(
            4 * n * rows * group * width, 8 * n * rows * width, n * rows * group
        ),
        name="attend",
    )(*blocks, *after)


def grads_kernel(n, split, k_ref, v_ref, rate_ref, one_ref, three_ref, two_ref, *rest):
    outs, total = rest[1:-1], rest[-1]
    count, width = k_ref.shape
    hid = one_ref.shape[1]
    one, three, two = one_ref[0], three_ref[0], two_ref[0]
    tile = min(count, TILE)
    for start in range(0, count, tile):
        k = k_ref[start : start + tile, :]
        h_one = dot_bt(k, one)
        h_three = dot_bt(k, three)
        sigma = jax.nn.sigmoid(h_one)
        gated = h_one * sigma
        active = (gated * h_three).astype(BF16)
        pieces = []
        for low in range(start, start + tile, LANES):
            rate = column(rate_ref[:, low : low + LANES])
            rate = jnp.concatenate([rate] * (width // LANES), axis=1)
            pieces.append((-rate * v_ref[low : low + LANES, :].astype(F32)).astype(BF16))
        error = jnp.concatenate(pieces, axis=0)
        back = dot(error, two)
        back_one = (back * h_three * sigma * (1.0 + h_one * (1.0 - sigma))).astype(BF16)
        back_three = (back * gated).astype(BF16)
        sums = (dot_at(back_one, k), dot_at(back_three, k), dot_at(error, active))
        for which, term in enumerate(sums):
            here = slice(which * hid, (which + 1) * hid)
            total[here, :] = term if start == 0 else total[here, :] + term
    if split:
        half = total.shape[0] // 2
        core = lax.axis_index("cam") & 1
        outs[0][...] = total[pl.ds(pl.multiple_of(core * half, half), half), :]
        outs[1][...] = total[pl.ds(pl.multiple_of((1 - core) * half, half), half), :]
    else:
        outs[0][...] = total[...]


def gradients(k, v, rate, one, three, two, after, n):
    count, width = k.shape
    hid = one.shape[1]
    split = n > 1 and power_of_two(n)
    assert hid == width
    rows = 3 * hid
    parts = 2 if split else 1
    return pl.pallas_call(
        functools.partial(grads_kernel, n, split),
        out_shape=[jax.ShapeDtypeStruct((rows // parts, width), F32)] * parts,
        in_specs=full(6) + [pl.BlockSpec(memory_space=pl.ANY)],
        out_specs=full(parts),
        scratch_shapes=[pltpu.VMEM((rows, width), F32)],
        compiler_params=params(),
        cost_estimate=cost(12 * count * width * hid, 8 * count * width, count * hid),
        name="gradients",
    )(k, v, rate, one, three, two, after)


def merge_kernel(keep_ref, got_ref, *rest):
    rest[-1][...] = keep_ref[...] + got_ref[...].astype(F32)


def merge(keep, got, after):
    return pl.pallas_call(
        merge_kernel,
        out_shape=jax.ShapeDtypeStruct(keep.shape, F32),
        in_specs=full(2) + [pl.BlockSpec(memory_space=pl.ANY)] * len(after),
        out_specs=pl.BlockSpec(memory_space=pltpu.VMEM),
        compiler_params=params(),
        cost_estimate=cost(keep.size, 12 * keep.size),
        name="merge",
    )(keep, got, *after)


def core_step(parts, after, n):
    if len(parts) == 1:
        return parts[0]
    pair = [(at, at ^ 1) for at in range(n)]
    return merge(parts[0], lax.ppermute(parts[1], "cam", pair), after)


def sum_over_chips(mine, split, after, n):
    if not split:
        return [lax.psum(mine, "cam")]
    span = n.bit_length() - 2
    for step in range(span):
        pairs = []
        for at in range(n):
            bit = 1 + (step + (at & 1)) % span
            pairs.append((at, at ^ (1 << bit)))
        got = lax.ppermute(mine.astype(BF16), "cam", pairs)
        if step < len(after):
            mine = merge(mine, got, after[step])
        else:
            mine = mine + got.astype(F32)
    return [mine, lax.ppermute(mine, "cam", [(at, at ^ 1) for at in range(n)])]


def readout_kernel(parts, q_ref, one_ref, three_ref, two_ref, *rest):
    grads, (y_ref, sq_ref, total, fresh) = rest[:parts], rest[-4:]
    hid, width = one_ref.shape[1:]
    if parts == 2:
        half = total.shape[0] // 2
        core = lax.axis_index("cam") & 1
        total[pl.ds(pl.multiple_of(core * half, half), half), :] = grads[0][...]
        total[pl.ds(pl.multiple_of((1 - core) * half, half), half), :] = grads[1][...]
    else:
        total[...] = grads[0][...]
    entries = hid * width
    for which, ref in enumerate((one_ref, three_ref, two_ref)):
        grad = total[which * hid : (which + 1) * hid, :]
        weight = ref[0].astype(F32)
        row_sq = jnp.sum(weight * weight, axis=1, keepdims=True)
        weight_sq = jnp.sum(row_sq, axis=0, keepdims=True)
        grad_sq = jnp.sum(jnp.sum(grad * grad, axis=1, keepdims=True), axis=0, keepdims=True)
        scale = jnp.sqrt(weight_sq / entries) / jnp.sqrt(grad_sq / entries + EPSILON)
        moved = weight - scale * grad
        ratio = jnp.sqrt(row_sq) / jnp.sqrt(
            jnp.sum(moved * moved, axis=1, keepdims=True) + EPSILON
        )
        fresh[which * hid : (which + 1) * hid, :] = (moved * ratio).astype(BF16)
    count = q_ref.shape[0]
    tile = min(count, TILE)
    ones = jnp.ones((8, width), BF16)
    for start in range(0, count, tile):
        here = slice(start, start + tile)
        q = q_ref[here, :]
        h_one = dot_bt(q, fresh[0:hid, :])
        h_three = dot_bt(q, fresh[hid : 2 * hid, :])
        active = (h_one * jax.nn.sigmoid(h_one) * h_three).astype(BF16)
        y = dot_bt(active, fresh[2 * hid :, :])
        y_ref[here, :] = y
        square = y * y
        high = square.astype(BF16)
        low = (square - high.astype(F32)).astype(BF16)
        sq_ref[:, here] = (dot_bt(ones, high) + dot_bt(ones, low))[0:1, :]


def read_out(q, one, three, two, grads, after):
    count, width = q.shape
    hid = one.shape[1]
    parts = len(grads)
    return pl.pallas_call(
        functools.partial(readout_kernel, parts),
        out_shape=[
            jax.ShapeDtypeStruct((count, width), F32),
            jax.ShapeDtypeStruct((1, count), F32),
        ],
        in_specs=full(4 + parts) + [pl.BlockSpec(memory_space=pl.ANY)] * len(after),
        out_specs=full(2),
        scratch_shapes=[pltpu.VMEM((3 * hid, width), F32), pltpu.VMEM((3 * hid, width), BF16)],
        compiler_params=params(),
        cost_estimate=cost(6 * count * width * hid, 8 * count * width, count * hid),
        name="read_out",
    )(q, one, three, two, *grads, *after)


def place_kernel(n, steps, order_ref, *outs):
    me = lax.axis_index("cam")
    count = order_ref.shape[1]
    rows = count // n
    size = len(steps) * rows
    at = lax.broadcasted_iota(jnp.int32, (8, size), 1)
    slots = at * 0
    for which, step in enumerate(steps):
        inside = jnp.logical_and(at >= which * rows, at < (which + 1) * rows)
        slots = jnp.where(inside, peer(me, step, n) * rows + at - which * rows, slots)
    slots = slots[0:1, :].astype(F32)
    each = outs[0].shape[1]
    for low in range(0, count, LANES):
        wanted = column(order_ref[:, low : low + LANES].astype(F32))
        for lane in range(0, size, LANES):
            hit = wanted == slots[:, lane : lane + LANES]
            out = outs[lane // each]
            start = lane % each
            out[low : low + LANES, start : start + LANES] = hit.astype(F32).astype(BF16)


def place(order, n, steps):
    count = order.shape[1]
    shape = jax.ShapeDtypeStruct((count, count // 2), BF16)
    return pl.pallas_call(
        functools.partial(place_kernel, n, tuple(steps)),
        out_shape=[shape, shape],
        in_specs=full(1),
        out_specs=full(2),
        compiler_params=params(),
        cost_estimate=cost(count * count, 2 * count * count),
        name="place",
    )(order)


def gathered(onehot, here, blocks):
    rows = blocks[0].shape[0]
    total = None
    for at, block in enumerate(blocks):
        part = dot(onehot[here, at * rows : (at + 1) * rows], block[...])
        total = part if total is None else total + part
    return total


def base_kernel(heads, gain_ref, y_ref, onehot, total_ref, *rest):
    blocks, out_ref = rest[:-1], rest[-1]
    count, width = y_ref.shape
    inverse = 1.0 / jnp.sqrt(total_ref[...] / (width * heads) + EPSILON)
    gain = gain_ref[...]
    tile = min(count, TILE)
    for low in range(0, count, tile):
        part = gathered(onehot, slice(low, low + tile), blocks)
        for at in range(0, tile, LANES):
            here = slice(low + at, low + at + LANES)
            norm = column(inverse[:, here])
            norm = jnp.concatenate([norm] * (width // LANES), axis=1)
            out_ref[here, :] = y_ref[here, :] * norm * gain + part[at : at + LANES]


def base(gain, y, onehot, total, heads, blocks):
    count, width = y.shape
    moved = len(blocks) * blocks[0].shape[0]
    return pl.pallas_call(
        functools.partial(base_kernel, heads),
        out_shape=jax.ShapeDtypeStruct((count, width), F32),
        in_specs=full(4 + len(blocks)),
        out_specs=pl.BlockSpec(memory_space=pltpu.VMEM),
        compiler_params=params(),
        cost_estimate=cost(2 * count * moved * width, 8 * count * width),
        name="base",
    )(gain, y, onehot, total, *blocks)


def mix_kernel(base_ref, onehot, *rest):
    blocks, (out_ref, held, sems) = rest[:-3], rest[-3:]
    count = base_ref.shape[0]
    tile = min(count, TILE)
    copies = []
    for at in range(count // tile):
        here = slice(at * tile, (at + 1) * tile)
        held[here, :] = (base_ref[here, :] + gathered(onehot, here, blocks)).astype(BF16)
        copies += fetch([(held.at[here], out_ref.at[here])], sems.at[at : at + 1])
    for copy in copies:
        copy.wait()


def mix(given, onehot, blocks):
    count, width = given.shape
    moved = len(blocks) * blocks[0].shape[0]
    tile = min(count, TILE)
    return pl.pallas_call(
        mix_kernel,
        out_shape=jax.ShapeDtypeStruct((count, width), BF16),
        in_specs=full(2 + len(blocks)),
        out_specs=pl.BlockSpec(memory_space=pltpu.HBM),
        scratch_shapes=[
            pltpu.VMEM((count, width), BF16),
            pltpu.SemaphoreType.DMA((count // tile,)),
        ],
        compiler_params=params(),
        cost_estimate=cost(2 * count * moved * width, 8 * count * width),
        name="mix",
    )(given, onehot, *blocks)


def sum_over_heads(square, heads):
    if not power_of_two(heads):
        return lax.psum(square, "head")
    step = 1
    while step < heads:
        pairs = [(at, at ^ step) for at in range(heads)]
        square = square + lax.ppermute(square, "head", pairs)
        step *= 2
    return square


def exchange(block, step, n):
    return lax.ppermute(block, "cam", routes(step, n)) if step else block


def give_back(block, step, n):
    pairs = [(target, at) for at, target in routes(step, n)]
    return lax.ppermute(block, "cam", pairs) if step else block


def per_device(queries, keys, values, rates, w_one, w_three, w_two, gain, order):
    count, width = queries.shape
    n = lax.axis_size("cam")
    heads = lax.axis_size("head")
    steps = far_first(n)
    few = max(1, n // 4)
    weights = (w_one, w_three, w_two)
    groups = (tuple(steps[:few]), tuple(steps[few : 2 * few]), tuple(steps[2 * few :]))
    marks = mark(order, n, groups)
    parts = gradients(keys, values, rates.reshape(1, count), *weights, marks[-1], n)
    arrived = {}
    tokens = []
    for group, onehot in zip(groups, marks):
        blocks = sort_tokens(onehot, queries, keys, values, [], n)
        tokens.append(blocks[-1])
        for step, block in zip(group, blocks):
            arrived[step] = exchange(block, step, n)
    mine = core_step(parts, tokens[:1], n)
    summed = sum_over_chips(mine, len(parts) == 2, [tokens[1:2], [arrived[s] for s in steps[:2]] + tokens[2:]], n)
    early = steps[:few] + steps[n - few :]
    late = steps[few : n - few]
    early_places, late_places = place(order, n, early + late)
    y, square = read_out(queries, *weights, summed, [late_places])
    total = sum_over_heads(square, heads)
    attended = attend([arrived[step] for step in range(n)], [total], n, width)
    returned = {step: give_back(attended[step], step, n) for step in early + late}
    given = base(
        gain.reshape(1, width), y, early_places, total, heads, [returned[step] for step in early]
    )
    return mix(given, late_places, [returned[step] for step in late])


def solution(mesh):
    in_specs = (
        P("cam", "head"),
        P("cam", "head"),
        P("cam", "head"),
        P("cam", "head"),
        P("head", None, None),
        P("head", None, None),
        P("head", None, None),
        P("head"),
        P("cam", None),
    )
    out_specs = P("cam", "head")
    return jax.shard_map(
        per_device, mesh=mesh, in_specs=in_specs, out_specs=out_specs, check_vma=False
    )
```

```python
import functools

import jax
import jax.numpy as jnp
from jax import lax
from jax.experimental import pallas as pl
from jax.experimental.pallas import tpu as pltpu
from jax.sharding import PartitionSpec as P

PATCHES = 32
EPSILON = 1e-06
LANES = 128
TILE = 512
LIMIT = 24
COST = 1
FIRST_COST = pl.CostEstimate(flops=10**12, bytes_accessed=1024, transcendentals=0)
MIB = 1024 * 1024
F32 = jnp.float32
BF16 = jnp.bfloat16
TOKEN = jax.ShapeDtypeStruct((8, LANES), F32)


def dot(a, b):
    return lax.dot_general(a, b, (((1,), (0,)), ((), ())), preferred_element_type=F32)


def dot_bt(a, b):
    return lax.dot_general(a, b, (((1,), (1,)), ((), ())), preferred_element_type=F32)


def dot_at(a, b):
    return lax.dot_general(a, b, (((0,), (0,)), ((), ())), preferred_element_type=F32)


def params(limit=LIMIT):
    return pltpu.CompilerParams(vmem_limit_bytes=int(limit * MIB))


def full(count):
    return [pl.BlockSpec(memory_space=pltpu.VMEM)] * count


def cost(flops, moved, exps=0):
    return pl.CostEstimate(
        flops=int(flops) // COST,
        bytes_accessed=int(moved) // COST,
        transcendentals=int(exps) // COST,
    )


def power_of_two(n):
    return n & (n - 1) == 0


def crossed(step):
    return (step & ~6) | ((step & 2) << 1) | ((step & 4) >> 1)


def peer(me, step, n):
    if power_of_two(n):
        if n < 8:
            return me ^ step
        odd = me & 1
        return me ^ (step * (1 - odd) + crossed(step) * odd)
    ahead = me + step
    wrap = ahead - n
    return wrap * (wrap >= 0) + ahead * (wrap < 0)


def routes(step, n):
    return [(at, int(peer(at, step, n))) for at in range(n)]


def column(row):
    return jnp.broadcast_to(row, (LANES, LANES)).T


def far_first(n):
    return sorted(range(n), key=lambda step: (-(step >> 1).bit_count(), -step))


def fetch(pairs, sems):
    copies = []
    for at, (source, target) in enumerate(pairs):
        copies.append(pltpu.make_async_copy(source, target, sems.at[at]))
        copies[-1].start()
    return copies


def mark_kernel(n, steps, order_ref, *rest):
    outs, token = rest[:-1], rest[-1]
    token[...] = jnp.zeros_like(token)
    me = lax.axis_index("cam")
    count = order_ref.shape[1]
    rows = count // n
    order = order_ref[...]
    slot = lax.broadcasted_iota(jnp.int32, (rows, count), 0)
    for group, out in zip(steps, outs):
        for at, step in enumerate(group):
            hit = slot + peer(me, step, n) * rows == order
            out[at * rows : (at + 1) * rows, :] = hit.astype(F32).astype(BF16)


def mark(order, n, steps):
    count = order.shape[1]
    rows = count // n
    return pl.pallas_call(
        functools.partial(mark_kernel, n, steps),
        out_shape=[jax.ShapeDtypeStruct((len(group) * rows, count), BF16) for group in steps]
        + [TOKEN],
        in_specs=full(1),
        out_specs=full(len(steps) + 1),
        compiler_params=params(),
        cost_estimate=FIRST_COST,
        name="mark",
    )(order)


def sort_kernel(size, onehot, q_ref, k_ref, v_ref, *rest):
    outs, token = rest[-1 - size : -1], rest[-1]
    token[...] = jnp.zeros_like(token)
    rows, width = outs[0].shape[0], q_ref.shape[1]
    group = max(1, min(len(outs), TILE // rows))
    while len(outs) % group:
        group -= 1
    for first in range(0, len(outs), group):
        marks = onehot[first * rows : (first + group) * rows, :]
        for which, ref in enumerate((q_ref, k_ref, v_ref)):
            picked = dot(marks, ref[...]).astype(BF16)
            for at in range(group):
                outs[first + at][:, which * width : (which + 1) * width] = picked[
                    at * rows : (at + 1) * rows
                ]


def sort_tokens(onehot, q, k, v, after, n):
    count, width = q.shape
    rows = count // n
    size = onehot.shape[0] // rows
    return pl.pallas_call(
        functools.partial(sort_kernel, size),
        out_shape=[jax.ShapeDtypeStruct((rows, 3 * width), BF16)] * size + [TOKEN],
        in_specs=full(4) + [pl.BlockSpec(memory_space=pl.ANY)] * len(after),
        out_specs=full(size + 1),
        compiler_params=params(),
        cost_estimate=cost(6 * size * rows * count * width, 6 * count * width),
        name="sort_tokens",
    )(onehot, q, k, v, *after)


def attend_kernel(n, scale, *refs):
    ins, outs = refs[:n], refs[-3 - n : -3]
    q_all, k_all, v_all = refs[-3:]
    rows = ins[0].shape[0]
    width = outs[0].shape[1]
    group = n * PATCHES
    block = min(group, 256)
    for stamp in range(rows // PATCHES):
        here = slice(stamp * PATCHES, (stamp + 1) * PATCHES)
        for cam in range(n):
            there = slice(cam * PATCHES, (cam + 1) * PATCHES)
            q_all[there, :] = ins[cam][here, 0:width]
            k_all[there, :] = ins[cam][here, width : 2 * width]
            v_all[there, :] = ins[cam][here, 2 * width : 3 * width]
        for low in range(0, group, block):
            scores = dot_bt(q_all[low : low + block, :], k_all[...]) * scale
            scores = scores - jnp.max(scores, axis=-1, keepdims=True)
            expo = jnp.exp(scores)
            probs = (expo / jnp.sum(expo, axis=-1, keepdims=True)).astype(BF16)
            result = dot(probs, v_all[...]).astype(BF16)
            for cam in range(low // PATCHES, (low + block) // PATCHES):
                at = cam * PATCHES - low
                outs[cam][here, :] = result[at : at + PATCHES]


def attend(blocks, after, n, width):
    rows = blocks[0].shape[0]
    group = n * PATCHES
    return pl.pallas_call(
        functools.partial(attend_kernel, n, width**-0.5),
        out_shape=[jax.ShapeDtypeStruct((rows, width), BF16)] * n,
        in_specs=full(n) + [pl.BlockSpec(memory_space=pl.ANY)] * len(after),
        out_specs=full(n),
        scratch_shapes=[pltpu.VMEM((group, width), BF16)] * 3,
        compiler_params=params(),
        cost_estimate=cost(
            4 * n * rows * group * width, 8 * n * rows * width, n * rows * group
        ),
        name="attend",
    )(*blocks, *after)


def grads_kernel(n, split, k_ref, v_ref, rate_ref, one_ref, three_ref, two_ref, *rest):
    outs, total = rest[1:-1], rest[-1]
    count, width = k_ref.shape
    hid = one_ref.shape[1]
    one, three, two = one_ref[0], three_ref[0], two_ref[0]
    tile = min(count, TILE)
    for start in range(0, count, tile):
        k = k_ref[start : start + tile, :]
        h_one = dot_bt(k, one)
        h_three = dot_bt(k, three)
        sigma = jax.nn.sigmoid(h_one)
        gated = h_one * sigma
        active = (gated * h_three).astype(BF16)
        pieces = []
        for low in range(start, start + tile, LANES):
            rate = column(rate_ref[:, low : low + LANES])
            rate = jnp.concatenate([rate] * (width // LANES), axis=1)
            pieces.append((-rate * v_ref[low : low + LANES, :].astype(F32)).astype(BF16))
        error = jnp.concatenate(pieces, axis=0)
        back = dot(error, two)
        back_one = (back * h_three * sigma * (1.0 + h_one * (1.0 - sigma))).astype(BF16)
        back_three = (back * gated).astype(BF16)
        sums = (dot_at(back_one, k), dot_at(back_three, k), dot_at(error, active))
        for which, term in enumerate(sums):
            here = slice(which * hid, (which + 1) * hid)
            total[here, :] = term if start == 0 else total[here, :] + term
    if split:
        half = total.shape[0] // 2
        core = lax.axis_index("cam") & 1
        outs[0][...] = total[pl.ds(pl.multiple_of(core * half, half), half), :]
        outs[1][...] = total[pl.ds(pl.multiple_of((1 - core) * half, half), half), :]
    else:
        outs[0][...] = total[...]


def gradients(k, v, rate, one, three, two, after, n):
    count, width = k.shape
    hid = one.shape[1]
    split = n > 1 and power_of_two(n)
    assert hid == width
    rows = 3 * hid
    parts = 2 if split else 1
    return pl.pallas_call(
        functools.partial(grads_kernel, n, split),
        out_shape=[jax.ShapeDtypeStruct((rows // parts, width), F32)] * parts,
        in_specs=full(6) + [pl.BlockSpec(memory_space=pl.ANY)],
        out_specs=full(parts),
        scratch_shapes=[pltpu.VMEM((rows, width), F32)],
        compiler_params=params(),
        cost_estimate=cost(12 * count * width * hid, 8 * count * width, count * hid),
        name="gradients",
    )(k, v, rate, one, three, two, after)


def merge_kernel(keep_ref, got_ref, *rest):
    rest[-1][...] = keep_ref[...] + got_ref[...].astype(F32)


def merge(keep, got, after):
    return pl.pallas_call(
        merge_kernel,
        out_shape=jax.ShapeDtypeStruct(keep.shape, F32),
        in_specs=full(2) + [pl.BlockSpec(memory_space=pl.ANY)] * len(after),
        out_specs=pl.BlockSpec(memory_space=pltpu.VMEM),
        compiler_params=params(),
        cost_estimate=cost(keep.size, 12 * keep.size),
        name="merge",
    )(keep, got, *after)


def core_step(parts, after, n):
    if len(parts) == 1:
        return parts[0]
    pair = [(at, at ^ 1) for at in range(n)]
    return merge(parts[0], lax.ppermute(parts[1], "cam", pair), after)


def sum_over_chips(mine, split, after, n):
    if not split:
        return [lax.psum(mine, "cam")]
    span = n.bit_length() - 2
    for step in range(span):
        pairs = []
        for at in range(n):
            bit = 1 + (step + (at & 1)) % span
            pairs.append((at, at ^ (1 << bit)))
        got = lax.ppermute(mine.astype(BF16), "cam", pairs)
        if step < len(after):
            mine = merge(mine, got, after[step])
        else:
            mine = mine + got.astype(F32)
    return [mine, lax.ppermute(mine, "cam", [(at, at ^ 1) for at in range(n)])]


def readout_kernel(parts, q_ref, one_ref, three_ref, two_ref, *rest):
    grads, (y_ref, sq_ref, total, fresh) = rest[:parts], rest[-4:]
    hid, width = one_ref.shape[1:]
    if parts == 2:
        half = total.shape[0] // 2
        core = lax.axis_index("cam") & 1
        total[pl.ds(pl.multiple_of(core * half, half), half), :] = grads[0][...]
        total[pl.ds(pl.multiple_of((1 - core) * half, half), half), :] = grads[1][...]
    else:
        total[...] = grads[0][...]
    entries = hid * width
    for which, ref in enumerate((one_ref, three_ref, two_ref)):
        grad = total[which * hid : (which + 1) * hid, :]
        weight = ref[0].astype(F32)
        row_sq = jnp.sum(weight * weight, axis=1, keepdims=True)
        weight_sq = jnp.sum(row_sq, axis=0, keepdims=True)
        grad_sq = jnp.sum(jnp.sum(grad * grad, axis=1, keepdims=True), axis=0, keepdims=True)
        scale = jnp.sqrt(weight_sq / entries) / jnp.sqrt(grad_sq / entries + EPSILON)
        moved = weight - scale * grad
        ratio = jnp.sqrt(row_sq) / jnp.sqrt(
            jnp.sum(moved * moved, axis=1, keepdims=True) + EPSILON
        )
        fresh[which * hid : (which + 1) * hid, :] = (moved * ratio).astype(BF16)
    count = q_ref.shape[0]
    tile = min(count, TILE)
    ones = jnp.ones((8, width), BF16)
    for start in range(0, count, tile):
        here = slice(start, start + tile)
        q = q_ref[here, :]
        h_one = dot_bt(q, fresh[0:hid, :])
        h_three = dot_bt(q, fresh[hid : 2 * hid, :])
        active = (h_one * jax.nn.sigmoid(h_one) * h_three).astype(BF16)
        y = dot_bt(active, fresh[2 * hid :, :])
        y_ref[here, :] = y
        square = y * y
        high = square.astype(BF16)
        low = (square - high.astype(F32)).astype(BF16)
        sq_ref[:, here] = (dot_bt(ones, high) + dot_bt(ones, low))[0:1, :]


def read_out(q, one, three, two, grads, after):
    count, width = q.shape
    hid = one.shape[1]
    parts = len(grads)
    return pl.pallas_call(
        functools.partial(readout_kernel, parts),
        out_shape=[
            jax.ShapeDtypeStruct((count, width), F32),
            jax.ShapeDtypeStruct((1, count), F32),
        ],
        in_specs=full(4 + parts) + [pl.BlockSpec(memory_space=pl.ANY)] * len(after),
        out_specs=full(2),
        scratch_shapes=[pltpu.VMEM((3 * hid, width), F32), pltpu.VMEM((3 * hid, width), BF16)],
        compiler_params=params(),
        cost_estimate=cost(6 * count * width * hid, 8 * count * width, count * hid),
        name="read_out",
    )(q, one, three, two, *grads, *after)


def place_kernel(n, steps, order_ref, *outs):
    me = lax.axis_index("cam")
    count = order_ref.shape[1]
    rows = count // n
    size = len(steps) * rows
    at = lax.broadcasted_iota(jnp.int32, (8, size), 1)
    slots = at * 0
    for which, step in enumerate(steps):
        inside = jnp.logical_and(at >= which * rows, at < (which + 1) * rows)
        slots = jnp.where(inside, peer(me, step, n) * rows + at - which * rows, slots)
    slots = slots[0:1, :].astype(F32)
    each = outs[0].shape[1]
    for low in range(0, count, LANES):
        wanted = column(order_ref[:, low : low + LANES].astype(F32))
        for lane in range(0, size, LANES):
            hit = wanted == slots[:, lane : lane + LANES]
            out = outs[lane // each]
            start = lane % each
            out[low : low + LANES, start : start + LANES] = hit.astype(F32).astype(BF16)


def place(order, n, steps):
    count = order.shape[1]
    shape = jax.ShapeDtypeStruct((count, count // 2), BF16)
    return pl.pallas_call(
        functools.partial(place_kernel, n, tuple(steps)),
        out_shape=[shape, shape],
        in_specs=full(1),
        out_specs=full(2),
        compiler_params=params(),
        cost_estimate=cost(count * count, 2 * count * count),
        name="place",
    )(order)


def gathered(onehot, here, blocks):
    rows = blocks[0].shape[0]
    total = None
    for at, block in enumerate(blocks):
        part = dot(onehot[here, at * rows : (at + 1) * rows], block[...])
        total = part if total is None else total + part
    return total


def base_kernel(heads, gain_ref, y_ref, onehot, total_ref, *rest):
    blocks, out_ref = rest[:-1], rest[-1]
    count, width = y_ref.shape
    inverse = 1.0 / jnp.sqrt(total_ref[...] / (width * heads) + EPSILON)
    gain = gain_ref[...]
    tile = min(count, TILE)
    for low in range(0, count, tile):
        part = gathered(onehot, slice(low, low + tile), blocks)
        for at in range(0, tile, LANES):
            here = slice(low + at, low + at + LANES)
            norm = column(inverse[:, here])
            norm = jnp.concatenate([norm] * (width // LANES), axis=1)
            out_ref[here, :] = y_ref[here, :] * norm * gain + part[at : at + LANES]


def base(gain, y, onehot, total, heads, blocks):
    count, width = y.shape
    moved = len(blocks) * blocks[0].shape[0]
    return pl.pallas_call(
        functools.partial(base_kernel, heads),
        out_shape=jax.ShapeDtypeStruct((count, width), F32),
        in_specs=full(4 + len(blocks)),
        out_specs=pl.BlockSpec(memory_space=pltpu.VMEM),
        compiler_params=params(),
        cost_estimate=cost(2 * count * moved * width, 8 * count * width),
        name="base",
    )(gain, y, onehot, total, *blocks)


def mix_kernel(base_ref, onehot, *rest):
    blocks, (out_ref, held, sems) = rest[:-3], rest[-3:]
    count = base_ref.shape[0]
    tile = min(count, TILE)
    copies = []
    for at in range(count // tile):
        here = slice(at * tile, (at + 1) * tile)
        held[here, :] = (base_ref[here, :] + gathered(onehot, here, blocks)).astype(BF16)
        copies += fetch([(held.at[here], out_ref.at[here])], sems.at[at : at + 1])
    for copy in copies:
        copy.wait()


def mix(given, onehot, blocks):
    count, width = given.shape
    moved = len(blocks) * blocks[0].shape[0]
    tile = min(count, TILE)
    return pl.pallas_call(
        mix_kernel,
        out_shape=jax.ShapeDtypeStruct((count, width), BF16),
        in_specs=full(2 + len(blocks)),
        out_specs=pl.BlockSpec(memory_space=pltpu.HBM),
        scratch_shapes=[
            pltpu.VMEM((count, width), BF16),
            pltpu.SemaphoreType.DMA((count // tile,)),
        ],
        compiler_params=params(),
        cost_estimate=cost(2 * count * moved * width, 8 * count * width),
        name="mix",
    )(given, onehot, *blocks)


def sum_over_heads(square, heads):
    if not power_of_two(heads):
        return lax.psum(square, "head")
    step = 1
    while step < heads:
        pairs = [(at, at ^ step) for at in range(heads)]
        square = square + lax.ppermute(square, "head", pairs)
        step *= 2
    return square


def exchange(block, step, n):
    return lax.ppermute(block, "cam", routes(step, n)) if step else block


def give_back(block, step, n):
    pairs = [(target, at) for at, target in routes(step, n)]
    return lax.ppermute(block, "cam", pairs) if step else block


def per_device(queries, keys, values, rates, w_one, w_three, w_two, gain, order):
    count, width = queries.shape
    n = lax.axis_size("cam")
    heads = lax.axis_size("head")
    steps = far_first(n)
    few = max(1, n // 4)
    weights = (w_one, w_three, w_two)
    groups = (tuple(steps[:few]), tuple(steps[few : 2 * few]), tuple(steps[2 * few :]))
    marks = mark(order, n, groups)
    arrived = {}
    tokens = []
    for group, onehot in zip(groups, marks):
        blocks = sort_tokens(onehot, queries, keys, values, [], n)
        tokens.append(blocks[-1])
        for step, block in zip(group, blocks):
            arrived[step] = exchange(block, step, n)
    came = [arrived[step] for step in steps]
    parts = gradients(keys, values, rates.reshape(1, count), *weights, marks[-1], n)
    mine = core_step(parts, tokens[:1], n)
    summed = sum_over_chips(mine, len(parts) == 2, [tokens[1:2], came[:2] + tokens[2:]], n)
    early = steps[:few] + steps[n - few :]
    late = steps[few : n - few]
    early_places, late_places = place(order, n, early + late)
    y, square = read_out(queries, *weights, summed, [late_places] + came[2:4])
    total = sum_over_heads(square, heads)
    attended = attend([arrived[step] for step in range(n)], [total], n, width)
    returned = {step: give_back(attended[step], step, n) for step in early + late}
    given = base(
        gain.reshape(1, width), y, early_places, total, heads, [returned[step] for step in early]
    )
    return mix(given, late_places, [returned[step] for step in late])


def solution(mesh):
    in_specs = (
        P("cam", "head"),
        P("cam", "head"),
        P("cam", "head"),
        P("cam", "head"),
        P("head", None, None),
        P("head", None, None),
        P("head", None, None),
        P("head"),
        P("cam", None),
    )
    out_specs = P("cam", "head")
    return jax.shard_map(
        per_device, mesh=mesh, in_specs=in_specs, out_specs=out_specs, check_vma=False
    )
```

```python
import functools

import jax
import jax.numpy as jnp
from jax import lax
from jax.experimental import pallas as pl
from jax.experimental.pallas import tpu as pltpu
from jax.sharding import PartitionSpec as P

PATCHES = 32
EPSILON = 1e-06
LANES = 128
TILE = 512
LIMIT = 24
COST = 1
FIRST_COST = pl.CostEstimate(flops=10**12, bytes_accessed=1024, transcendentals=0)
MIB = 1024 * 1024
F32 = jnp.float32
BF16 = jnp.bfloat16
TOKEN = jax.ShapeDtypeStruct((8, LANES), F32)


def dot(a, b):
    return lax.dot_general(a, b, (((1,), (0,)), ((), ())), preferred_element_type=F32)


def dot_bt(a, b):
    return lax.dot_general(a, b, (((1,), (1,)), ((), ())), preferred_element_type=F32)


def dot_at(a, b):
    return lax.dot_general(a, b, (((0,), (0,)), ((), ())), preferred_element_type=F32)


def params(limit=LIMIT):
    return pltpu.CompilerParams(vmem_limit_bytes=int(limit * MIB))


def full(count):
    return [pl.BlockSpec(memory_space=pltpu.VMEM)] * count


def cost(flops, moved, exps=0):
    return pl.CostEstimate(
        flops=int(flops) // COST,
        bytes_accessed=int(moved) // COST,
        transcendentals=int(exps) // COST,
    )


def power_of_two(n):
    return n & (n - 1) == 0


def crossed(step):
    return (step & ~6) | ((step & 2) << 1) | ((step & 4) >> 1)


def peer(me, step, n):
    if power_of_two(n):
        if n < 8:
            return me ^ step
        odd = me & 1
        return me ^ (step * (1 - odd) + crossed(step) * odd)
    ahead = me + step
    wrap = ahead - n
    return wrap * (wrap >= 0) + ahead * (wrap < 0)


def routes(step, n):
    return [(at, int(peer(at, step, n))) for at in range(n)]


def column(row):
    return jnp.broadcast_to(row, (LANES, LANES)).T


def far_first(n):
    return sorted(range(n), key=lambda step: (-(step >> 1).bit_count(), -step))


def fetch(pairs, sems):
    copies = []
    for at, (source, target) in enumerate(pairs):
        copies.append(pltpu.make_async_copy(source, target, sems.at[at]))
        copies[-1].start()
    return copies


def mark_kernel(n, steps, order_ref, *rest):
    outs, token = rest[:-1], rest[-1]
    token[...] = jnp.zeros_like(token)
    me = lax.axis_index("cam")
    count = order_ref.shape[1]
    rows = count // n
    order = order_ref[...]
    slot = lax.broadcasted_iota(jnp.int32, (rows, count), 0)
    for group, out in zip(steps, outs):
        for at, step in enumerate(group):
            hit = slot + peer(me, step, n) * rows == order
            out[at * rows : (at + 1) * rows, :] = hit.astype(F32).astype(BF16)


def mark(order, n, steps):
    count = order.shape[1]
    rows = count // n
    return pl.pallas_call(
        functools.partial(mark_kernel, n, steps),
        out_shape=[jax.ShapeDtypeStruct((len(group) * rows, count), BF16) for group in steps]
        + [TOKEN],
        in_specs=full(1),
        out_specs=full(len(steps) + 1),
        compiler_params=params(),
        cost_estimate=FIRST_COST,
        name="mark",
    )(order)


def sort_kernel(size, onehot, q_ref, k_ref, v_ref, *rest):
    outs, token = rest[-1 - size : -1], rest[-1]
    token[...] = jnp.zeros_like(token)
    rows, width = outs[0].shape[0], q_ref.shape[1]
    group = max(1, min(len(outs), TILE // rows))
    while len(outs) % group:
        group -= 1
    for first in range(0, len(outs), group):
        marks = onehot[first * rows : (first + group) * rows, :]
        for which, ref in enumerate((q_ref, k_ref, v_ref)):
            picked = dot(marks, ref[...]).astype(BF16)
            for at in range(group):
                outs[first + at][:, which * width : (which + 1) * width] = picked[
                    at * rows : (at + 1) * rows
                ]


def sort_tokens(onehot, q, k, v, after, n):
    count, width = q.shape
    rows = count // n
    size = onehot.shape[0] // rows
    return pl.pallas_call(
        functools.partial(sort_kernel, size),
        out_shape=[jax.ShapeDtypeStruct((rows, 3 * width), BF16)] * size + [TOKEN],
        in_specs=full(4) + [pl.BlockSpec(memory_space=pl.ANY)] * len(after),
        out_specs=full(size + 1),
        compiler_params=params(),
        cost_estimate=cost(6 * size * rows * count * width, 6 * count * width),
        name="sort_tokens",
    )(onehot, q, k, v, *after)


def attend_kernel(n, scale, *refs):
    ins, outs = refs[:n], refs[-3 - n : -3]
    q_all, k_all, v_all = refs[-3:]
    rows = ins[0].shape[0]
    width = outs[0].shape[1]
    group = n * PATCHES
    block = min(group, 256)
    for stamp in range(rows // PATCHES):
        here = slice(stamp * PATCHES, (stamp + 1) * PATCHES)
        for cam in range(n):
            there = slice(cam * PATCHES, (cam + 1) * PATCHES)
            q_all[there, :] = ins[cam][here, 0:width]
            k_all[there, :] = ins[cam][here, width : 2 * width]
            v_all[there, :] = ins[cam][here, 2 * width : 3 * width]
        for low in range(0, group, block):
            scores = dot_bt(q_all[low : low + block, :], k_all[...]) * scale
            scores = scores - jnp.max(scores, axis=-1, keepdims=True)
            expo = jnp.exp(scores)
            probs = (expo / jnp.sum(expo, axis=-1, keepdims=True)).astype(BF16)
            result = dot(probs, v_all[...]).astype(BF16)
            for cam in range(low // PATCHES, (low + block) // PATCHES):
                at = cam * PATCHES - low
                outs[cam][here, :] = result[at : at + PATCHES]


def attend(blocks, after, n, width):
    rows = blocks[0].shape[0]
    group = n * PATCHES
    return pl.pallas_call(
        functools.partial(attend_kernel, n, width**-0.5),
        out_shape=[jax.ShapeDtypeStruct((rows, width), BF16)] * n,
        in_specs=full(n) + [pl.BlockSpec(memory_space=pl.ANY)] * len(after),
        out_specs=full(n),
        scratch_shapes=[pltpu.VMEM((group, width), BF16)] * 3,
        compiler_params=params(),
        cost_estimate=cost(
            4 * n * rows * group * width, 8 * n * rows * width, n * rows * group
        ),
        name="attend",
    )(*blocks, *after)


def grads_kernel(n, split, k_ref, v_ref, rate_ref, one_ref, three_ref, two_ref, *rest):
    outs, total = rest[1:-1], rest[-1]
    count, width = k_ref.shape
    hid = one_ref.shape[1]
    one, three, two = one_ref[0], three_ref[0], two_ref[0]
    tile = min(count, TILE)
    for start in range(0, count, tile):
        k = k_ref[start : start + tile, :]
        h_one = dot_bt(k, one)
        h_three = dot_bt(k, three)
        sigma = jax.nn.sigmoid(h_one)
        gated = h_one * sigma
        active = (gated * h_three).astype(BF16)
        pieces = []
        for low in range(start, start + tile, LANES):
            rate = column(rate_ref[:, low : low + LANES])
            rate = jnp.concatenate([rate] * (width // LANES), axis=1)
            pieces.append((-rate * v_ref[low : low + LANES, :].astype(F32)).astype(BF16))
        error = jnp.concatenate(pieces, axis=0)
        back = dot(error, two)
        back_one = (back * h_three * sigma * (1.0 + h_one * (1.0 - sigma))).astype(BF16)
        back_three = (back * gated).astype(BF16)
        sums = (dot_at(back_one, k), dot_at(back_three, k), dot_at(error, active))
        for which, term in enumerate(sums):
            here = slice(which * hid, (which + 1) * hid)
            total[here, :] = term if start == 0 else total[here, :] + term
    if split:
        half = total.shape[0] // 2
        core = lax.axis_index("cam") & 1
        outs[0][...] = total[pl.ds(pl.multiple_of(core * half, half), half), :]
        outs[1][...] = total[pl.ds(pl.multiple_of((1 - core) * half, half), half), :]
    else:
        outs[0][...] = total[...]


def gradients(k, v, rate, one, three, two, after, n):
    count, width = k.shape
    hid = one.shape[1]
    split = n > 1 and power_of_two(n)
    assert hid == width
    rows = 3 * hid
    parts = 2 if split else 1
    return pl.pallas_call(
        functools.partial(grads_kernel, n, split),
        out_shape=[jax.ShapeDtypeStruct((rows // parts, width), F32)] * parts,
        in_specs=full(6) + [pl.BlockSpec(memory_space=pl.ANY)],
        out_specs=full(parts),
        scratch_shapes=[pltpu.VMEM((rows, width), F32)],
        compiler_params=params(),
        cost_estimate=cost(12 * count * width * hid, 8 * count * width, count * hid),
        name="gradients",
    )(k, v, rate, one, three, two, after)


def merge_kernel(keep_ref, got_ref, *rest):
    rest[-1][...] = keep_ref[...] + got_ref[...].astype(F32)


def merge(keep, got, after):
    return pl.pallas_call(
        merge_kernel,
        out_shape=jax.ShapeDtypeStruct(keep.shape, F32),
        in_specs=full(2) + [pl.BlockSpec(memory_space=pl.ANY)] * len(after),
        out_specs=pl.BlockSpec(memory_space=pltpu.VMEM),
        compiler_params=params(),
        cost_estimate=cost(keep.size, 12 * keep.size),
        name="merge",
    )(keep, got, *after)


def core_step(parts, after, n):
    if len(parts) == 1:
        return parts[0]
    pair = [(at, at ^ 1) for at in range(n)]
    return merge(parts[0], lax.ppermute(parts[1], "cam", pair), after)


def sum_over_chips(mine, split, after, n):
    if not split:
        return [lax.psum(mine, "cam")]
    span = n.bit_length() - 2
    for step in range(span):
        pairs = []
        for at in range(n):
            bit = 1 + (step + (at & 1)) % span
            pairs.append((at, at ^ (1 << bit)))
        got = lax.ppermute(mine.astype(BF16), "cam", pairs)
        if step < len(after):
            mine = merge(mine, got, after[step])
        else:
            mine = mine + got.astype(F32)
    return [mine, lax.ppermute(mine, "cam", [(at, at ^ 1) for at in range(n)])]


def readout_kernel(parts, q_ref, one_ref, three_ref, two_ref, *rest):
    grads, (y_ref, sq_ref, total, fresh) = rest[:parts], rest[-4:]
    hid, width = one_ref.shape[1:]
    if parts == 2:
        half = total.shape[0] // 2
        core = lax.axis_index("cam") & 1
        total[pl.ds(pl.multiple_of(core * half, half), half), :] = grads[0][...]
        total[pl.ds(pl.multiple_of((1 - core) * half, half), half), :] = grads[1][...]
    else:
        total[...] = grads[0][...]
    entries = hid * width
    for which, ref in enumerate((one_ref, three_ref, two_ref)):
        grad = total[which * hid : (which + 1) * hid, :]
        weight = ref[0].astype(F32)
        row_sq = jnp.sum(weight * weight, axis=1, keepdims=True)
        weight_sq = jnp.sum(row_sq, axis=0, keepdims=True)
        grad_sq = jnp.sum(jnp.sum(grad * grad, axis=1, keepdims=True), axis=0, keepdims=True)
        scale = jnp.sqrt(weight_sq / entries) / jnp.sqrt(grad_sq / entries + EPSILON)
        moved = weight - scale * grad
        ratio = jnp.sqrt(row_sq) / jnp.sqrt(
            jnp.sum(moved * moved, axis=1, keepdims=True) + EPSILON
        )
        fresh[which * hid : (which + 1) * hid, :] = (moved * ratio).astype(BF16)
    count = q_ref.shape[0]
    tile = min(count, TILE)
    ones = jnp.ones((8, width), BF16)
    for start in range(0, count, tile):
        here = slice(start, start + tile)
        q = q_ref[here, :]
        h_one = dot_bt(q, fresh[0:hid, :])
        h_three = dot_bt(q, fresh[hid : 2 * hid, :])
        active = (h_one * jax.nn.sigmoid(h_one) * h_three).astype(BF16)
        y = dot_bt(active, fresh[2 * hid :, :])
        y_ref[here, :] = y
        square = y * y
        high = square.astype(BF16)
        low = (square - high.astype(F32)).astype(BF16)
        sq_ref[:, here] = (dot_bt(ones, high) + dot_bt(ones, low))[0:1, :]


def read_out(q, one, three, two, grads, after):
    count, width = q.shape
    hid = one.shape[1]
    parts = len(grads)
    return pl.pallas_call(
        functools.partial(readout_kernel, parts),
        out_shape=[
            jax.ShapeDtypeStruct((count, width), F32),
            jax.ShapeDtypeStruct((1, count), F32),
        ],
        in_specs=full(4 + parts) + [pl.BlockSpec(memory_space=pl.ANY)] * len(after),
        out_specs=full(2),
        scratch_shapes=[pltpu.VMEM((3 * hid, width), F32), pltpu.VMEM((3 * hid, width), BF16)],
        compiler_params=params(),
        cost_estimate=cost(6 * count * width * hid, 8 * count * width, count * hid),
        name="read_out",
    )(q, one, three, two, *grads, *after)


def place_kernel(n, steps, order_ref, *outs):
    me = lax.axis_index("cam")
    count = order_ref.shape[1]
    rows = count // n
    size = len(steps) * rows
    at = lax.broadcasted_iota(jnp.int32, (8, size), 1)
    slots = at * 0
    for which, step in enumerate(steps):
        inside = jnp.logical_and(at >= which * rows, at < (which + 1) * rows)
        slots = jnp.where(inside, peer(me, step, n) * rows + at - which * rows, slots)
    slots = slots[0:1, :].astype(F32)
    each = outs[0].shape[1]
    for low in range(0, count, LANES):
        wanted = column(order_ref[:, low : low + LANES].astype(F32))
        for lane in range(0, size, LANES):
            hit = wanted == slots[:, lane : lane + LANES]
            out = outs[lane // each]
            start = lane % each
            out[low : low + LANES, start : start + LANES] = hit.astype(F32).astype(BF16)


def place(order, n, steps):
    count = order.shape[1]
    shape = jax.ShapeDtypeStruct((count, count // 2), BF16)
    return pl.pallas_call(
        functools.partial(place_kernel, n, tuple(steps)),
        out_shape=[shape, shape],
        in_specs=full(1),
        out_specs=full(2),
        compiler_params=params(),
        cost_estimate=cost(count * count, 2 * count * count),
        name="place",
    )(order)


def gathered(onehot, here, blocks):
    rows = blocks[0].shape[0]
    total = None
    for at, block in enumerate(blocks):
        part = dot(onehot[here, at * rows : (at + 1) * rows], block[...])
        total = part if total is None else total + part
    return total


def base_kernel(heads, gain_ref, y_ref, onehot, total_ref, *rest):
    blocks, out_ref = rest[:-1], rest[-1]
    count, width = y_ref.shape
    inverse = 1.0 / jnp.sqrt(total_ref[...] / (width * heads) + EPSILON)
    gain = gain_ref[...]
    tile = min(count, TILE)
    for low in range(0, count, tile):
        part = gathered(onehot, slice(low, low + tile), blocks)
        for at in range(0, tile, LANES):
            here = slice(low + at, low + at + LANES)
            norm = column(inverse[:, here])
            norm = jnp.concatenate([norm] * (width // LANES), axis=1)
            out_ref[here, :] = y_ref[here, :] * norm * gain + part[at : at + LANES]


def base(gain, y, onehot, total, heads, blocks):
    count, width = y.shape
    moved = len(blocks) * blocks[0].shape[0]
    return pl.pallas_call(
        functools.partial(base_kernel, heads),
        out_shape=jax.ShapeDtypeStruct((count, width), F32),
        in_specs=full(4 + len(blocks)),
        out_specs=pl.BlockSpec(memory_space=pltpu.VMEM),
        compiler_params=params(),
        cost_estimate=cost(2 * count * moved * width, 8 * count * width),
        name="base",
    )(gain, y, onehot, total, *blocks)


def mix_kernel(base_ref, onehot, *rest):
    blocks, (out_ref, held, sems) = rest[:-3], rest[-3:]
    count = base_ref.shape[0]
    tile = min(count, TILE)
    copies = []
    for at in range(count // tile):
        here = slice(at * tile, (at + 1) * tile)
        held[here, :] = (base_ref[here, :] + gathered(onehot, here, blocks)).astype(BF16)
        copies += fetch([(held.at[here], out_ref.at[here])], sems.at[at : at + 1])
    for copy in copies:
        copy.wait()


def mix(given, onehot, blocks):
    count, width = given.shape
    moved = len(blocks) * blocks[0].shape[0]
    tile = min(count, TILE)
    return pl.pallas_call(
        mix_kernel,
        out_shape=jax.ShapeDtypeStruct((count, width), BF16),
        in_specs=full(2 + len(blocks)),
        out_specs=pl.BlockSpec(memory_space=pltpu.HBM),
        scratch_shapes=[
            pltpu.VMEM((count, width), BF16),
            pltpu.SemaphoreType.DMA((count // tile,)),
        ],
        compiler_params=params(),
        cost_estimate=cost(2 * count * moved * width, 8 * count * width),
        name="mix",
    )(given, onehot, *blocks)


def sum_over_heads(square, heads):
    if not power_of_two(heads):
        return lax.psum(square, "head")
    step = 1
    while step < heads:
        pairs = [(at, at ^ step) for at in range(heads)]
        square = square + lax.ppermute(square, "head", pairs)
        step *= 2
    return square


def exchange(block, step, n):
    return lax.ppermute(block, "cam", routes(step, n)) if step else block


def give_back(block, step, n):
    pairs = [(target, at) for at, target in routes(step, n)]
    return lax.ppermute(block, "cam", pairs) if step else block


def per_device(queries, keys, values, rates, w_one, w_three, w_two, gain, order):
    count, width = queries.shape
    n = lax.axis_size("cam")
    heads = lax.axis_size("head")
    steps = far_first(n)
    few = max(1, n // 4)
    weights = (w_one, w_three, w_two)
    groups = (tuple(steps[:few]), tuple(steps[few : 2 * few]), tuple(steps[2 * few :]))
    marks = mark(order, n, groups)
    arrived = {}
    tokens = []
    for group, onehot in zip(groups, marks):
        blocks = sort_tokens(onehot, queries, keys, values, [], n)
        tokens.append(blocks[-1])
        for step, block in zip(group, blocks):
            arrived[step] = exchange(block, step, n)
    came = [arrived[step] for step in steps]
    parts = gradients(keys, values, rates.reshape(1, count), *weights, marks[-1], n)
    mine = core_step(parts, tokens[:1], n)
    summed = sum_over_chips(mine, len(parts) == 2, [[], came[:2] + tokens[1:2]], n)
    early = steps[:few] + steps[n - few :]
    late = steps[few : n - few]
    early_places, late_places = place(order, n, early + late)
    y, square = read_out(queries, *weights, summed, [late_places] + came[2:4] + tokens[2:])
    total = sum_over_heads(square, heads)
    attended = attend([arrived[step] for step in range(n)], [total], n, width)
    returned = {step: give_back(attended[step], step, n) for step in early + late}
    given = base(
        gain.reshape(1, width), y, early_places, total, heads, [returned[step] for step in early]
    )
    return mix(given, late_places, [returned[step] for step in late])


def solution(mesh):
    in_specs = (
        P("cam", "head"),
        P("cam", "head"),
        P("cam", "head"),
        P("cam", "head"),
        P("head", None, None),
        P("head", None, None),
        P("head", None, None),
        P("head"),
        P("cam", None),
    )
    out_specs = P("cam", "head")
    return jax.shard_map(
        per_device, mesh=mesh, in_specs=in_specs, out_specs=out_specs, check_vma=False
    )
```

```python
import functools

import jax
import jax.numpy as jnp
from jax import lax
from jax.experimental import pallas as pl
from jax.experimental.pallas import tpu as pltpu
from jax.sharding import PartitionSpec as P

PATCHES = 32
EPSILON = 1e-06
LANES = 128
TILE = 512
LIMIT = 24
COST = 1
FIRST_COST = pl.CostEstimate(flops=10**12, bytes_accessed=1024, transcendentals=0)
MIB = 1024 * 1024
F32 = jnp.float32
BF16 = jnp.bfloat16
TOKEN = jax.ShapeDtypeStruct((8, LANES), F32)


def dot(a, b):
    return lax.dot_general(a, b, (((1,), (0,)), ((), ())), preferred_element_type=F32)


def dot_bt(a, b):
    return lax.dot_general(a, b, (((1,), (1,)), ((), ())), preferred_element_type=F32)


def dot_at(a, b):
    return lax.dot_general(a, b, (((0,), (0,)), ((), ())), preferred_element_type=F32)


def params(limit=LIMIT):
    return pltpu.CompilerParams(vmem_limit_bytes=int(limit * MIB))


def full(count):
    return [pl.BlockSpec(memory_space=pltpu.VMEM)] * count


def cost(flops, moved, exps=0):
    return pl.CostEstimate(
        flops=int(flops) // COST,
        bytes_accessed=int(moved) // COST,
        transcendentals=int(exps) // COST,
    )


def power_of_two(n):
    return n & (n - 1) == 0


def crossed(step):
    return (step & ~6) | ((step & 2) << 1) | ((step & 4) >> 1)


def peer(me, step, n):
    if power_of_two(n):
        if n < 8:
            return me ^ step
        odd = me & 1
        return me ^ (step * (1 - odd) + crossed(step) * odd)
    ahead = me + step
    wrap = ahead - n
    return wrap * (wrap >= 0) + ahead * (wrap < 0)


def routes(step, n):
    return [(at, int(peer(at, step, n))) for at in range(n)]


def column(row):
    return jnp.broadcast_to(row, (LANES, LANES)).T


def far_first(n):
    return sorted(range(n), key=lambda step: (-(step >> 1).bit_count(), -step))


def fetch(pairs, sems):
    copies = []
    for at, (source, target) in enumerate(pairs):
        copies.append(pltpu.make_async_copy(source, target, sems.at[at]))
        copies[-1].start()
    return copies


def mark_kernel(n, steps, order_ref, *rest):
    outs, token = rest[:-1], rest[-1]
    token[...] = jnp.zeros_like(token)
    me = lax.axis_index("cam")
    count = order_ref.shape[1]
    rows = count // n
    order = order_ref[...]
    slot = lax.broadcasted_iota(jnp.int32, (rows, count), 0)
    for group, out in zip(steps, outs):
        for at, step in enumerate(group):
            hit = slot + peer(me, step, n) * rows == order
            out[at * rows : (at + 1) * rows, :] = hit.astype(F32).astype(BF16)


def mark(order, n, steps):
    count = order.shape[1]
    rows = count // n
    return pl.pallas_call(
        functools.partial(mark_kernel, n, steps),
        out_shape=[jax.ShapeDtypeStruct((len(group) * rows, count), BF16) for group in steps]
        + [TOKEN],
        in_specs=full(1),
        out_specs=full(len(steps) + 1),
        compiler_params=params(),
        cost_estimate=FIRST_COST,
        name="mark",
    )(order)


def sort_kernel(size, onehot, q_ref, k_ref, v_ref, *rest):
    outs, token = rest[-1 - size : -1], rest[-1]
    token[...] = jnp.zeros_like(token)
    rows, width = outs[0].shape[0], q_ref.shape[1]
    group = max(1, min(len(outs), TILE // rows))
    while len(outs) % group:
        group -= 1
    for first in range(0, len(outs), group):
        marks = onehot[first * rows : (first + group) * rows, :]
        for which, ref in enumerate((q_ref, k_ref, v_ref)):
            picked = dot(marks, ref[...]).astype(BF16)
            for at in range(group):
                outs[first + at][:, which * width : (which + 1) * width] = picked[
                    at * rows : (at + 1) * rows
                ]


def sort_tokens(onehot, q, k, v, after, n):
    count, width = q.shape
    rows = count // n
    size = onehot.shape[0] // rows
    return pl.pallas_call(
        functools.partial(sort_kernel, size),
        out_shape=[jax.ShapeDtypeStruct((rows, 3 * width), BF16)] * size + [TOKEN],
        in_specs=full(4) + [pl.BlockSpec(memory_space=pl.ANY)] * len(after),
        out_specs=full(size + 1),
        compiler_params=params(),
        cost_estimate=cost(6 * size * rows * count * width, 6 * count * width),
        name="sort_tokens",
    )(onehot, q, k, v, *after)


def attend_kernel(n, scale, *refs):
    ins, outs = refs[:n], refs[-3 - n : -3]
    q_all, k_all, v_all = refs[-3:]
    rows = ins[0].shape[0]
    width = outs[0].shape[1]
    group = n * PATCHES
    block = min(group, 256)
    for stamp in range(rows // PATCHES):
        here = slice(stamp * PATCHES, (stamp + 1) * PATCHES)
        for cam in range(n):
            there = slice(cam * PATCHES, (cam + 1) * PATCHES)
            q_all[there, :] = ins[cam][here, 0:width]
            k_all[there, :] = ins[cam][here, width : 2 * width]
            v_all[there, :] = ins[cam][here, 2 * width : 3 * width]
        for low in range(0, group, block):
            scores = dot_bt(q_all[low : low + block, :], k_all[...]) * scale
            scores = scores - jnp.max(scores, axis=-1, keepdims=True)
            expo = jnp.exp(scores)
            probs = (expo / jnp.sum(expo, axis=-1, keepdims=True)).astype(BF16)
            result = dot(probs, v_all[...]).astype(BF16)
            for cam in range(low // PATCHES, (low + block) // PATCHES):
                at = cam * PATCHES - low
                outs[cam][here, :] = result[at : at + PATCHES]


def attend(blocks, after, n, width):
    rows = blocks[0].shape[0]
    group = n * PATCHES
    return pl.pallas_call(
        functools.partial(attend_kernel, n, width**-0.5),
        out_shape=[jax.ShapeDtypeStruct((rows, width), BF16)] * n,
        in_specs=full(n) + [pl.BlockSpec(memory_space=pl.ANY)] * len(after),
        out_specs=full(n),
        scratch_shapes=[pltpu.VMEM((group, width), BF16)] * 3,
        compiler_params=params(),
        cost_estimate=cost(
            4 * n * rows * group * width, 8 * n * rows * width, n * rows * group
        ),
        name="attend",
    )(*blocks, *after)


def grads_kernel(n, split, k_ref, v_ref, rate_ref, one_ref, three_ref, two_ref, *rest):
    outs, total = rest[1:-1], rest[-1]
    count, width = k_ref.shape
    hid = one_ref.shape[1]
    one, three, two = one_ref[0], three_ref[0], two_ref[0]
    tile = min(count, TILE)
    for start in range(0, count, tile):
        k = k_ref[start : start + tile, :]
        h_one = dot_bt(k, one)
        h_three = dot_bt(k, three)
        sigma = jax.nn.sigmoid(h_one)
        gated = h_one * sigma
        active = (gated * h_three).astype(BF16)
        pieces = []
        for low in range(start, start + tile, LANES):
            rate = column(rate_ref[:, low : low + LANES])
            rate = jnp.concatenate([rate] * (width // LANES), axis=1)
            pieces.append((-rate * v_ref[low : low + LANES, :].astype(F32)).astype(BF16))
        error = jnp.concatenate(pieces, axis=0)
        back = dot(error, two)
        back_one = (back * h_three * sigma * (1.0 + h_one * (1.0 - sigma))).astype(BF16)
        back_three = (back * gated).astype(BF16)
        sums = (dot_at(back_one, k), dot_at(back_three, k), dot_at(error, active))
        for which, term in enumerate(sums):
            here = slice(which * hid, (which + 1) * hid)
            total[here, :] = term if start == 0 else total[here, :] + term
    if split:
        half = total.shape[0] // 2
        core = lax.axis_index("cam") & 1
        outs[0][...] = total[pl.ds(pl.multiple_of(core * half, half), half), :]
        other = total[pl.ds(pl.multiple_of((1 - core) * half, half), half), :]
        outs[1][...] = other.astype(BF16)
    else:
        outs[0][...] = total[...]


def gradients(k, v, rate, one, three, two, after, n):
    count, width = k.shape
    hid = one.shape[1]
    split = n > 1 and power_of_two(n)
    assert hid == width
    rows = 3 * hid
    parts = 2 if split else 1
    return pl.pallas_call(
        functools.partial(grads_kernel, n, split),
        out_shape=[
            jax.ShapeDtypeStruct((rows // parts, width), kind) for kind in (F32, BF16)[:parts]
        ],
        in_specs=full(6) + [pl.BlockSpec(memory_space=pl.ANY)],
        out_specs=full(parts),
        scratch_shapes=[pltpu.VMEM((rows, width), F32)],
        compiler_params=params(),
        cost_estimate=cost(12 * count * width * hid, 8 * count * width, count * hid),
        name="gradients",
    )(k, v, rate, one, three, two, after)


def merge_kernel(keep_ref, got_ref, *rest):
    rest[-1][...] = keep_ref[...] + got_ref[...].astype(F32)


def merge(keep, got, after):
    return pl.pallas_call(
        merge_kernel,
        out_shape=jax.ShapeDtypeStruct(keep.shape, F32),
        in_specs=full(2) + [pl.BlockSpec(memory_space=pl.ANY)] * len(after),
        out_specs=pl.BlockSpec(memory_space=pltpu.VMEM),
        compiler_params=params(),
        cost_estimate=cost(keep.size, 12 * keep.size),
        name="merge",
    )(keep, got, *after)


def core_step(parts, after, n):
    if len(parts) == 1:
        return parts[0]
    pair = [(at, at ^ 1) for at in range(n)]
    return merge(parts[0], lax.ppermute(parts[1], "cam", pair), after)


def sum_over_chips(mine, split, after, n):
    if not split:
        return [lax.psum(mine, "cam")]
    span = n.bit_length() - 2
    for step in range(span):
        pairs = []
        for at in range(n):
            bit = 1 + (step + (at & 1)) % span
            pairs.append((at, at ^ (1 << bit)))
        got = lax.ppermute(mine.astype(BF16), "cam", pairs)
        if step < len(after):
            mine = merge(mine, got, after[step])
        else:
            mine = mine + got.astype(F32)
    return [mine, lax.ppermute(mine, "cam", [(at, at ^ 1) for at in range(n)])]


def readout_kernel(parts, q_ref, one_ref, three_ref, two_ref, *rest):
    grads, (y_ref, sq_ref, total, fresh) = rest[:parts], rest[-4:]
    hid, width = one_ref.shape[1:]
    if parts == 2:
        half = total.shape[0] // 2
        core = lax.axis_index("cam") & 1
        total[pl.ds(pl.multiple_of(core * half, half), half), :] = grads[0][...]
        total[pl.ds(pl.multiple_of((1 - core) * half, half), half), :] = grads[1][...]
    else:
        total[...] = grads[0][...]
    entries = hid * width
    for which, ref in enumerate((one_ref, three_ref, two_ref)):
        grad = total[which * hid : (which + 1) * hid, :]
        weight = ref[0].astype(F32)
        row_sq = jnp.sum(weight * weight, axis=1, keepdims=True)
        weight_sq = jnp.sum(row_sq, axis=0, keepdims=True)
        grad_sq = jnp.sum(jnp.sum(grad * grad, axis=1, keepdims=True), axis=0, keepdims=True)
        scale = jnp.sqrt(weight_sq / entries) / jnp.sqrt(grad_sq / entries + EPSILON)
        moved = weight - scale * grad
        ratio = jnp.sqrt(row_sq) / jnp.sqrt(
            jnp.sum(moved * moved, axis=1, keepdims=True) + EPSILON
        )
        fresh[which * hid : (which + 1) * hid, :] = (moved * ratio).astype(BF16)
    count = q_ref.shape[0]
    tile = min(count, TILE)
    ones = jnp.ones((8, width), BF16)
    for start in range(0, count, tile):
        here = slice(start, start + tile)
        q = q_ref[here, :]
        h_one = dot_bt(q, fresh[0:hid, :])
        h_three = dot_bt(q, fresh[hid : 2 * hid, :])
        active = (h_one * jax.nn.sigmoid(h_one) * h_three).astype(BF16)
        y = dot_bt(active, fresh[2 * hid :, :])
        y_ref[here, :] = y
        square = y * y
        high = square.astype(BF16)
        low = (square - high.astype(F32)).astype(BF16)
        sq_ref[:, here] = (dot_bt(ones, high) + dot_bt(ones, low))[0:1, :]


def read_out(q, one, three, two, grads, after):
    count, width = q.shape
    hid = one.shape[1]
    parts = len(grads)
    return pl.pallas_call(
        functools.partial(readout_kernel, parts),
        out_shape=[
            jax.ShapeDtypeStruct((count, width), F32),
            jax.ShapeDtypeStruct((1, count), F32),
        ],
        in_specs=full(4 + parts) + [pl.BlockSpec(memory_space=pl.ANY)] * len(after),
        out_specs=full(2),
        scratch_shapes=[pltpu.VMEM((3 * hid, width), F32), pltpu.VMEM((3 * hid, width), BF16)],
        compiler_params=params(),
        cost_estimate=cost(6 * count * width * hid, 8 * count * width, count * hid),
        name="read_out",
    )(q, one, three, two, *grads, *after)


def place_kernel(n, steps, order_ref, *outs):
    me = lax.axis_index("cam")
    count = order_ref.shape[1]
    rows = count // n
    size = len(steps) * rows
    at = lax.broadcasted_iota(jnp.int32, (8, size), 1)
    slots = at * 0
    for which, step in enumerate(steps):
        inside = jnp.logical_and(at >= which * rows, at < (which + 1) * rows)
        slots = jnp.where(inside, peer(me, step, n) * rows + at - which * rows, slots)
    slots = slots[0:1, :].astype(F32)
    each = outs[0].shape[1]
    for low in range(0, count, LANES):
        wanted = column(order_ref[:, low : low + LANES].astype(F32))
        for lane in range(0, size, LANES):
            hit = wanted == slots[:, lane : lane + LANES]
            out = outs[lane // each]
            start = lane % each
            out[low : low + LANES, start : start + LANES] = hit.astype(F32).astype(BF16)


def place(order, n, steps):
    count = order.shape[1]
    shape = jax.ShapeDtypeStruct((count, count // 2), BF16)
    return pl.pallas_call(
        functools.partial(place_kernel, n, tuple(steps)),
        out_shape=[shape, shape],
        in_specs=full(1),
        out_specs=full(2),
        compiler_params=params(),
        cost_estimate=cost(count * count, 2 * count * count),
        name="place",
    )(order)


def gathered(onehot, here, blocks):
    rows = blocks[0].shape[0]
    total = None
    for at, block in enumerate(blocks):
        part = dot(onehot[here, at * rows : (at + 1) * rows], block[...])
        total = part if total is None else total + part
    return total


def base_kernel(heads, gain_ref, y_ref, onehot, total_ref, *rest):
    blocks, out_ref = rest[:-1], rest[-1]
    count, width = y_ref.shape
    inverse = 1.0 / jnp.sqrt(total_ref[...] / (width * heads) + EPSILON)
    gain = gain_ref[...]
    tile = min(count, TILE)
    for low in range(0, count, tile):
        part = gathered(onehot, slice(low, low + tile), blocks)
        for at in range(0, tile, LANES):
            here = slice(low + at, low + at + LANES)
            norm = column(inverse[:, here])
            norm = jnp.concatenate([norm] * (width // LANES), axis=1)
            out_ref[here, :] = y_ref[here, :] * norm * gain + part[at : at + LANES]


def base(gain, y, onehot, total, heads, blocks):
    count, width = y.shape
    moved = len(blocks) * blocks[0].shape[0]
    return pl.pallas_call(
        functools.partial(base_kernel, heads),
        out_shape=jax.ShapeDtypeStruct((count, width), F32),
        in_specs=full(4 + len(blocks)),
        out_specs=pl.BlockSpec(memory_space=pltpu.VMEM),
        compiler_params=params(),
        cost_estimate=cost(2 * count * moved * width, 8 * count * width),
        name="base",
    )(gain, y, onehot, total, *blocks)


def mix_kernel(base_ref, onehot, *rest):
    blocks, (out_ref, held, sems) = rest[:-3], rest[-3:]
    count = base_ref.shape[0]
    tile = min(count, TILE)
    copies = []
    for at in range(count // tile):
        here = slice(at * tile, (at + 1) * tile)
        held[here, :] = (base_ref[here, :] + gathered(onehot, here, blocks)).astype(BF16)
        copies += fetch([(held.at[here], out_ref.at[here])], sems.at[at : at + 1])
    for copy in copies:
        copy.wait()


def mix(given, onehot, blocks):
    count, width = given.shape
    moved = len(blocks) * blocks[0].shape[0]
    tile = min(count, TILE)
    return pl.pallas_call(
        mix_kernel,
        out_shape=jax.ShapeDtypeStruct((count, width), BF16),
        in_specs=full(2 + len(blocks)),
        out_specs=pl.BlockSpec(memory_space=pltpu.HBM),
        scratch_shapes=[
            pltpu.VMEM((count, width), BF16),
            pltpu.SemaphoreType.DMA((count // tile,)),
        ],
        compiler_params=params(),
        cost_estimate=cost(2 * count * moved * width, 8 * count * width),
        name="mix",
    )(given, onehot, *blocks)


def sum_over_heads(square, heads):
    if not power_of_two(heads):
        return lax.psum(square, "head")
    step = 1
    while step < heads:
        pairs = [(at, at ^ step) for at in range(heads)]
        square = square + lax.ppermute(square, "head", pairs)
        step *= 2
    return square


def exchange(block, step, n):
    return lax.ppermute(block, "cam", routes(step, n)) if step else block


def give_back(block, step, n):
    pairs = [(target, at) for at, target in routes(step, n)]
    return lax.ppermute(block, "cam", pairs) if step else block


def per_device(queries, keys, values, rates, w_one, w_three, w_two, gain, order):
    count, width = queries.shape
    n = lax.axis_size("cam")
    heads = lax.axis_size("head")
    steps = far_first(n)
    few = max(1, n // 4)
    weights = (w_one, w_three, w_two)
    groups = (tuple(steps[:few]), tuple(steps[few : 2 * few]), tuple(steps[2 * few :]))
    marks = mark(order, n, groups)
    arrived = {}
    tokens = []
    for group, onehot in zip(groups, marks):
        blocks = sort_tokens(onehot, queries, keys, values, [], n)
        tokens.append(blocks[-1])
        for step, block in zip(group, blocks):
            arrived[step] = exchange(block, step, n)
    came = [arrived[step] for step in steps]
    parts = gradients(keys, values, rates.reshape(1, count), *weights, tokens[0], n)
    early = steps[:few] + steps[n - few :]
    late = steps[few : n - few]
    early_places, late_places = place(order, n, early + late)
    mine = core_step(parts, [came[0]], n)
    summed = sum_over_chips(mine, len(parts) == 2, [tokens[1:2], came[1:3] + tokens[2:] + [late_places]], n)
    y, square = read_out(queries, *weights, summed, came[3:4])
    total = sum_over_heads(square, heads)
    attended = attend([arrived[step] for step in range(n)], [total], n, width)
    returned = {step: give_back(attended[step], step, n) for step in early + late}
    given = base(
        gain.reshape(1, width), y, early_places, total, heads, [returned[step] for step in early]
    )
    return mix(given, late_places, [returned[step] for step in late])


def solution(mesh):
    in_specs = (
        P("cam", "head"),
        P("cam", "head"),
        P("cam", "head"),
        P("cam", "head"),
        P("head", None, None),
        P("head", None, None),
        P("head", None, None),
        P("head"),
        P("cam", None),
    )
    out_specs = P("cam", "head")
    return jax.shard_map(
        per_device, mesh=mesh, in_specs=in_specs, out_specs=out_specs, check_vma=False
    )
```

```python
import functools

import jax
import jax.numpy as jnp
from jax import lax
from jax.experimental import pallas as pl
from jax.experimental.pallas import tpu as pltpu
from jax.sharding import PartitionSpec as P

PATCHES = 32
EPSILON = 1e-06
LANES = 128
TILE = 512
LIMIT = 24
COST = 1
FIRST_COST = pl.CostEstimate(flops=10**12, bytes_accessed=1024, transcendentals=0)
MIB = 1024 * 1024
F32 = jnp.float32
BF16 = jnp.bfloat16
TOKEN = jax.ShapeDtypeStruct((8, LANES), F32)


def dot(a, b):
    return lax.dot_general(a, b, (((1,), (0,)), ((), ())), preferred_element_type=F32)


def dot_bt(a, b):
    return lax.dot_general(a, b, (((1,), (1,)), ((), ())), preferred_element_type=F32)


def dot_at(a, b):
    return lax.dot_general(a, b, (((0,), (0,)), ((), ())), preferred_element_type=F32)


def params(limit=LIMIT):
    return pltpu.CompilerParams(vmem_limit_bytes=int(limit * MIB))


def full(count):
    return [pl.BlockSpec(memory_space=pltpu.VMEM)] * count


def cost(flops, moved, exps=0):
    return pl.CostEstimate(
        flops=int(flops) // COST,
        bytes_accessed=int(moved) // COST,
        transcendentals=int(exps) // COST,
    )


def power_of_two(n):
    return n & (n - 1) == 0


def crossed(step):
    return (step & ~6) | ((step & 2) << 1) | ((step & 4) >> 1)


def peer(me, step, n):
    if power_of_two(n):
        if n < 8:
            return me ^ step
        odd = me & 1
        return me ^ (step * (1 - odd) + crossed(step) * odd)
    ahead = me + step
    wrap = ahead - n
    return wrap * (wrap >= 0) + ahead * (wrap < 0)


def routes(step, n):
    return [(at, int(peer(at, step, n))) for at in range(n)]


def column(row):
    return jnp.broadcast_to(row, (LANES, LANES)).T


def far_first(n):
    return sorted(range(n), key=lambda step: (-(step >> 1).bit_count(), -step))


def fetch(pairs, sems):
    copies = []
    for at, (source, target) in enumerate(pairs):
        copies.append(pltpu.make_async_copy(source, target, sems.at[at]))
        copies[-1].start()
    return copies


def mark_kernel(n, steps, order_ref, *rest):
    outs, token = rest[:-1], rest[-1]
    token[...] = jnp.zeros_like(token)
    me = lax.axis_index("cam")
    count = order_ref.shape[1]
    rows = count // n
    order = order_ref[...]
    slot = lax.broadcasted_iota(jnp.int32, (rows, count), 0)
    for group, out in zip(steps, outs):
        for at, step in enumerate(group):
            hit = slot + peer(me, step, n) * rows == order
            out[at * rows : (at + 1) * rows, :] = hit.astype(F32).astype(BF16)


def mark(order, n, steps):
    count = order.shape[1]
    rows = count // n
    return pl.pallas_call(
        functools.partial(mark_kernel, n, steps),
        out_shape=[jax.ShapeDtypeStruct((len(group) * rows, count), BF16) for group in steps]
        + [TOKEN],
        in_specs=full(1),
        out_specs=full(len(steps) + 1),
        compiler_params=params(),
        cost_estimate=FIRST_COST,
        name="mark",
    )(order)


def sort_kernel(size, cut, onehot, q_ref, k_ref, v_ref, *rest):
    width = q_ref.shape[1]
    outs, token = rest[-1 - size - cut : -1], rest[-1]
    places = [[(out, at * width) for at in range(3)] for out in outs[cut:]]
    if cut:
        places[0] = [(outs[0], 0), (outs[0], width), (outs[1], 0)]
    token[...] = jnp.zeros_like(token)
    rows = outs[0].shape[0]
    group = max(1, min(size, TILE // rows))
    while size % group:
        group -= 1
    for first in range(0, size, group):
        marks = onehot[first * rows : (first + group) * rows, :]
        for which, ref in enumerate((q_ref, k_ref, v_ref)):
            picked = dot(marks, ref[...]).astype(BF16)
            for at in range(group):
                out, low = places[first + at][which]
                out[:, low : low + width] = picked[at * rows : (at + 1) * rows]


def sort_tokens(onehot, q, k, v, cut, n):
    count, width = q.shape
    rows = count // n
    size = onehot.shape[0] // rows
    widths = [2 * width, width] * cut + [3 * width] * (size - cut)
    return pl.pallas_call(
        functools.partial(sort_kernel, size, cut),
        out_shape=[jax.ShapeDtypeStruct((rows, each), BF16) for each in widths] + [TOKEN],
        in_specs=full(4),
        out_specs=full(len(widths) + 1),
        compiler_params=params(),
        cost_estimate=cost(6 * size * rows * count * width, 6 * count * width),
        name="sort_tokens",
    )(onehot, q, k, v)


def attend_kernel(n, scale, cut, *refs):
    ins, outs = list(refs[:n]), refs[-3 - n : -3]
    q_all, k_all, v_all = refs[-3:]
    rows = ins[0].shape[0]
    width = outs[0].shape[1]
    group = n * PATCHES
    block = min(group, 256)
    for stamp in range(rows // PATCHES):
        here = slice(stamp * PATCHES, (stamp + 1) * PATCHES)
        for cam in range(n):
            there = slice(cam * PATCHES, (cam + 1) * PATCHES)
            q_all[there, :] = ins[cam][here, 0:width]
            k_all[there, :] = ins[cam][here, width : 2 * width]
            if cam == cut:
                v_all[there, :] = refs[n][here, :]
            else:
                v_all[there, :] = ins[cam][here, 2 * width : 3 * width]
        for low in range(0, group, block):
            scores = dot_bt(q_all[low : low + block, :], k_all[...]) * scale
            scores = scores - jnp.max(scores, axis=-1, keepdims=True)
            expo = jnp.exp(scores)
            probs = (expo / jnp.sum(expo, axis=-1, keepdims=True)).astype(BF16)
            result = dot(probs, v_all[...]).astype(BF16)
            for cam in range(low // PATCHES, (low + block) // PATCHES):
                at = cam * PATCHES - low
                outs[cam][here, :] = result[at : at + PATCHES]


def attend(blocks, cut, rest, after, n, width):
    rows = blocks[0].shape[0]
    group = n * PATCHES
    return pl.pallas_call(
        functools.partial(attend_kernel, n, width**-0.5, cut),
        out_shape=[jax.ShapeDtypeStruct((rows, width), BF16)] * n,
        in_specs=full(n + 1) + [pl.BlockSpec(memory_space=pl.ANY)] * len(after),
        out_specs=full(n),
        scratch_shapes=[pltpu.VMEM((group, width), BF16)] * 3,
        compiler_params=params(),
        cost_estimate=cost(
            4 * n * rows * group * width, 8 * n * rows * width, n * rows * group
        ),
        name="attend",
    )(*blocks, rest, *after)


def grads_kernel(n, split, k_ref, v_ref, rate_ref, one_ref, three_ref, two_ref, *rest):
    outs, total = rest[1:-1], rest[-1]
    count, width = k_ref.shape
    hid = one_ref.shape[1]
    one, three, two = one_ref[0], three_ref[0], two_ref[0]
    tile = min(count, TILE)
    for start in range(0, count, tile):
        k = k_ref[start : start + tile, :]
        h_one = dot_bt(k, one)
        h_three = dot_bt(k, three)
        sigma = jax.nn.sigmoid(h_one)
        gated = h_one * sigma
        active = (gated * h_three).astype(BF16)
        pieces = []
        for low in range(start, start + tile, LANES):
            rate = column(rate_ref[:, low : low + LANES])
            rate = jnp.concatenate([rate] * (width // LANES), axis=1)
            pieces.append((-rate * v_ref[low : low + LANES, :].astype(F32)).astype(BF16))
        error = jnp.concatenate(pieces, axis=0)
        back = dot(error, two)
        back_one = (back * h_three * sigma * (1.0 + h_one * (1.0 - sigma))).astype(BF16)
        back_three = (back * gated).astype(BF16)
        sums = (dot_at(back_one, k), dot_at(back_three, k), dot_at(error, active))
        for which, term in enumerate(sums):
            here = slice(which * hid, (which + 1) * hid)
            total[here, :] = term if start == 0 else total[here, :] + term
    if split:
        half = total.shape[0] // 2
        core = lax.axis_index("cam") & 1
        outs[0][...] = total[pl.ds(pl.multiple_of(core * half, half), half), :]
        other = total[pl.ds(pl.multiple_of((1 - core) * half, half), half), :]
        outs[1][...] = other.astype(BF16)
    else:
        outs[0][...] = total[...]


def gradients(k, v, rate, one, three, two, after, n):
    count, width = k.shape
    hid = one.shape[1]
    split = n > 1 and power_of_two(n)
    assert hid == width
    rows = 3 * hid
    parts = 2 if split else 1
    return pl.pallas_call(
        functools.partial(grads_kernel, n, split),
        out_shape=[
            jax.ShapeDtypeStruct((rows // parts, width), kind) for kind in (F32, BF16)[:parts]
        ],
        in_specs=full(6) + [pl.BlockSpec(memory_space=pl.ANY)],
        out_specs=full(parts),
        scratch_shapes=[pltpu.VMEM((rows, width), F32)],
        compiler_params=params(),
        cost_estimate=cost(12 * count * width * hid, 8 * count * width, count * hid),
        name="gradients",
    )(k, v, rate, one, three, two, after)


def merge_kernel(keep_ref, got_ref, *rest):
    rest[-1][...] = keep_ref[...] + got_ref[...].astype(F32)


def merge(keep, got, after):
    return pl.pallas_call(
        merge_kernel,
        out_shape=jax.ShapeDtypeStruct(keep.shape, F32),
        in_specs=full(2) + [pl.BlockSpec(memory_space=pl.ANY)] * len(after),
        out_specs=pl.BlockSpec(memory_space=pltpu.VMEM),
        compiler_params=params(),
        cost_estimate=cost(keep.size, 12 * keep.size),
        name="merge",
    )(keep, got, *after)


def core_step(parts, after, n):
    if len(parts) == 1:
        return parts[0]
    pair = [(at, at ^ 1) for at in range(n)]
    return merge(parts[0], lax.ppermute(parts[1], "cam", pair), after)


def sum_over_chips(mine, split, after, n):
    if not split:
        return [lax.psum(mine, "cam")]
    span = n.bit_length() - 2
    for step in range(span):
        pairs = []
        for at in range(n):
            bit = 1 + (step + (at & 1)) % span
            pairs.append((at, at ^ (1 << bit)))
        got = lax.ppermute(mine.astype(BF16), "cam", pairs)
        if step < len(after):
            mine = merge(mine, got, after[step])
        else:
            mine = mine + got.astype(F32)
    return [mine, lax.ppermute(mine.astype(BF16), "cam", [(at, at ^ 1) for at in range(n)])]


def readout_kernel(parts, q_ref, one_ref, three_ref, two_ref, *rest):
    grads, (y_ref, sq_ref, total, fresh) = rest[:parts], rest[-4:]
    hid, width = one_ref.shape[1:]
    if parts == 2:
        half = total.shape[0] // 2
        core = lax.axis_index("cam") & 1
        total[pl.ds(pl.multiple_of(core * half, half), half), :] = grads[0][...]
        total[pl.ds(pl.multiple_of((1 - core) * half, half), half), :] = grads[1][...].astype(F32)
    else:
        total[...] = grads[0][...]
    entries = hid * width
    for which, ref in enumerate((one_ref, three_ref, two_ref)):
        grad = total[which * hid : (which + 1) * hid, :]
        weight = ref[0].astype(F32)
        row_sq = jnp.sum(weight * weight, axis=1, keepdims=True)
        weight_sq = jnp.sum(row_sq, axis=0, keepdims=True)
        grad_sq = jnp.sum(jnp.sum(grad * grad, axis=1, keepdims=True), axis=0, keepdims=True)
        scale = jnp.sqrt(weight_sq / entries) / jnp.sqrt(grad_sq / entries + EPSILON)
        moved = weight - scale * grad
        ratio = jnp.sqrt(row_sq) / jnp.sqrt(
            jnp.sum(moved * moved, axis=1, keepdims=True) + EPSILON
        )
        fresh[which * hid : (which + 1) * hid, :] = (moved * ratio).astype(BF16)
    count = q_ref.shape[0]
    tile = min(count, TILE)
    ones = jnp.ones((8, width), BF16)
    for start in range(0, count, tile):
        here = slice(start, start + tile)
        q = q_ref[here, :]
        h_one = dot_bt(q, fresh[0:hid, :])
        h_three = dot_bt(q, fresh[hid : 2 * hid, :])
        active = (h_one * jax.nn.sigmoid(h_one) * h_three).astype(BF16)
        y = dot_bt(active, fresh[2 * hid :, :])
        y_ref[here, :] = y
        square = y * y
        high = square.astype(BF16)
        low = (square - high.astype(F32)).astype(BF16)
        sq_ref[:, here] = (dot_bt(ones, high) + dot_bt(ones, low))[0:1, :]


def read_out(q, one, three, two, grads, after):
    count, width = q.shape
    hid = one.shape[1]
    parts = len(grads)
    return pl.pallas_call(
        functools.partial(readout_kernel, parts),
        out_shape=[
            jax.ShapeDtypeStruct((count, width), F32),
            jax.ShapeDtypeStruct((1, count), F32),
        ],
        in_specs=full(4 + parts) + [pl.BlockSpec(memory_space=pl.ANY)] * len(after),
        out_specs=full(2),
        scratch_shapes=[pltpu.VMEM((3 * hid, width), F32), pltpu.VMEM((3 * hid, width), BF16)],
        compiler_params=params(),
        cost_estimate=cost(6 * count * width * hid, 8 * count * width, count * hid),
        name="read_out",
    )(q, one, three, two, *grads, *after)


def place_kernel(n, steps, order_ref, *outs):
    me = lax.axis_index("cam")
    count = order_ref.shape[1]
    rows = count // n
    size = len(steps) * rows
    at = lax.broadcasted_iota(jnp.int32, (8, size), 1)
    slots = at * 0
    for which, step in enumerate(steps):
        inside = jnp.logical_and(at >= which * rows, at < (which + 1) * rows)
        slots = jnp.where(inside, peer(me, step, n) * rows + at - which * rows, slots)
    slots = slots[0:1, :].astype(F32)
    each = outs[0].shape[1]
    for low in range(0, count, LANES):
        wanted = column(order_ref[:, low : low + LANES].astype(F32))
        for lane in range(0, size, LANES):
            hit = wanted == slots[:, lane : lane + LANES]
            out = outs[lane // each]
            start = lane % each
            out[low : low + LANES, start : start + LANES] = hit.astype(F32).astype(BF16)


def place(order, n, steps):
    count = order.shape[1]
    shape = jax.ShapeDtypeStruct((count, count // 2), BF16)
    return pl.pallas_call(
        functools.partial(place_kernel, n, tuple(steps)),
        out_shape=[shape, shape],
        in_specs=full(1),
        out_specs=full(2),
        compiler_params=params(),
        cost_estimate=cost(count * count, 2 * count * count),
        name="place",
    )(order)


def gathered(onehot, here, blocks):
    rows = blocks[0].shape[0]
    total = None
    for at, block in enumerate(blocks):
        part = dot(onehot[here, at * rows : (at + 1) * rows], block[...])
        total = part if total is None else total + part
    return total


def base_kernel(heads, gain_ref, y_ref, onehot, total_ref, *rest):
    blocks, out_ref = rest[:-1], rest[-1]
    count, width = y_ref.shape
    inverse = 1.0 / jnp.sqrt(total_ref[...] / (width * heads) + EPSILON)
    gain = gain_ref[...]
    tile = min(count, TILE)
    for low in range(0, count, tile):
        part = gathered(onehot, slice(low, low + tile), blocks)
        for at in range(0, tile, LANES):
            here = slice(low + at, low + at + LANES)
            norm = column(inverse[:, here])
            norm = jnp.concatenate([norm] * (width // LANES), axis=1)
            out_ref[here, :] = y_ref[here, :] * norm * gain + part[at : at + LANES]


def base(gain, y, onehot, total, heads, blocks):
    count, width = y.shape
    moved = len(blocks) * blocks[0].shape[0]
    return pl.pallas_call(
        functools.partial(base_kernel, heads),
        out_shape=jax.ShapeDtypeStruct((count, width), F32),
        in_specs=full(4 + len(blocks)),
        out_specs=pl.BlockSpec(memory_space=pltpu.VMEM),
        compiler_params=params(),
        cost_estimate=cost(2 * count * moved * width, 8 * count * width),
        name="base",
    )(gain, y, onehot, total, *blocks)


def mix_kernel(base_ref, onehot, *rest):
    blocks, (out_ref, held, sems) = rest[:-3], rest[-3:]
    count = base_ref.shape[0]
    tile = min(count, TILE)
    copies = []
    for at in range(count // tile):
        here = slice(at * tile, (at + 1) * tile)
        held[here, :] = (base_ref[here, :] + gathered(onehot, here, blocks)).astype(BF16)
        copies += fetch([(held.at[here], out_ref.at[here])], sems.at[at : at + 1])
    for copy in copies:
        copy.wait()


def mix(given, onehot, blocks):
    count, width = given.shape
    moved = len(blocks) * blocks[0].shape[0]
    tile = min(count, TILE)
    return pl.pallas_call(
        mix_kernel,
        out_shape=jax.ShapeDtypeStruct((count, width), BF16),
        in_specs=full(2 + len(blocks)),
        out_specs=pl.BlockSpec(memory_space=pltpu.HBM),
        scratch_shapes=[
            pltpu.VMEM((count, width), BF16),
            pltpu.SemaphoreType.DMA((count // tile,)),
        ],
        compiler_params=params(),
        cost_estimate=cost(2 * count * moved * width, 8 * count * width),
        name="mix",
    )(given, onehot, *blocks)


def sum_over_heads(square, heads, direct):
    if not power_of_two(heads) or direct:
        return square + sum(
            lax.ppermute(square, "head", [(at, (at + step) % heads) for at in range(heads)])
            for step in range(1, heads)
        )
    step = 1
    while step < heads:
        pairs = [(at, at ^ step) for at in range(heads)]
        square = square + lax.ppermute(square, "head", pairs)
        step *= 2
    return square


def exchange(block, step, n):
    return lax.ppermute(block, "cam", routes(step, n)) if step else block


def give_back(block, step, n):
    pairs = [(target, at) for at, target in routes(step, n)]
    return lax.ppermute(block, "cam", pairs) if step else block


def per_device(queries, keys, values, rates, w_one, w_three, w_two, gain, order):
    count, width = queries.shape
    n = lax.axis_size("cam")
    heads = lax.axis_size("head")
    steps = far_first(n)
    few = max(1, n // 4)
    weights = (w_one, w_three, w_two)
    groups = (tuple(steps[:few]), (*steps[few : 2 * few], 1), (*steps[2 * few : -2], 0))
    marks = mark(order, n, groups)
    arrived = {}
    tokens = []
    for which, (group, onehot) in enumerate(zip(groups, marks)):
        cut = 1 if which == 0 else 0
        blocks = list(sort_tokens(onehot, queries, keys, values, cut, n))
        tokens.append(blocks.pop())
        if cut:
            rest = exchange(blocks.pop(1), group[0], n)
        for step, block in zip(group, blocks):
            arrived[step] = exchange(block, step, n)
    came = [arrived[step] for step in steps]
    parts = gradients(keys, values, rates.reshape(1, count), *weights, tokens[0], n)
    early = steps[:few] + steps[n - few :]
    late = steps[few : n - few]
    early_places, late_places = place(order, n, early + late)
    mine = core_step(parts, [came[0]], n)
    summed = sum_over_chips(mine, len(parts) == 2, [tokens[1:2], [rest] + came[1:3] + tokens[2:] + [late_places]], n)
    y, square = read_out(queries, *weights, summed, came[3:4])
    total = sum_over_heads(square, heads, False)
    blocks = [arrived[step] for step in range(n)]
    attended = attend(blocks, steps[0], rest, [total], n, width)
    returned = {step: give_back(attended[step], step, n) for step in early + late}
    given = base(
        gain.reshape(1, width), y, early_places, total, heads, [returned[step] for step in early]
    )
    return mix(given, late_places, [returned[step] for step in late])


def solution(mesh):
    in_specs = (
        P("cam", "head"),
        P("cam", "head"),
        P("cam", "head"),
        P("cam", "head"),
        P("head", None, None),
        P("head", None, None),
        P("head", None, None),
        P("head"),
        P("cam", None),
    )
    out_specs = P("cam", "head")
    return jax.shard_map(
        per_device, mesh=mesh, in_specs=in_specs, out_specs=out_specs, check_vma=False
    )
```

```python
import functools

import jax
import jax.numpy as jnp
from jax import lax
from jax.experimental import pallas as pl
from jax.experimental.pallas import tpu as pltpu
from jax.sharding import PartitionSpec as P

PATCHES = 32
EPSILON = 1e-06
LANES = 128
TILE = 512
LIMIT = 24
COST = 1
FIRST_COST = pl.CostEstimate(flops=10**12, bytes_accessed=1024, transcendentals=0)
MIB = 1024 * 1024
F32 = jnp.float32
BF16 = jnp.bfloat16
TOKEN = jax.ShapeDtypeStruct((8, LANES), F32)


def dot(a, b):
    return lax.dot_general(a, b, (((1,), (0,)), ((), ())), preferred_element_type=F32)


def dot_bt(a, b):
    return lax.dot_general(a, b, (((1,), (1,)), ((), ())), preferred_element_type=F32)


def dot_at(a, b):
    return lax.dot_general(a, b, (((0,), (0,)), ((), ())), preferred_element_type=F32)


def params(limit=LIMIT):
    return pltpu.CompilerParams(vmem_limit_bytes=int(limit * MIB))


def full(count):
    return [pl.BlockSpec(memory_space=pltpu.VMEM)] * count


def cost(flops, moved, exps=0):
    return pl.CostEstimate(
        flops=int(flops) // COST,
        bytes_accessed=int(moved) // COST,
        transcendentals=int(exps) // COST,
    )


def power_of_two(n):
    return n & (n - 1) == 0


def crossed(step):
    return (step & ~6) | ((step & 2) << 1) | ((step & 4) >> 1)


def peer(me, step, n):
    if power_of_two(n):
        if n < 8:
            return me ^ step
        odd = me & 1
        return me ^ (step * (1 - odd) + crossed(step) * odd)
    ahead = me + step
    wrap = ahead - n
    return wrap * (wrap >= 0) + ahead * (wrap < 0)


def routes(step, n):
    return [(at, int(peer(at, step, n))) for at in range(n)]


def column(row):
    return jnp.broadcast_to(row, (LANES, LANES)).T


def far_first(n):
    return sorted(range(n), key=lambda step: (-(step >> 1).bit_count(), -step))


def fetch(pairs, sems):
    copies = []
    for at, (source, target) in enumerate(pairs):
        copies.append(pltpu.make_async_copy(source, target, sems.at[at]))
        copies[-1].start()
    return copies


def mark_kernel(n, steps, order_ref, *rest):
    outs, token = rest[:-1], rest[-1]
    token[...] = jnp.zeros_like(token)
    me = lax.axis_index("cam")
    count = order_ref.shape[1]
    rows = count // n
    order = order_ref[...]
    slot = lax.broadcasted_iota(jnp.int32, (rows, count), 0)
    for group, out in zip(steps, outs):
        for at, step in enumerate(group):
            hit = slot + peer(me, step, n) * rows == order
            out[at * rows : (at + 1) * rows, :] = hit.astype(F32).astype(BF16)


def mark(order, n, steps):
    count = order.shape[1]
    rows = count // n
    return pl.pallas_call(
        functools.partial(mark_kernel, n, steps),
        out_shape=[jax.ShapeDtypeStruct((len(group) * rows, count), BF16) for group in steps]
        + [TOKEN],
        in_specs=full(1),
        out_specs=full(len(steps) + 1),
        compiler_params=params(),
        cost_estimate=FIRST_COST,
        name="mark",
    )(order)


def sort_kernel(size, onehot, q_ref, k_ref, v_ref, *rest):
    outs, token = rest[-1 - size : -1], rest[-1]
    token[...] = jnp.zeros_like(token)
    rows, width = outs[0].shape[0], q_ref.shape[1]
    group = max(1, min(len(outs), TILE // rows))
    while len(outs) % group:
        group -= 1
    for first in range(0, len(outs), group):
        marks = onehot[first * rows : (first + group) * rows, :]
        for which, ref in enumerate((q_ref, k_ref, v_ref)):
            picked = dot(marks, ref[...]).astype(BF16)
            for at in range(group):
                outs[first + at][:, which * width : (which + 1) * width] = picked[
                    at * rows : (at + 1) * rows
                ]


def sort_tokens(onehot, q, k, v, after, n):
    count, width = q.shape
    rows = count // n
    size = onehot.shape[0] // rows
    return pl.pallas_call(
        functools.partial(sort_kernel, size),
        out_shape=[jax.ShapeDtypeStruct((rows, 3 * width), BF16)] * size + [TOKEN],
        in_specs=full(4) + [pl.BlockSpec(memory_space=pl.ANY)] * len(after),
        out_specs=full(size + 1),
        compiler_params=params(),
        cost_estimate=cost(6 * size * rows * count * width, 6 * count * width),
        name="sort_tokens",
    )(onehot, q, k, v, *after)


def attend_kernel(n, scale, *refs):
    ins, outs = refs[:n], refs[-3 - n : -3]
    q_all, k_all, v_all = refs[-3:]
    rows = ins[0].shape[0]
    width = outs[0].shape[1]
    group = n * PATCHES
    block = min(group, 256)
    for stamp in range(rows // PATCHES):
        here = slice(stamp * PATCHES, (stamp + 1) * PATCHES)
        for cam in range(n):
            there = slice(cam * PATCHES, (cam + 1) * PATCHES)
            q_all[there, :] = ins[cam][here, 0:width]
            k_all[there, :] = ins[cam][here, width : 2 * width]
            v_all[there, :] = ins[cam][here, 2 * width : 3 * width]
        for low in range(0, group, block):
            scores = dot_bt(q_all[low : low + block, :], k_all[...]) * scale
            scores = scores - jnp.max(scores, axis=-1, keepdims=True)
            expo = jnp.exp(scores)
            probs = (expo / jnp.sum(expo, axis=-1, keepdims=True)).astype(BF16)
            result = dot(probs, v_all[...]).astype(BF16)
            for cam in range(low // PATCHES, (low + block) // PATCHES):
                at = cam * PATCHES - low
                outs[cam][here, :] = result[at : at + PATCHES]


def attend(blocks, after, n, width):
    rows = blocks[0].shape[0]
    group = n * PATCHES
    return pl.pallas_call(
        functools.partial(attend_kernel, n, width**-0.5),
        out_shape=[jax.ShapeDtypeStruct((rows, width), BF16)] * n,
        in_specs=full(n) + [pl.BlockSpec(memory_space=pl.ANY)] * len(after),
        out_specs=full(n),
        scratch_shapes=[pltpu.VMEM((group, width), BF16)] * 3,
        compiler_params=params(),
        cost_estimate=cost(
            4 * n * rows * group * width, 8 * n * rows * width, n * rows * group
        ),
        name="attend",
    )(*blocks, *after)


def grads_kernel(n, split, k_ref, v_ref, rate_ref, one_ref, three_ref, two_ref, *rest):
    outs, total = rest[1:-1], rest[-1]
    count, width = k_ref.shape
    hid = one_ref.shape[1]
    one, three, two = one_ref[0], three_ref[0], two_ref[0]
    tile = min(count, TILE)
    for start in range(0, count, tile):
        k = k_ref[start : start + tile, :]
        h_one = dot_bt(k, one)
        h_three = dot_bt(k, three)
        sigma = jax.nn.sigmoid(h_one)
        gated = h_one * sigma
        active = (gated * h_three).astype(BF16)
        pieces = []
        for low in range(start, start + tile, LANES):
            rate = column(rate_ref[:, low : low + LANES])
            rate = jnp.concatenate([rate] * (width // LANES), axis=1)
            pieces.append((-rate * v_ref[low : low + LANES, :].astype(F32)).astype(BF16))
        error = jnp.concatenate(pieces, axis=0)
        back = dot(error, two)
        back_one = (back * h_three * sigma * (1.0 + h_one * (1.0 - sigma))).astype(BF16)
        back_three = (back * gated).astype(BF16)
        sums = (dot_at(back_one, k), dot_at(back_three, k), dot_at(error, active))
        for which, term in enumerate(sums):
            here = slice(which * hid, (which + 1) * hid)
            total[here, :] = term if start == 0 else total[here, :] + term
    if split:
        half = total.shape[0] // 2
        core = lax.axis_index("cam") & 1
        outs[0][...] = total[pl.ds(pl.multiple_of(core * half, half), half), :]
        other = total[pl.ds(pl.multiple_of((1 - core) * half, half), half), :]
        outs[1][...] = other.astype(BF16)
    else:
        outs[0][...] = total[...]


def gradients(k, v, rate, one, three, two, after, n):
    count, width = k.shape
    hid = one.shape[1]
    split = n > 1 and power_of_two(n)
    assert hid == width
    rows = 3 * hid
    parts = 2 if split else 1
    return pl.pallas_call(
        functools.partial(grads_kernel, n, split),
        out_shape=[
            jax.ShapeDtypeStruct((rows // parts, width), kind) for kind in (F32, BF16)[:parts]
        ],
        in_specs=full(6) + [pl.BlockSpec(memory_space=pl.ANY)],
        out_specs=full(parts),
        scratch_shapes=[pltpu.VMEM((rows, width), F32)],
        compiler_params=params(),
        cost_estimate=cost(12 * count * width * hid, 8 * count * width, count * hid),
        name="gradients",
    )(k, v, rate, one, three, two, after)


def merge_kernel(keep_ref, got_ref, *rest):
    rest[-1][...] = keep_ref[...] + got_ref[...].astype(F32)


def merge(keep, got, after):
    return pl.pallas_call(
        merge_kernel,
        out_shape=jax.ShapeDtypeStruct(keep.shape, F32),
        in_specs=full(2) + [pl.BlockSpec(memory_space=pl.ANY)] * len(after),
        out_specs=pl.BlockSpec(memory_space=pltpu.VMEM),
        compiler_params=params(),
        cost_estimate=cost(keep.size, 12 * keep.size),
        name="merge",
    )(keep, got, *after)


def core_step(parts, after, n):
    if len(parts) == 1:
        return parts[0]
    pair = [(at, at ^ 1) for at in range(n)]
    return merge(parts[0], lax.ppermute(parts[1], "cam", pair), after)


def sum_over_chips(mine, split, before, n):
    if not split:
        return [lax.psum(mine, "cam")]
    span = n.bit_length() - 2
    for step in range(span):
        pairs = []
        for at in range(n):
            bit = 1 + (step + (at & 1)) % span
            pairs.append((at, at ^ (1 << bit)))
        got = lax.ppermute(mine.astype(BF16), "cam", pairs)
        mine = merge(mine, got, before(step, mine))
    return [mine, lax.ppermute(mine.astype(BF16), "cam", [(at, at ^ 1) for at in range(n)])]


def readout_kernel(parts, q_ref, one_ref, three_ref, two_ref, *rest):
    grads, (y_ref, sq_ref, total, fresh) = rest[:parts], rest[-4:]
    hid, width = one_ref.shape[1:]
    if parts == 2:
        half = total.shape[0] // 2
        core = lax.axis_index("cam") & 1
        total[pl.ds(pl.multiple_of(core * half, half), half), :] = grads[0][...]
        total[pl.ds(pl.multiple_of((1 - core) * half, half), half), :] = grads[1][...].astype(F32)
    else:
        total[...] = grads[0][...]
    entries = hid * width
    for which, ref in enumerate((one_ref, three_ref, two_ref)):
        grad = total[which * hid : (which + 1) * hid, :]
        weight = ref[0].astype(F32)
        row_sq = jnp.sum(weight * weight, axis=1, keepdims=True)
        weight_sq = jnp.sum(row_sq, axis=0, keepdims=True)
        grad_sq = jnp.sum(jnp.sum(grad * grad, axis=1, keepdims=True), axis=0, keepdims=True)
        scale = jnp.sqrt(weight_sq / entries) / jnp.sqrt(grad_sq / entries + EPSILON)
        moved = weight - scale * grad
        ratio = jnp.sqrt(row_sq) / jnp.sqrt(
            jnp.sum(moved * moved, axis=1, keepdims=True) + EPSILON
        )
        fresh[which * hid : (which + 1) * hid, :] = (moved * ratio).astype(BF16)
    count = q_ref.shape[0]
    tile = min(count, TILE)
    ones = jnp.ones((8, width), BF16)
    for start in range(0, count, tile):
        here = slice(start, start + tile)
        q = q_ref[here, :]
        h_one = dot_bt(q, fresh[0:hid, :])
        h_three = dot_bt(q, fresh[hid : 2 * hid, :])
        active = (h_one * jax.nn.sigmoid(h_one) * h_three).astype(BF16)
        y = dot_bt(active, fresh[2 * hid :, :])
        y_ref[here, :] = y
        square = y * y
        high = square.astype(BF16)
        low = (square - high.astype(F32)).astype(BF16)
        sq_ref[:, here] = (dot_bt(ones, high) + dot_bt(ones, low))[0:1, :]


def read_out(q, one, three, two, grads, after):
    count, width = q.shape
    hid = one.shape[1]
    parts = len(grads)
    return pl.pallas_call(
        functools.partial(readout_kernel, parts),
        out_shape=[
            jax.ShapeDtypeStruct((count, width), F32),
            jax.ShapeDtypeStruct((1, count), F32),
        ],
        in_specs=full(4 + parts) + [pl.BlockSpec(memory_space=pl.ANY)] * len(after),
        out_specs=full(2),
        scratch_shapes=[pltpu.VMEM((3 * hid, width), F32), pltpu.VMEM((3 * hid, width), BF16)],
        compiler_params=params(),
        cost_estimate=cost(6 * count * width * hid, 8 * count * width, count * hid),
        name="read_out",
    )(q, one, three, two, *grads, *after)


def place_kernel(n, steps, order_ref, *outs):
    me = lax.axis_index("cam")
    count = order_ref.shape[1]
    rows = count // n
    size = len(steps) * rows
    at = lax.broadcasted_iota(jnp.int32, (8, size), 1)
    slots = at * 0
    for which, step in enumerate(steps):
        inside = jnp.logical_and(at >= which * rows, at < (which + 1) * rows)
        slots = jnp.where(inside, peer(me, step, n) * rows + at - which * rows, slots)
    slots = slots[0:1, :].astype(F32)
    each = outs[0].shape[1]
    for low in range(0, count, LANES):
        wanted = column(order_ref[:, low : low + LANES].astype(F32))
        for lane in range(0, size, LANES):
            hit = wanted == slots[:, lane : lane + LANES]
            out = outs[lane // each]
            start = lane % each
            out[low : low + LANES, start : start + LANES] = hit.astype(F32).astype(BF16)


def place(order, n, steps):
    count = order.shape[1]
    shape = jax.ShapeDtypeStruct((count, count // 2), BF16)
    return pl.pallas_call(
        functools.partial(place_kernel, n, tuple(steps)),
        out_shape=[shape, shape],
        in_specs=full(1),
        out_specs=full(2),
        compiler_params=params(),
        cost_estimate=cost(count * count, 2 * count * count),
        name="place",
    )(order)


def gathered(onehot, here, blocks):
    rows = blocks[0].shape[0]
    total = None
    for at, block in enumerate(blocks):
        part = dot(onehot[here, at * rows : (at + 1) * rows], block[...])
        total = part if total is None else total + part
    return total


def base_kernel(heads, gain_ref, y_ref, onehot, total_ref, *rest):
    blocks, out_ref = rest[:-1], rest[-1]
    count, width = y_ref.shape
    inverse = 1.0 / jnp.sqrt(total_ref[...] / (width * heads) + EPSILON)
    gain = gain_ref[...]
    tile = min(count, TILE)
    for low in range(0, count, tile):
        part = gathered(onehot, slice(low, low + tile), blocks)
        for at in range(0, tile, LANES):
            here = slice(low + at, low + at + LANES)
            norm = column(inverse[:, here])
            norm = jnp.concatenate([norm] * (width // LANES), axis=1)
            out_ref[here, :] = y_ref[here, :] * norm * gain + part[at : at + LANES]


def base(gain, y, onehot, total, heads, blocks):
    count, width = y.shape
    moved = len(blocks) * blocks[0].shape[0]
    return pl.pallas_call(
        functools.partial(base_kernel, heads),
        out_shape=jax.ShapeDtypeStruct((count, width), F32),
        in_specs=full(4 + len(blocks)),
        out_specs=pl.BlockSpec(memory_space=pltpu.VMEM),
        compiler_params=params(),
        cost_estimate=cost(2 * count * moved * width, 8 * count * width),
        name="base",
    )(gain, y, onehot, total, *blocks)


def mix_kernel(base_ref, onehot, *rest):
    blocks, (out_ref, held, sems) = rest[:-3], rest[-3:]
    count = base_ref.shape[0]
    tile = min(count, TILE)
    copies = []
    for at in range(count // tile):
        here = slice(at * tile, (at + 1) * tile)
        held[here, :] = (base_ref[here, :] + gathered(onehot, here, blocks)).astype(BF16)
        copies += fetch([(held.at[here], out_ref.at[here])], sems.at[at : at + 1])
    for copy in copies:
        copy.wait()


def mix(given, onehot, blocks):
    count, width = given.shape
    moved = len(blocks) * blocks[0].shape[0]
    tile = min(count, TILE)
    return pl.pallas_call(
        mix_kernel,
        out_shape=jax.ShapeDtypeStruct((count, width), BF16),
        in_specs=full(2 + len(blocks)),
        out_specs=pl.BlockSpec(memory_space=pltpu.HBM),
        scratch_shapes=[
            pltpu.VMEM((count, width), BF16),
            pltpu.SemaphoreType.DMA((count // tile,)),
        ],
        compiler_params=params(),
        cost_estimate=cost(2 * count * moved * width, 8 * count * width),
        name="mix",
    )(given, onehot, *blocks)


def sum_over_heads(square, heads, direct):
    if not power_of_two(heads) or direct:
        return square + sum(
            lax.ppermute(square, "head", [(at, (at + step) % heads) for at in range(heads)])
            for step in range(1, heads)
        )
    step = 1
    while step < heads:
        pairs = [(at, at ^ step) for at in range(heads)]
        square = square + lax.ppermute(square, "head", pairs)
        step *= 2
    return square


def exchange(block, step, n):
    return lax.ppermute(block, "cam", routes(step, n)) if step else block


def give_back(block, step, n):
    pairs = [(target, at) for at, target in routes(step, n)]
    return lax.ppermute(block, "cam", pairs) if step else block


def per_device(queries, keys, values, rates, w_one, w_three, w_two, gain, order):
    count, width = queries.shape
    n = lax.axis_size("cam")
    heads = lax.axis_size("head")
    steps = far_first(n)
    few = max(2, n // 4)
    half = few // 2
    weights = (w_one, w_three, w_two)
    groups = ((*steps[:half],), (*steps[half:few],), (*steps[few : 2 * few], 1), (*steps[2 * few : -2], 0))
    marks = mark(order, n, groups)
    arrived = {}
    tokens = []

    def send(which, after):
        blocks = sort_tokens(marks[which], queries, keys, values, after, n)
        tokens.append(blocks[-1])
        for step, block in zip(groups[which], blocks):
            arrived[step] = exchange(block, step, n)

    send(0, [])
    parts = gradients(keys, values, rates.reshape(1, count), *weights, tokens[0], n)
    early = steps[:few] + steps[n - few :]
    late = steps[few : n - few]
    early_places, late_places = place(order, n, early + late)
    mine = core_step(parts, [arrived[step] for step in steps[:half]], n)
    send(1, [mine])

    def before(step, mine):
        if step != 1:
            return []
        send(2, [mine])
        send(3, [])
        return [arrived[steps[1]], late_places] + tokens[2:3]

    summed = sum_over_chips(mine, len(parts) == 2, before, n)
    for which in range(len(tokens), len(groups)):
        send(which, [])
    came = [arrived[step] for step in steps]
    y, square = read_out(queries, *weights, summed, came[2:4] + tokens[3:])
    total = sum_over_heads(square, heads, False)
    attended = attend([arrived[step] for step in range(n)], [total], n, width)
    returned = {step: give_back(attended[step], step, n) for step in early + late}
    given = base(
        gain.reshape(1, width), y, early_places, total, heads, [returned[step] for step in early]
    )
    return mix(given, late_places, [returned[step] for step in late])


def solution(mesh):
    in_specs = (
        P("cam", "head"),
        P("cam", "head"),
        P("cam", "head"),
        P("cam", "head"),
        P("head", None, None),
        P("head", None, None),
        P("head", None, None),
        P("head"),
        P("cam", None),
    )
    out_specs = P("cam", "head")
    return jax.shard_map(
        per_device, mesh=mesh, in_specs=in_specs, out_specs=out_specs, check_vma=False
    )
```

```python
import functools

import jax
import jax.numpy as jnp
from jax import lax
from jax.experimental import pallas as pl
from jax.experimental.pallas import tpu as pltpu
from jax.sharding import PartitionSpec as P

PATCHES = 32
EPSILON = 1e-06
LANES = 128
TILE = 512
LIMIT = 24
COST = 1
FIRST_COST = pl.CostEstimate(flops=10**12, bytes_accessed=1024, transcendentals=0)
MIB = 1024 * 1024
F32 = jnp.float32
BF16 = jnp.bfloat16
TOKEN = jax.ShapeDtypeStruct((8, LANES), F32)


def dot(a, b):
    return lax.dot_general(a, b, (((1,), (0,)), ((), ())), preferred_element_type=F32)


def dot_bt(a, b):
    return lax.dot_general(a, b, (((1,), (1,)), ((), ())), preferred_element_type=F32)


def dot_at(a, b):
    return lax.dot_general(a, b, (((0,), (0,)), ((), ())), preferred_element_type=F32)


def params(limit=LIMIT):
    return pltpu.CompilerParams(vmem_limit_bytes=int(limit * MIB))


def full(count):
    return [pl.BlockSpec(memory_space=pltpu.VMEM)] * count


def cost(flops, moved, exps=0):
    return pl.CostEstimate(
        flops=int(flops) // COST,
        bytes_accessed=int(moved) // COST,
        transcendentals=int(exps) // COST,
    )


def power_of_two(n):
    return n & (n - 1) == 0


def crossed(step):
    return (step & ~6) | ((step & 2) << 1) | ((step & 4) >> 1)


def peer(me, step, n):
    if power_of_two(n):
        if n < 8:
            return me ^ step
        odd = me & 1
        return me ^ (step * (1 - odd) + crossed(step) * odd)
    ahead = me + step
    wrap = ahead - n
    return wrap * (wrap >= 0) + ahead * (wrap < 0)


def routes(step, n):
    return [(at, int(peer(at, step, n))) for at in range(n)]


def column(row):
    return jnp.broadcast_to(row, (LANES, LANES)).T


def far_first(n):
    return sorted(range(n), key=lambda step: (-(step >> 1).bit_count(), -step))


def fetch(pairs, sems):
    copies = []
    for at, (source, target) in enumerate(pairs):
        copies.append(pltpu.make_async_copy(source, target, sems.at[at]))
        copies[-1].start()
    return copies


def mark_kernel(n, steps, order_ref, *rest):
    outs, token = rest[:-1], rest[-1]
    token[...] = jnp.zeros_like(token)
    me = lax.axis_index("cam")
    count = order_ref.shape[1]
    rows = count // n
    order = order_ref[...]
    slot = lax.broadcasted_iota(jnp.int32, (rows, count), 0)
    for group, out in zip(steps, outs):
        for at, step in enumerate(group):
            hit = slot + peer(me, step, n) * rows == order
            out[at * rows : (at + 1) * rows, :] = hit.astype(F32).astype(BF16)


def mark(order, n, steps):
    count = order.shape[1]
    rows = count // n
    return pl.pallas_call(
        functools.partial(mark_kernel, n, steps),
        out_shape=[jax.ShapeDtypeStruct((len(group) * rows, count), BF16) for group in steps]
        + [TOKEN],
        in_specs=full(1),
        out_specs=full(len(steps) + 1),
        compiler_params=params(),
        cost_estimate=FIRST_COST,
        name="mark",
    )(order)


def sort_kernel(size, onehot, q_ref, k_ref, v_ref, *rest):
    outs, token = rest[-1 - size : -1], rest[-1]
    token[...] = jnp.zeros_like(token)
    rows, width = outs[0].shape[0], q_ref.shape[1]
    group = max(1, min(len(outs), TILE // rows))
    while len(outs) % group:
        group -= 1
    for first in range(0, len(outs), group):
        marks = onehot[first * rows : (first + group) * rows, :]
        for which, ref in enumerate((q_ref, k_ref, v_ref)):
            picked = dot(marks, ref[...]).astype(BF16)
            for at in range(group):
                outs[first + at][:, which * width : (which + 1) * width] = picked[
                    at * rows : (at + 1) * rows
                ]


def sort_tokens(onehot, q, k, v, after, n):
    count, width = q.shape
    rows = count // n
    size = onehot.shape[0] // rows
    return pl.pallas_call(
        functools.partial(sort_kernel, size),
        out_shape=[jax.ShapeDtypeStruct((rows, 3 * width), BF16)] * size + [TOKEN],
        in_specs=full(4) + [pl.BlockSpec(memory_space=pl.ANY)] * len(after),
        out_specs=full(size + 1),
        compiler_params=params(),
        cost_estimate=cost(6 * size * rows * count * width, 6 * count * width),
        name="sort_tokens",
    )(onehot, q, k, v, *after)


def attend_kernel(n, scale, *refs):
    ins, outs = refs[:n], refs[-3 - n : -3]
    q_all, k_all, v_all = refs[-3:]
    rows = ins[0].shape[0]
    width = outs[0].shape[1]
    group = n * PATCHES
    block = min(group, 256)
    for stamp in range(rows // PATCHES):
        here = slice(stamp * PATCHES, (stamp + 1) * PATCHES)
        for cam in range(n):
            there = slice(cam * PATCHES, (cam + 1) * PATCHES)
            q_all[there, :] = ins[cam][here, 0:width]
            k_all[there, :] = ins[cam][here, width : 2 * width]
            v_all[there, :] = ins[cam][here, 2 * width : 3 * width]
        for low in range(0, group, block):
            scores = dot_bt(q_all[low : low + block, :], k_all[...]) * scale
            scores = scores - jnp.max(scores, axis=-1, keepdims=True)
            expo = jnp.exp(scores)
            probs = (expo / jnp.sum(expo, axis=-1, keepdims=True)).astype(BF16)
            result = dot(probs, v_all[...]).astype(BF16)
            for cam in range(low // PATCHES, (low + block) // PATCHES):
                at = cam * PATCHES - low
                outs[cam][here, :] = result[at : at + PATCHES]


def attend(blocks, after, n, width):
    rows = blocks[0].shape[0]
    group = n * PATCHES
    return pl.pallas_call(
        functools.partial(attend_kernel, n, width**-0.5),
        out_shape=[jax.ShapeDtypeStruct((rows, width), BF16)] * n,
        in_specs=full(n) + [pl.BlockSpec(memory_space=pl.ANY)] * len(after),
        out_specs=full(n),
        scratch_shapes=[pltpu.VMEM((group, width), BF16)] * 3,
        compiler_params=params(),
        cost_estimate=cost(
            4 * n * rows * group * width, 8 * n * rows * width, n * rows * group
        ),
        name="attend",
    )(*blocks, *after)


def grads_kernel(n, split, k_ref, v_ref, rate_ref, one_ref, three_ref, two_ref, *rest):
    outs, total = rest[1:-1], rest[-1]
    count, width = k_ref.shape
    hid = one_ref.shape[1]
    one, three, two = one_ref[0], three_ref[0], two_ref[0]
    tile = min(count, TILE)
    for start in range(0, count, tile):
        k = k_ref[start : start + tile, :]
        h_one = dot_bt(k, one)
        h_three = dot_bt(k, three)
        sigma = jax.nn.sigmoid(h_one)
        gated = h_one * sigma
        active = (gated * h_three).astype(BF16)
        pieces = []
        for low in range(start, start + tile, LANES):
            rate = column(rate_ref[:, low : low + LANES])
            rate = jnp.concatenate([rate] * (width // LANES), axis=1)
            pieces.append((-rate * v_ref[low : low + LANES, :].astype(F32)).astype(BF16))
        error = jnp.concatenate(pieces, axis=0)
        back = dot(error, two)
        back_one = (back * h_three * sigma * (1.0 + h_one * (1.0 - sigma))).astype(BF16)
        back_three = (back * gated).astype(BF16)
        sums = (dot_at(back_one, k), dot_at(back_three, k), dot_at(error, active))
        for which, term in enumerate(sums):
            here = slice(which * hid, (which + 1) * hid)
            total[here, :] = term if start == 0 else total[here, :] + term
    if split:
        half = total.shape[0] // 2
        core = lax.axis_index("cam") & 1
        outs[0][...] = total[pl.ds(pl.multiple_of(core * half, half), half), :]
        other = total[pl.ds(pl.multiple_of((1 - core) * half, half), half), :]
        outs[1][...] = other.astype(BF16)
    else:
        outs[0][...] = total[...]


def gradients(k, v, rate, one, three, two, after, n):
    count, width = k.shape
    hid = one.shape[1]
    split = n > 1 and power_of_two(n)
    assert hid == width
    rows = 3 * hid
    parts = 2 if split else 1
    return pl.pallas_call(
        functools.partial(grads_kernel, n, split),
        out_shape=[
            jax.ShapeDtypeStruct((rows // parts, width), kind) for kind in (F32, BF16)[:parts]
        ],
        in_specs=full(6) + [pl.BlockSpec(memory_space=pl.ANY)],
        out_specs=full(parts),
        scratch_shapes=[pltpu.VMEM((rows, width), F32)],
        compiler_params=params(),
        cost_estimate=cost(12 * count * width * hid, 8 * count * width, count * hid),
        name="gradients",
    )(k, v, rate, one, three, two, after)


def merge_kernel(keep_ref, got_ref, *rest):
    rest[-1][...] = keep_ref[...] + got_ref[...].astype(F32)


def merge(keep, got, after):
    return pl.pallas_call(
        merge_kernel,
        out_shape=jax.ShapeDtypeStruct(keep.shape, F32),
        in_specs=full(2) + [pl.BlockSpec(memory_space=pl.ANY)] * len(after),
        out_specs=pl.BlockSpec(memory_space=pltpu.VMEM),
        compiler_params=params(),
        cost_estimate=cost(keep.size, 12 * keep.size),
        name="merge",
    )(keep, got, *after)


def core_step(parts, after, n):
    if len(parts) == 1:
        return parts[0]
    pair = [(at, at ^ 1) for at in range(n)]
    return merge(parts[0], lax.ppermute(parts[1], "cam", pair), after)


def sum_over_chips(mine, split, after, n):
    if not split:
        return [lax.psum(mine, "cam")]
    span = n.bit_length() - 2
    for step in range(span):
        pairs = []
        for at in range(n):
            bit = 1 + (step + (at & 1)) % span
            pairs.append((at, at ^ (1 << bit)))
        got = lax.ppermute(mine.astype(BF16), "cam", pairs)
        if step < len(after):
            mine = merge(mine, got, after[step])
        else:
            mine = mine + got.astype(F32)
    return [mine, lax.ppermute(mine, "cam", [(at, at ^ 1) for at in range(n)])]


def readout_kernel(parts, q_ref, one_ref, three_ref, two_ref, *rest):
    grads, (y_ref, sq_ref, total, fresh) = rest[:parts], rest[-4:]
    hid, width = one_ref.shape[1:]
    if parts == 2:
        half = total.shape[0] // 2
        core = lax.axis_index("cam") & 1
        total[pl.ds(pl.multiple_of(core * half, half), half), :] = grads[0][...]
        total[pl.ds(pl.multiple_of((1 - core) * half, half), half), :] = grads[1][...]
    else:
        total[...] = grads[0][...]
    entries = hid * width
    for which, ref in enumerate((one_ref, three_ref, two_ref)):
        grad = total[which * hid : (which + 1) * hid, :]
        weight = ref[0].astype(F32)
        row_sq = jnp.sum(weight * weight, axis=1, keepdims=True)
        weight_sq = jnp.sum(row_sq, axis=0, keepdims=True)
        grad_sq = jnp.sum(jnp.sum(grad * grad, axis=1, keepdims=True), axis=0, keepdims=True)
        scale = jnp.sqrt(weight_sq / entries) / jnp.sqrt(grad_sq / entries + EPSILON)
        moved = weight - scale * grad
        ratio = jnp.sqrt(row_sq) / jnp.sqrt(
            jnp.sum(moved * moved, axis=1, keepdims=True) + EPSILON
        )
        fresh[which * hid : (which + 1) * hid, :] = (moved * ratio).astype(BF16)
    count = q_ref.shape[0]
    tile = min(count, TILE)
    ones = jnp.ones((8, width), BF16)
    for start in range(0, count, tile):
        here = slice(start, start + tile)
        q = q_ref[here, :]
        h_one = dot_bt(q, fresh[0:hid, :])
        h_three = dot_bt(q, fresh[hid : 2 * hid, :])
        active = (h_one * jax.nn.sigmoid(h_one) * h_three).astype(BF16)
        y = dot_bt(active, fresh[2 * hid :, :])
        y_ref[here, :] = y
        square = y * y
        high = square.astype(BF16)
        low = (square - high.astype(F32)).astype(BF16)
        sq_ref[:, here] = (dot_bt(ones, high) + dot_bt(ones, low))[0:1, :]


def read_out(q, one, three, two, grads, after):
    count, width = q.shape
    hid = one.shape[1]
    parts = len(grads)
    return pl.pallas_call(
        functools.partial(readout_kernel, parts),
        out_shape=[
            jax.ShapeDtypeStruct((count, width), F32),
            jax.ShapeDtypeStruct((1, count), F32),
        ],
        in_specs=full(4 + parts) + [pl.BlockSpec(memory_space=pl.ANY)] * len(after),
        out_specs=full(2),
        scratch_shapes=[pltpu.VMEM((3 * hid, width), F32), pltpu.VMEM((3 * hid, width), BF16)],
        compiler_params=params(),
        cost_estimate=cost(6 * count * width * hid, 8 * count * width, count * hid),
        name="read_out",
    )(q, one, three, two, *grads, *after)


def place_kernel(n, steps, order_ref, *outs):
    me = lax.axis_index("cam")
    count = order_ref.shape[1]
    rows = count // n
    size = len(steps) * rows
    at = lax.broadcasted_iota(jnp.int32, (8, size), 1)
    slots = at * 0
    for which, step in enumerate(steps):
        inside = jnp.logical_and(at >= which * rows, at < (which + 1) * rows)
        slots = jnp.where(inside, peer(me, step, n) * rows + at - which * rows, slots)
    slots = slots[0:1, :].astype(F32)
    each = outs[0].shape[1]
    for low in range(0, count, LANES):
        wanted = column(order_ref[:, low : low + LANES].astype(F32))
        for lane in range(0, size, LANES):
            hit = wanted == slots[:, lane : lane + LANES]
            out = outs[lane // each]
            start = lane % each
            out[low : low + LANES, start : start + LANES] = hit.astype(F32).astype(BF16)


def place(order, n, steps):
    count = order.shape[1]
    shape = jax.ShapeDtypeStruct((count, count // 2), BF16)
    return pl.pallas_call(
        functools.partial(place_kernel, n, tuple(steps)),
        out_shape=[shape, shape],
        in_specs=full(1),
        out_specs=full(2),
        compiler_params=params(),
        cost_estimate=cost(count * count, 2 * count * count),
        name="place",
    )(order)


def gathered(onehot, here, blocks):
    rows = blocks[0].shape[0]
    total = None
    for at, block in enumerate(blocks):
        part = dot(onehot[here, at * rows : (at + 1) * rows], block[...])
        total = part if total is None else total + part
    return total


def base_kernel(heads, gain_ref, y_ref, onehot, total_ref, *rest):
    blocks, out_ref = rest[:-1], rest[-1]
    count, width = y_ref.shape
    inverse = 1.0 / jnp.sqrt(total_ref[...] / (width * heads) + EPSILON)
    gain = gain_ref[...]
    tile = min(count, TILE)
    for low in range(0, count, tile):
        part = gathered(onehot, slice(low, low + tile), blocks)
        for at in range(0, tile, LANES):
            here = slice(low + at, low + at + LANES)
            norm = column(inverse[:, here])
            norm = jnp.concatenate([norm] * (width // LANES), axis=1)
            out_ref[here, :] = y_ref[here, :] * norm * gain + part[at : at + LANES]


def base(gain, y, onehot, total, heads, blocks):
    count, width = y.shape
    moved = len(blocks) * blocks[0].shape[0]
    return pl.pallas_call(
        functools.partial(base_kernel, heads),
        out_shape=jax.ShapeDtypeStruct((count, width), F32),
        in_specs=full(4 + len(blocks)),
        out_specs=pl.BlockSpec(memory_space=pltpu.VMEM),
        compiler_params=params(),
        cost_estimate=cost(2 * count * moved * width, 8 * count * width),
        name="base",
    )(gain, y, onehot, total, *blocks)


def mix_kernel(base_ref, onehot, *rest):
    blocks, (out_ref, held, sems) = rest[:-3], rest[-3:]
    count = base_ref.shape[0]
    tile = min(count, TILE)
    copies = []
    for at in range(count // tile):
        here = slice(at * tile, (at + 1) * tile)
        held[here, :] = (base_ref[here, :] + gathered(onehot, here, blocks)).astype(BF16)
        copies += fetch([(held.at[here], out_ref.at[here])], sems.at[at : at + 1])
    for copy in copies:
        copy.wait()


def mix(given, onehot, blocks):
    count, width = given.shape
    moved = len(blocks) * blocks[0].shape[0]
    tile = min(count, TILE)
    return pl.pallas_call(
        mix_kernel,
        out_shape=jax.ShapeDtypeStruct((count, width), BF16),
        in_specs=full(2 + len(blocks)),
        out_specs=pl.BlockSpec(memory_space=pltpu.HBM),
        scratch_shapes=[
            pltpu.VMEM((count, width), BF16),
            pltpu.SemaphoreType.DMA((count // tile,)),
        ],
        compiler_params=params(),
        cost_estimate=cost(2 * count * moved * width, 8 * count * width),
        name="mix",
    )(given, onehot, *blocks)


def sum_over_heads(square, heads):
    if not power_of_two(heads):
        return [lax.psum(square, "head")]
    sums = [square]
    step = 1
    while step < heads:
        pairs = [(at, at ^ step) for at in range(heads)]
        sums.append(sums[-1] + lax.ppermute(sums[-1], "head", pairs))
        step *= 2
    return sums


def exchange(block, step, n):
    return lax.ppermute(block, "cam", routes(step, n)) if step else block


def give_back(block, step, n):
    pairs = [(target, at) for at, target in routes(step, n)]
    return lax.ppermute(block, "cam", pairs) if step else block


def per_device(queries, keys, values, rates, w_one, w_three, w_two, gain, order):
    count, width = queries.shape
    n = lax.axis_size("cam")
    heads = lax.axis_size("head")
    steps = far_first(n)
    few = max(1, n // 4)
    weights = (w_one, w_three, w_two)
    groups = (tuple(steps[:few]), tuple(steps[few : 2 * few]), tuple(steps[2 * few :]))
    marks = mark(order, n, groups)
    arrived = {}
    tokens = []
    for group, onehot in zip(groups, marks):
        blocks = sort_tokens(onehot, queries, keys, values, [], n)
        tokens.append(blocks[-1])
        for step, block in zip(group, blocks):
            arrived[step] = exchange(block, step, n)
    came = [arrived[step] for step in steps]
    parts = gradients(keys, values, rates.reshape(1, count), *weights, tokens[0], n)
    early = steps[:few] + steps[n - few :]
    late = steps[few : n - few]
    early_places, late_places = place(order, n, early + late)
    mine = core_step(parts, [came[0]], n)
    summed = sum_over_chips(mine, len(parts) == 2, [tokens[1:2], came[1:3] + tokens[2:] + [late_places]], n)
    y, square = read_out(queries, *weights, summed, came[3:4])
    sums = sum_over_heads(square, heads)
    total = sums[-1]
    attended = attend([arrived[step] for step in range(n)], [sums[len(sums) // 2]], n, width)
    returned = {step: give_back(attended[step], step, n) for step in early + late}
    given = base(
        gain.reshape(1, width), y, early_places, total, heads, [returned[step] for step in early]
    )
    return mix(given, late_places, [returned[step] for step in late])


def solution(mesh):
    in_specs = (
        P("cam", "head"),
        P("cam", "head"),
        P("cam", "head"),
        P("cam", "head"),
        P("head", None, None),
        P("head", None, None),
        P("head", None, None),
        P("head"),
        P("cam", None),
    )
    out_specs = P("cam", "head")
    return jax.shard_map(
        per_device, mesh=mesh, in_specs=in_specs, out_specs=out_specs, check_vma=False
    )
```

```python
import functools

import jax
import jax.numpy as jnp
from jax import lax
from jax.experimental import pallas as pl
from jax.experimental.pallas import tpu as pltpu
from jax.sharding import PartitionSpec as P

PATCHES = 32
EPSILON = 1e-06
LANES = 128
TILE = 512
LIMIT = 24
COST = 1
FIRST_COST = pl.CostEstimate(flops=10**12, bytes_accessed=1024, transcendentals=0)
MIB = 1024 * 1024
F32 = jnp.float32
BF16 = jnp.bfloat16
TOKEN = jax.ShapeDtypeStruct((8, LANES), F32)


def dot(a, b):
    return lax.dot_general(a, b, (((1,), (0,)), ((), ())), preferred_element_type=F32)


def dot_bt(a, b):
    return lax.dot_general(a, b, (((1,), (1,)), ((), ())), preferred_element_type=F32)


def dot_at(a, b):
    return lax.dot_general(a, b, (((0,), (0,)), ((), ())), preferred_element_type=F32)


def params(limit=LIMIT):
    return pltpu.CompilerParams(vmem_limit_bytes=int(limit * MIB))


def full(count):
    return [pl.BlockSpec(memory_space=pltpu.VMEM)] * count


def cost(flops, moved, exps=0):
    return pl.CostEstimate(
        flops=int(flops) // COST,
        bytes_accessed=int(moved) // COST,
        transcendentals=int(exps) // COST,
    )


def power_of_two(n):
    return n & (n - 1) == 0


def crossed(step):
    return (step & ~6) | ((step & 2) << 1) | ((step & 4) >> 1)


def peer(me, step, n):
    if power_of_two(n):
        if n < 8:
            return me ^ step
        odd = me & 1
        return me ^ (step * (1 - odd) + crossed(step) * odd)
    ahead = me + step
    wrap = ahead - n
    return wrap * (wrap >= 0) + ahead * (wrap < 0)


def routes(step, n):
    return [(at, int(peer(at, step, n))) for at in range(n)]


def column(row):
    return jnp.broadcast_to(row, (LANES, LANES)).T


def far_first(n):
    return sorted(range(n), key=lambda step: (-(step >> 1).bit_count(), -step))


def fetch(pairs, sems):
    copies = []
    for at, (source, target) in enumerate(pairs):
        copies.append(pltpu.make_async_copy(source, target, sems.at[at]))
        copies[-1].start()
    return copies


def mark_kernel(n, steps, order_ref, *rest):
    outs, token = rest[:-1], rest[-1]
    token[...] = jnp.zeros_like(token)
    me = lax.axis_index("cam")
    count = order_ref.shape[1]
    rows = count // n
    order = order_ref[...]
    slot = lax.broadcasted_iota(jnp.int32, (rows, count), 0)
    for group, out in zip(steps, outs):
        for at, step in enumerate(group):
            hit = slot + peer(me, step, n) * rows == order
            out[at * rows : (at + 1) * rows, :] = hit.astype(F32).astype(BF16)


def mark(order, n, steps):
    count = order.shape[1]
    rows = count // n
    return pl.pallas_call(
        functools.partial(mark_kernel, n, steps),
        out_shape=[jax.ShapeDtypeStruct((len(group) * rows, count), BF16) for group in steps]
        + [TOKEN],
        in_specs=full(1),
        out_specs=full(len(steps) + 1),
        compiler_params=params(),
        cost_estimate=FIRST_COST,
        name="mark",
    )(order)


def sort_kernel(size, onehot, q_ref, k_ref, v_ref, *rest):
    outs, token = rest[-1 - size : -1], rest[-1]
    token[...] = jnp.zeros_like(token)
    rows, width = outs[0].shape[0], q_ref.shape[1]
    group = max(1, min(len(outs), TILE // rows))
    while len(outs) % group:
        group -= 1
    for first in range(0, len(outs), group):
        marks = onehot[first * rows : (first + group) * rows, :]
        for which, ref in enumerate((q_ref, k_ref, v_ref)):
            picked = dot(marks, ref[...]).astype(BF16)
            for at in range(group):
                outs[first + at][:, which * width : (which + 1) * width] = picked[
                    at * rows : (at + 1) * rows
                ]


def sort_tokens(onehot, q, k, v, after, n):
    count, width = q.shape
    rows = count // n
    size = onehot.shape[0] // rows
    return pl.pallas_call(
        functools.partial(sort_kernel, size),
        out_shape=[jax.ShapeDtypeStruct((rows, 3 * width), BF16)] * size + [TOKEN],
        in_specs=full(4) + [pl.BlockSpec(memory_space=pl.ANY)] * len(after),
        out_specs=full(size + 1),
        compiler_params=params(),
        cost_estimate=cost(6 * size * rows * count * width, 6 * count * width),
        name="sort_tokens",
    )(onehot, q, k, v, *after)


def attend_kernel(n, scale, *refs):
    ins, outs = refs[:n], refs[-3 - n : -3]
    q_all, k_all, v_all = refs[-3:]
    rows = ins[0].shape[0]
    width = outs[0].shape[1]
    group = n * PATCHES
    block = min(group, 256)
    for stamp in range(rows // PATCHES):
        here = slice(stamp * PATCHES, (stamp + 1) * PATCHES)
        for cam in range(n):
            there = slice(cam * PATCHES, (cam + 1) * PATCHES)
            q_all[there, :] = ins[cam][here, 0:width]
            k_all[there, :] = ins[cam][here, width : 2 * width]
            v_all[there, :] = ins[cam][here, 2 * width : 3 * width]
        for low in range(0, group, block):
            scores = dot_bt(q_all[low : low + block, :], k_all[...]) * scale
            scores = scores - jnp.max(scores, axis=-1, keepdims=True)
            expo = jnp.exp(scores)
            probs = (expo / jnp.sum(expo, axis=-1, keepdims=True)).astype(BF16)
            result = dot(probs, v_all[...]).astype(BF16)
            for cam in range(low // PATCHES, (low + block) // PATCHES):
                at = cam * PATCHES - low
                outs[cam][here, :] = result[at : at + PATCHES]


def attend(blocks, after, n, width):
    rows = blocks[0].shape[0]
    group = n * PATCHES
    return pl.pallas_call(
        functools.partial(attend_kernel, n, width**-0.5),
        out_shape=[jax.ShapeDtypeStruct((rows, width), BF16)] * n,
        in_specs=full(n) + [pl.BlockSpec(memory_space=pl.ANY)] * len(after),
        out_specs=full(n),
        scratch_shapes=[pltpu.VMEM((group, width), BF16)] * 3,
        compiler_params=params(),
        cost_estimate=cost(
            4 * n * rows * group * width, 8 * n * rows * width, n * rows * group
        ),
        name="attend",
    )(*blocks, *after)


def grads_kernel(n, split, k_ref, v_ref, rate_ref, one_ref, three_ref, two_ref, *rest):
    outs, total = rest[1:-1], rest[-1]
    count, width = k_ref.shape
    hid = one_ref.shape[1]
    one, three, two = one_ref[0], three_ref[0], two_ref[0]
    tile = min(count, TILE)
    for start in range(0, count, tile):
        k = k_ref[start : start + tile, :]
        h_one = dot_bt(k, one)
        h_three = dot_bt(k, three)
        sigma = jax.nn.sigmoid(h_one)
        gated = h_one * sigma
        active = (gated * h_three).astype(BF16)
        pieces = []
        for low in range(start, start + tile, LANES):
            rate = column(rate_ref[:, low : low + LANES])
            rate = jnp.concatenate([rate] * (width // LANES), axis=1)
            pieces.append((-rate * v_ref[low : low + LANES, :].astype(F32)).astype(BF16))
        error = jnp.concatenate(pieces, axis=0)
        back = dot(error, two)
        back_one = (back * h_three * sigma * (1.0 + h_one * (1.0 - sigma))).astype(BF16)
        back_three = (back * gated).astype(BF16)
        sums = (dot_at(back_one, k), dot_at(back_three, k), dot_at(error, active))
        for which, term in enumerate(sums):
            here = slice(which * hid, (which + 1) * hid)
            total[here, :] = term if start == 0 else total[here, :] + term
    if split:
        half = total.shape[0] // 2
        core = lax.axis_index("cam") & 1
        outs[0][...] = total[pl.ds(pl.multiple_of(core * half, half), half), :]
        other = total[pl.ds(pl.multiple_of((1 - core) * half, half), half), :]
        outs[1][...] = other.astype(BF16)
    else:
        outs[0][...] = total[...]


def gradients(k, v, rate, one, three, two, after, n):
    count, width = k.shape
    hid = one.shape[1]
    split = n > 1 and power_of_two(n)
    assert hid == width
    rows = 3 * hid
    parts = 2 if split else 1
    return pl.pallas_call(
        functools.partial(grads_kernel, n, split),
        out_shape=[
            jax.ShapeDtypeStruct((rows // parts, width), kind) for kind in (F32, BF16)[:parts]
        ],
        in_specs=full(6) + [pl.BlockSpec(memory_space=pl.ANY)],
        out_specs=full(parts),
        scratch_shapes=[pltpu.VMEM((rows, width), F32)],
        compiler_params=params(),
        cost_estimate=cost(12 * count * width * hid, 8 * count * width, count * hid),
        name="gradients",
    )(k, v, rate, one, three, two, after)


def merge_kernel(keep_ref, got_ref, *rest):
    rest[-1][...] = keep_ref[...] + got_ref[...].astype(F32)


def merge(keep, got, after):
    return pl.pallas_call(
        merge_kernel,
        out_shape=jax.ShapeDtypeStruct(keep.shape, F32),
        in_specs=full(2) + [pl.BlockSpec(memory_space=pl.ANY)] * len(after),
        out_specs=pl.BlockSpec(memory_space=pltpu.VMEM),
        compiler_params=params(),
        cost_estimate=cost(keep.size, 12 * keep.size),
        name="merge",
    )(keep, got, *after)


def core_step(parts, after, n):
    if len(parts) == 1:
        return parts[0]
    pair = [(at, at ^ 1) for at in range(n)]
    return merge(parts[0], lax.ppermute(parts[1], "cam", pair), after)


def sum_over_chips(mine, split, after, n):
    if not split:
        return [lax.psum(mine, "cam")]
    span = n.bit_length() - 2
    for step in range(span):
        pairs = []
        for at in range(n):
            bit = 1 + (step + (at & 1)) % span
            pairs.append((at, at ^ (1 << bit)))
        got = lax.ppermute(mine.astype(BF16), "cam", pairs)
        if step < len(after):
            mine = merge(mine, got, after[step])
        else:
            mine = mine + got.astype(F32)
    return [mine, lax.ppermute(mine, "cam", [(at, at ^ 1) for at in range(n)])]


def readout_kernel(parts, q_ref, one_ref, three_ref, two_ref, *rest):
    grads, (y_ref, sq_ref, total, fresh) = rest[:parts], rest[-4:]
    hid, width = one_ref.shape[1:]
    if parts == 2:
        half = total.shape[0] // 2
        core = lax.axis_index("cam") & 1
        total[pl.ds(pl.multiple_of(core * half, half), half), :] = grads[0][...]
        total[pl.ds(pl.multiple_of((1 - core) * half, half), half), :] = grads[1][...]
    else:
        total[...] = grads[0][...]
    entries = hid * width
    for which, ref in enumerate((one_ref, three_ref, two_ref)):
        grad = total[which * hid : (which + 1) * hid, :]
        weight = ref[0].astype(F32)
        row_sq = jnp.sum(weight * weight, axis=1, keepdims=True)
        weight_sq = jnp.sum(row_sq, axis=0, keepdims=True)
        grad_sq = jnp.sum(jnp.sum(grad * grad, axis=1, keepdims=True), axis=0, keepdims=True)
        scale = jnp.sqrt(weight_sq / entries) / jnp.sqrt(grad_sq / entries + EPSILON)
        moved = weight - scale * grad
        ratio = jnp.sqrt(row_sq) / jnp.sqrt(
            jnp.sum(moved * moved, axis=1, keepdims=True) + EPSILON
        )
        fresh[which * hid : (which + 1) * hid, :] = (moved * ratio).astype(BF16)
    count = q_ref.shape[0]
    tile = min(count, TILE)
    ones = jnp.ones((8, width), BF16)
    for start in range(0, count, tile):
        here = slice(start, start + tile)
        q = q_ref[here, :]
        h_one = dot_bt(q, fresh[0:hid, :])
        h_three = dot_bt(q, fresh[hid : 2 * hid, :])
        active = (h_one * jax.nn.sigmoid(h_one) * h_three).astype(BF16)
        y = dot_bt(active, fresh[2 * hid :, :])
        y_ref[here, :] = y
        square = y * y
        high = square.astype(BF16)
        low = (square - high.astype(F32)).astype(BF16)
        sq_ref[:, here] = (dot_bt(ones, high) + dot_bt(ones, low))[0:1, :]


def read_out(q, one, three, two, grads, after):
    count, width = q.shape
    hid = one.shape[1]
    parts = len(grads)
    return pl.pallas_call(
        functools.partial(readout_kernel, parts),
        out_shape=[
            jax.ShapeDtypeStruct((count, width), F32),
            jax.ShapeDtypeStruct((1, count), F32),
        ],
        in_specs=full(4 + parts) + [pl.BlockSpec(memory_space=pl.ANY)] * len(after),
        out_specs=full(2),
        scratch_shapes=[pltpu.VMEM((3 * hid, width), F32), pltpu.VMEM((3 * hid, width), BF16)],
        compiler_params=params(),
        cost_estimate=cost(6 * count * width * hid, 8 * count * width, count * hid),
        name="read_out",
    )(q, one, three, two, *grads, *after)


def place_kernel(n, steps, order_ref, *outs):
    me = lax.axis_index("cam")
    count = order_ref.shape[1]
    rows = count // n
    size = len(steps) * rows
    at = lax.broadcasted_iota(jnp.int32, (8, size), 1)
    slots = at * 0
    for which, step in enumerate(steps):
        inside = jnp.logical_and(at >= which * rows, at < (which + 1) * rows)
        slots = jnp.where(inside, peer(me, step, n) * rows + at - which * rows, slots)
    slots = slots[0:1, :].astype(F32)
    split = outs[0].shape[1]
    for low in range(0, count, LANES):
        wanted = column(order_ref[:, low : low + LANES].astype(F32))
        for lane in range(0, size, LANES):
            hit = wanted == slots[:, lane : lane + LANES]
            out = outs[0] if lane < split else outs[1]
            start = lane if lane < split else lane - split
            out[low : low + LANES, start : start + LANES] = hit.astype(F32).astype(BF16)


def place(order, n, early, late):
    count = order.shape[1]
    rows = count // n
    shapes = [jax.ShapeDtypeStruct((count, len(each) * rows), BF16) for each in (early, late)]
    return pl.pallas_call(
        functools.partial(place_kernel, n, (*early, *late)),
        out_shape=shapes,
        in_specs=full(1),
        out_specs=full(2),
        compiler_params=params(),
        cost_estimate=cost(count * count, 2 * count * count),
        name="place",
    )(order)


def gathered(onehot, here, blocks):
    rows = blocks[0].shape[0]
    total = None
    for at, block in enumerate(blocks):
        part = dot(onehot[here, at * rows : (at + 1) * rows], block[...])
        total = part if total is None else total + part
    return total


def base_kernel(heads, gain_ref, y_ref, onehot, total_ref, *rest):
    blocks, out_ref = rest[:-1], rest[-1]
    count, width = y_ref.shape
    inverse = 1.0 / jnp.sqrt(total_ref[...] / (width * heads) + EPSILON)
    gain = gain_ref[...]
    tile = min(count, TILE)
    for low in range(0, count, tile):
        part = gathered(onehot, slice(low, low + tile), blocks)
        for at in range(0, tile, LANES):
            here = slice(low + at, low + at + LANES)
            norm = column(inverse[:, here])
            norm = jnp.concatenate([norm] * (width // LANES), axis=1)
            out_ref[here, :] = y_ref[here, :] * norm * gain + part[at : at + LANES]


def base(gain, y, onehot, total, heads, blocks):
    count, width = y.shape
    moved = len(blocks) * blocks[0].shape[0]
    return pl.pallas_call(
        functools.partial(base_kernel, heads),
        out_shape=jax.ShapeDtypeStruct((count, width), F32),
        in_specs=full(4 + len(blocks)),
        out_specs=pl.BlockSpec(memory_space=pltpu.VMEM),
        compiler_params=params(),
        cost_estimate=cost(2 * count * moved * width, 8 * count * width),
        name="base",
    )(gain, y, onehot, total, *blocks)


def mix_kernel(base_ref, onehot, *rest):
    blocks, (out_ref, held, sems) = rest[:-3], rest[-3:]
    count = base_ref.shape[0]
    tile = min(count, TILE)
    copies = []
    for at in range(count // tile):
        here = slice(at * tile, (at + 1) * tile)
        held[here, :] = (base_ref[here, :] + gathered(onehot, here, blocks)).astype(BF16)
        copies += fetch([(held.at[here], out_ref.at[here])], sems.at[at : at + 1])
    for copy in copies:
        copy.wait()


def mix(given, onehot, blocks):
    count, width = given.shape
    moved = len(blocks) * blocks[0].shape[0]
    tile = min(count, TILE)
    return pl.pallas_call(
        mix_kernel,
        out_shape=jax.ShapeDtypeStruct((count, width), BF16),
        in_specs=full(2 + len(blocks)),
        out_specs=pl.BlockSpec(memory_space=pltpu.HBM),
        scratch_shapes=[
            pltpu.VMEM((count, width), BF16),
            pltpu.SemaphoreType.DMA((count // tile,)),
        ],
        compiler_params=params(),
        cost_estimate=cost(2 * count * moved * width, 8 * count * width),
        name="mix",
    )(given, onehot, *blocks)


def head_steps(heads):
    return heads.bit_length() - 1 if power_of_two(heads) else 0


def head_sum(square, heads, low, high):
    if head_steps(heads) == 0:
        return square if low else lax.psum(square, "head")
    for step in range(low, high):
        pairs = [(at, at ^ (1 << step)) for at in range(heads)]
        got = lax.ppermute(square, "head", pairs)
        square = square + got
    return square


def held(array, after):
    return merge(array, jnp.zeros_like(array), after)


def exchange(block, step, n):
    return lax.ppermute(block, "cam", routes(step, n)) if step else block


def give_back(block, step, n):
    pairs = [(target, at) for at, target in routes(step, n)]
    return lax.ppermute(block, "cam", pairs) if step else block


def per_device(queries, keys, values, rates, w_one, w_three, w_two, gain, order):
    count, width = queries.shape
    n = lax.axis_size("cam")
    heads = lax.axis_size("head")
    steps = far_first(n)
    few = max(1, n // 4)
    weights = (w_one, w_three, w_two)
    groups = (tuple(steps[:few]), tuple(steps[few : 2 * few]), tuple(steps[2 * few :]))
    marks = mark(order, n, groups)
    arrived = {}
    tokens = []
    for group, onehot in zip(groups, marks):
        blocks = sort_tokens(onehot, queries, keys, values, [], n)
        tokens.append(blocks[-1])
        for step, block in zip(group, blocks):
            arrived[step] = exchange(block, step, n)
    came = [arrived[step] for step in steps]
    parts = gradients(keys, values, rates.reshape(1, count), *weights, tokens[0], n)
    early = steps[: 2 * few] + steps[n - few :]
    late = steps[2 * few : n - few]
    early_places, late_places = place(order, n, early, late)
    mine = core_step(parts, [came[0]], n)
    summed = sum_over_chips(mine, len(parts) == 2, [tokens[1:2], came[1:3] + tokens[2:] + [late_places]], n)
    y, square = read_out(queries, *weights, summed, came[3:4])
    half = head_steps(heads) // 2
    square = head_sum(square, heads, 0, half)
    attended = attend([arrived[step] for step in range(n)], [square], n, width)
    returned = {step: give_back(attended[step], step, n) for step in early + late}
    square = held(square, [returned[steps[0]]])
    total = head_sum(square, heads, half, head_steps(heads))
    given = base(
        gain.reshape(1, width), y, early_places, total, heads, [returned[step] for step in early]
    )
    return mix(given, late_places, [returned[step] for step in late])


def solution(mesh):
    in_specs = (
        P("cam", "head"),
        P("cam", "head"),
        P("cam", "head"),
        P("cam", "head"),
        P("head", None, None),
        P("head", None, None),
        P("head", None, None),
        P("head"),
        P("cam", None),
    )
    out_specs = P("cam", "head")
    return jax.shard_map(
        per_device, mesh=mesh, in_specs=in_specs, out_specs=out_specs, check_vma=False
    )
```

```python
import functools

import jax
import jax.numpy as jnp
from jax import lax
from jax.experimental import pallas as pl
from jax.experimental.pallas import tpu as pltpu
from jax.sharding import PartitionSpec as P

PATCHES = 32
EPSILON = 1e-06
LANES = 128
TILE = 512
LIMIT = 24
COST = 1
FIRST_COST = pl.CostEstimate(flops=10**12, bytes_accessed=1024, transcendentals=0)
MIB = 1024 * 1024
F32 = jnp.float32
BF16 = jnp.bfloat16
TOKEN = jax.ShapeDtypeStruct((8, LANES), F32)


def dot(a, b):
    return lax.dot_general(a, b, (((1,), (0,)), ((), ())), preferred_element_type=F32)


def dot_bt(a, b):
    return lax.dot_general(a, b, (((1,), (1,)), ((), ())), preferred_element_type=F32)


def dot_at(a, b):
    return lax.dot_general(a, b, (((0,), (0,)), ((), ())), preferred_element_type=F32)


def params(limit=LIMIT):
    return pltpu.CompilerParams(vmem_limit_bytes=int(limit * MIB))


def full(count):
    return [pl.BlockSpec(memory_space=pltpu.VMEM)] * count


def cost(flops, moved, exps=0):
    return pl.CostEstimate(
        flops=int(flops) // COST,
        bytes_accessed=int(moved) // COST,
        transcendentals=int(exps) // COST,
    )


def power_of_two(n):
    return n & (n - 1) == 0


def crossed(step):
    return (step & ~6) | ((step & 2) << 1) | ((step & 4) >> 1)


def peer(me, step, n):
    if power_of_two(n):
        if n < 8:
            return me ^ step
        odd = me & 1
        return me ^ (step * (1 - odd) + crossed(step) * odd)
    ahead = me + step
    wrap = ahead - n
    return wrap * (wrap >= 0) + ahead * (wrap < 0)


def routes(step, n):
    return [(at, int(peer(at, step, n))) for at in range(n)]


def column(row):
    return jnp.broadcast_to(row, (LANES, LANES)).T


def far_first(n):
    return sorted(range(n), key=lambda step: (-(step >> 1).bit_count(), -step))


def fetch(pairs, sems):
    copies = []
    for at, (source, target) in enumerate(pairs):
        copies.append(pltpu.make_async_copy(source, target, sems.at[at]))
        copies[-1].start()
    return copies


def mark_kernel(n, steps, order_ref, *rest):
    outs, token = rest[:-1], rest[-1]
    token[...] = jnp.zeros_like(token)
    me = lax.axis_index("cam")
    count = order_ref.shape[1]
    rows = count // n
    order = order_ref[...]
    slot = lax.broadcasted_iota(jnp.int32, (rows, count), 0)
    for group, out in zip(steps, outs):
        for at, step in enumerate(group):
            hit = slot + peer(me, step, n) * rows == order
            out[at * rows : (at + 1) * rows, :] = hit.astype(F32).astype(BF16)


def mark(order, n, steps):
    count = order.shape[1]
    rows = count // n
    return pl.pallas_call(
        functools.partial(mark_kernel, n, steps),
        out_shape=[jax.ShapeDtypeStruct((len(group) * rows, count), BF16) for group in steps]
        + [TOKEN],
        in_specs=full(1),
        out_specs=full(len(steps) + 1),
        compiler_params=params(),
        cost_estimate=FIRST_COST,
        name="mark",
    )(order)


def sort_kernel(size, onehot, q_ref, k_ref, v_ref, *rest):
    outs, token = rest[-1 - size : -1], rest[-1]
    token[...] = jnp.zeros_like(token)
    rows, width = outs[0].shape[0], q_ref.shape[1]
    group = max(1, min(len(outs), TILE // rows))
    while len(outs) % group:
        group -= 1
    for first in range(0, len(outs), group):
        marks = onehot[first * rows : (first + group) * rows, :]
        for which, ref in enumerate((q_ref, k_ref, v_ref)):
            picked = dot(marks, ref[...]).astype(BF16)
            for at in range(group):
                outs[first + at][:, which * width : (which + 1) * width] = picked[
                    at * rows : (at + 1) * rows
                ]


def sort_tokens(onehot, q, k, v, after, n):
    count, width = q.shape
    rows = count // n
    size = onehot.shape[0] // rows
    return pl.pallas_call(
        functools.partial(sort_kernel, size),
        out_shape=[jax.ShapeDtypeStruct((rows, 3 * width), BF16)] * size + [TOKEN],
        in_specs=full(4) + [pl.BlockSpec(memory_space=pl.ANY)] * len(after),
        out_specs=full(size + 1),
        compiler_params=params(),
        cost_estimate=cost(6 * size * rows * count * width, 6 * count * width),
        name="sort_tokens",
    )(onehot, q, k, v, *after)


def attend_kernel(n, scale, chosen, *refs):
    ins, outs = refs[:n], refs[-3 - len(chosen) : -3]
    q_all, k_all, v_all = refs[-3:]
    rows = ins[0].shape[0]
    width = outs[0].shape[1]
    asked = len(chosen) * PATCHES
    block = min(asked, 256)
    while asked % block:
        block -= PATCHES
    for stamp in range(rows // PATCHES):
        here = slice(stamp * PATCHES, (stamp + 1) * PATCHES)
        for at, cam in enumerate(chosen):
            q_all[at * PATCHES : (at + 1) * PATCHES, :] = ins[cam][here, 0:width]
        for cam in range(n):
            there = slice(cam * PATCHES, (cam + 1) * PATCHES)
            k_all[there, :] = ins[cam][here, width : 2 * width]
            v_all[there, :] = ins[cam][here, 2 * width : 3 * width]
        for low in range(0, asked, block):
            scores = dot_bt(q_all[low : low + block, :], k_all[...]) * scale
            scores = scores - jnp.max(scores, axis=-1, keepdims=True)
            expo = jnp.exp(scores)
            probs = (expo / jnp.sum(expo, axis=-1, keepdims=True)).astype(BF16)
            result = dot(probs, v_all[...]).astype(BF16)
            for at in range(low // PATCHES, (low + block) // PATCHES):
                start = at * PATCHES - low
                outs[at][here, :] = result[start : start + PATCHES]


def attend(blocks, chosen, after, n, width):
    rows = blocks[0].shape[0]
    group = n * PATCHES
    asked = len(chosen)
    return pl.pallas_call(
        functools.partial(attend_kernel, n, width**-0.5, tuple(chosen)),
        out_shape=[jax.ShapeDtypeStruct((rows, width), BF16)] * asked,
        in_specs=full(n) + [pl.BlockSpec(memory_space=pl.ANY)] * len(after),
        out_specs=full(asked),
        scratch_shapes=[pltpu.VMEM((asked * PATCHES, width), BF16)]
        + [pltpu.VMEM((group, width), BF16)] * 2,
        compiler_params=params(),
        cost_estimate=cost(
            4 * asked * rows * group * width, 8 * n * rows * width, asked * rows * group
        ),
        name="attend",
    )(*blocks, *after)


def grads_kernel(n, split, k_ref, v_ref, rate_ref, one_ref, three_ref, two_ref, *rest):
    outs, total = rest[1:-1], rest[-1]
    count, width = k_ref.shape
    hid = one_ref.shape[1]
    one, three, two = one_ref[0], three_ref[0], two_ref[0]
    tile = min(count, TILE)
    for start in range(0, count, tile):
        k = k_ref[start : start + tile, :]
        h_one = dot_bt(k, one)
        h_three = dot_bt(k, three)
        sigma = jax.nn.sigmoid(h_one)
        gated = h_one * sigma
        active = (gated * h_three).astype(BF16)
        pieces = []
        for low in range(start, start + tile, LANES):
            rate = column(rate_ref[:, low : low + LANES])
            rate = jnp.concatenate([rate] * (width // LANES), axis=1)
            pieces.append((-rate * v_ref[low : low + LANES, :].astype(F32)).astype(BF16))
        error = jnp.concatenate(pieces, axis=0)
        back = dot(error, two)
        back_one = (back * h_three * sigma * (1.0 + h_one * (1.0 - sigma))).astype(BF16)
        back_three = (back * gated).astype(BF16)
        sums = (dot_at(back_one, k), dot_at(back_three, k), dot_at(error, active))
        for which, term in enumerate(sums):
            here = slice(which * hid, (which + 1) * hid)
            total[here, :] = term if start == 0 else total[here, :] + term
    if split:
        half = total.shape[0] // 2
        core = lax.axis_index("cam") & 1
        outs[0][...] = total[pl.ds(pl.multiple_of(core * half, half), half), :]
        other = total[pl.ds(pl.multiple_of((1 - core) * half, half), half), :]
        outs[1][...] = other.astype(BF16)
    else:
        outs[0][...] = total[...]


def gradients(k, v, rate, one, three, two, after, n):
    count, width = k.shape
    hid = one.shape[1]
    split = n > 1 and power_of_two(n)
    assert hid == width
    rows = 3 * hid
    parts = 2 if split else 1
    return pl.pallas_call(
        functools.partial(grads_kernel, n, split),
        out_shape=[
            jax.ShapeDtypeStruct((rows // parts, width), kind) for kind in (F32, BF16)[:parts]
        ],
        in_specs=full(6) + [pl.BlockSpec(memory_space=pl.ANY)],
        out_specs=full(parts),
        scratch_shapes=[pltpu.VMEM((rows, width), F32)],
        compiler_params=params(),
        cost_estimate=cost(12 * count * width * hid, 8 * count * width, count * hid),
        name="gradients",
    )(k, v, rate, one, three, two, after)


def merge_kernel(keep_ref, got_ref, *rest):
    rest[-1][...] = keep_ref[...] + got_ref[...].astype(F32)


def merge(keep, got, after):
    return pl.pallas_call(
        merge_kernel,
        out_shape=jax.ShapeDtypeStruct(keep.shape, F32),
        in_specs=full(2) + [pl.BlockSpec(memory_space=pl.ANY)] * len(after),
        out_specs=pl.BlockSpec(memory_space=pltpu.VMEM),
        compiler_params=params(),
        cost_estimate=cost(keep.size, 12 * keep.size),
        name="merge",
    )(keep, got, *after)


def core_step(parts, after, n):
    if len(parts) == 1:
        return parts[0]
    pair = [(at, at ^ 1) for at in range(n)]
    return merge(parts[0], lax.ppermute(parts[1], "cam", pair), after)


def sum_over_chips(mine, split, after, n):
    if not split:
        return [lax.psum(mine, "cam")]
    span = n.bit_length() - 2
    for step in range(span):
        pairs = []
        for at in range(n):
            bit = 1 + (step + (at & 1)) % span
            pairs.append((at, at ^ (1 << bit)))
        got = lax.ppermute(mine.astype(BF16), "cam", pairs)
        if step < len(after):
            mine = merge(mine, got, after[step])
        else:
            mine = mine + got.astype(F32)
    return [mine, lax.ppermute(mine, "cam", [(at, at ^ 1) for at in range(n)])]


def readout_kernel(parts, q_ref, one_ref, three_ref, two_ref, *rest):
    grads, (y_ref, sq_ref, total, fresh) = rest[:parts], rest[-4:]
    hid, width = one_ref.shape[1:]
    if parts == 2:
        half = total.shape[0] // 2
        core = lax.axis_index("cam") & 1
        total[pl.ds(pl.multiple_of(core * half, half), half), :] = grads[0][...]
        total[pl.ds(pl.multiple_of((1 - core) * half, half), half), :] = grads[1][...]
    else:
        total[...] = grads[0][...]
    entries = hid * width
    for which, ref in enumerate((one_ref, three_ref, two_ref)):
        grad = total[which * hid : (which + 1) * hid, :]
        weight = ref[0].astype(F32)
        row_sq = jnp.sum(weight * weight, axis=1, keepdims=True)
        weight_sq = jnp.sum(row_sq, axis=0, keepdims=True)
        grad_sq = jnp.sum(jnp.sum(grad * grad, axis=1, keepdims=True), axis=0, keepdims=True)
        scale = jnp.sqrt(weight_sq / entries) / jnp.sqrt(grad_sq / entries + EPSILON)
        moved = weight - scale * grad
        ratio = jnp.sqrt(row_sq) / jnp.sqrt(
            jnp.sum(moved * moved, axis=1, keepdims=True) + EPSILON
        )
        fresh[which * hid : (which + 1) * hid, :] = (moved * ratio).astype(BF16)
    count = q_ref.shape[0]
    tile = min(count, TILE)
    ones = jnp.ones((8, width), BF16)
    for start in range(0, count, tile):
        here = slice(start, start + tile)
        q = q_ref[here, :]
        h_one = dot_bt(q, fresh[0:hid, :])
        h_three = dot_bt(q, fresh[hid : 2 * hid, :])
        active = (h_one * jax.nn.sigmoid(h_one) * h_three).astype(BF16)
        y = dot_bt(active, fresh[2 * hid :, :])
        y_ref[here, :] = y
        square = y * y
        high = square.astype(BF16)
        low = (square - high.astype(F32)).astype(BF16)
        sq_ref[:, here] = (dot_bt(ones, high) + dot_bt(ones, low))[0:1, :]


def read_out(q, one, three, two, grads, after):
    count, width = q.shape
    hid = one.shape[1]
    parts = len(grads)
    return pl.pallas_call(
        functools.partial(readout_kernel, parts),
        out_shape=[
            jax.ShapeDtypeStruct((count, width), F32),
            jax.ShapeDtypeStruct((1, count), F32),
        ],
        in_specs=full(4 + parts) + [pl.BlockSpec(memory_space=pl.ANY)] * len(after),
        out_specs=full(2),
        scratch_shapes=[pltpu.VMEM((3 * hid, width), F32), pltpu.VMEM((3 * hid, width), BF16)],
        compiler_params=params(),
        cost_estimate=cost(6 * count * width * hid, 8 * count * width, count * hid),
        name="read_out",
    )(q, one, three, two, *grads, *after)


def place_kernel(n, steps, order_ref, *outs):
    me = lax.axis_index("cam")
    count = order_ref.shape[1]
    rows = count // n
    size = len(steps) * rows
    at = lax.broadcasted_iota(jnp.int32, (8, size), 1)
    slots = at * 0
    for which, step in enumerate(steps):
        inside = jnp.logical_and(at >= which * rows, at < (which + 1) * rows)
        slots = jnp.where(inside, peer(me, step, n) * rows + at - which * rows, slots)
    slots = slots[0:1, :].astype(F32)
    split = outs[0].shape[1]
    for low in range(0, count, LANES):
        wanted = column(order_ref[:, low : low + LANES].astype(F32))
        for lane in range(0, size, LANES):
            hit = wanted == slots[:, lane : lane + LANES]
            out = outs[0] if lane < split else outs[1]
            start = lane if lane < split else lane - split
            out[low : low + LANES, start : start + LANES] = hit.astype(F32).astype(BF16)


def place(order, n, early, late):
    count = order.shape[1]
    rows = count // n
    shapes = [jax.ShapeDtypeStruct((count, len(each) * rows), BF16) for each in (early, late)]
    return pl.pallas_call(
        functools.partial(place_kernel, n, (*early, *late)),
        out_shape=shapes,
        in_specs=full(1),
        out_specs=full(2),
        compiler_params=params(),
        cost_estimate=cost(count * count, 2 * count * count),
        name="place",
    )(order)


def gathered(onehot, here, blocks):
    rows = blocks[0].shape[0]
    total = None
    for at, block in enumerate(blocks):
        part = dot(onehot[here, at * rows : (at + 1) * rows], block[...])
        total = part if total is None else total + part
    return total


def base_kernel(heads, gain_ref, y_ref, onehot, total_ref, *rest):
    blocks, out_ref = rest[:-1], rest[-1]
    count, width = y_ref.shape
    inverse = 1.0 / jnp.sqrt(total_ref[...] / (width * heads) + EPSILON)
    gain = gain_ref[...]
    tile = min(count, TILE)
    for low in range(0, count, tile):
        part = gathered(onehot, slice(low, low + tile), blocks)
        for at in range(0, tile, LANES):
            here = slice(low + at, low + at + LANES)
            norm = column(inverse[:, here])
            norm = jnp.concatenate([norm] * (width // LANES), axis=1)
            out_ref[here, :] = y_ref[here, :] * norm * gain + part[at : at + LANES]


def base(gain, y, onehot, total, heads, blocks):
    count, width = y.shape
    moved = len(blocks) * blocks[0].shape[0]
    return pl.pallas_call(
        functools.partial(base_kernel, heads),
        out_shape=jax.ShapeDtypeStruct((count, width), F32),
        in_specs=full(4 + len(blocks)),
        out_specs=pl.BlockSpec(memory_space=pltpu.VMEM),
        compiler_params=params(),
        cost_estimate=cost(2 * count * moved * width, 8 * count * width),
        name="base",
    )(gain, y, onehot, total, *blocks)


def mix_kernel(base_ref, onehot, *rest):
    blocks, (out_ref, held, sems) = rest[:-3], rest[-3:]
    count = base_ref.shape[0]
    tile = min(count, TILE)
    copies = []
    for at in range(count // tile):
        here = slice(at * tile, (at + 1) * tile)
        held[here, :] = (base_ref[here, :] + gathered(onehot, here, blocks)).astype(BF16)
        copies += fetch([(held.at[here], out_ref.at[here])], sems.at[at : at + 1])
    for copy in copies:
        copy.wait()


def mix(given, onehot, blocks):
    count, width = given.shape
    moved = len(blocks) * blocks[0].shape[0]
    tile = min(count, TILE)
    return pl.pallas_call(
        mix_kernel,
        out_shape=jax.ShapeDtypeStruct((count, width), BF16),
        in_specs=full(2 + len(blocks)),
        out_specs=pl.BlockSpec(memory_space=pltpu.HBM),
        scratch_shapes=[
            pltpu.VMEM((count, width), BF16),
            pltpu.SemaphoreType.DMA((count // tile,)),
        ],
        compiler_params=params(),
        cost_estimate=cost(2 * count * moved * width, 8 * count * width),
        name="mix",
    )(given, onehot, *blocks)


def head_steps(heads):
    return heads.bit_length() - 1 if power_of_two(heads) else 0


def head_sum(square, heads, low, high):
    if head_steps(heads) == 0:
        return square if low else lax.psum(square, "head")
    for step in range(low, high):
        pairs = [(at, at ^ (1 << step)) for at in range(heads)]
        got = lax.ppermute(square, "head", pairs)
        square = square + got
    return square


def exchange(block, step, n):
    return lax.ppermute(block, "cam", routes(step, n)) if step else block


def give_back(block, step, n):
    pairs = [(target, at) for at, target in routes(step, n)]
    return lax.ppermute(block, "cam", pairs) if step else block


def per_device(queries, keys, values, rates, w_one, w_three, w_two, gain, order):
    count, width = queries.shape
    n = lax.axis_size("cam")
    heads = lax.axis_size("head")
    steps = far_first(n)
    few = max(1, n // 4)
    weights = (w_one, w_three, w_two)
    groups = (tuple(steps[:few]), tuple(steps[few : 2 * few]), tuple(steps[2 * few :]))
    marks = mark(order, n, groups)
    arrived = {}
    tokens = []
    for group, onehot in zip(groups, marks):
        blocks = sort_tokens(onehot, queries, keys, values, [], n)
        tokens.append(blocks[-1])
        for step, block in zip(group, blocks):
            arrived[step] = exchange(block, step, n)
    came = [arrived[step] for step in steps]
    parts = gradients(keys, values, rates.reshape(1, count), *weights, tokens[0], n)
    early = steps[: 2 * few] + steps[n - few :]
    late = steps[2 * few : n - few]
    early_places, late_places = place(order, n, early, late)
    mine = core_step(parts, [came[0]], n)
    summed = sum_over_chips(mine, len(parts) == 2, [tokens[1:2], came[1:3] + tokens[2:] + [late_places]], n)
    y, square = read_out(queries, *weights, summed, came[3:4])
    half = head_steps(heads) // 2
    square = head_sum(square, heads, 0, half)
    total = head_sum(square, heads, half, head_steps(heads))
    blocks = [arrived[step] for step in range(n)]
    returned = {}
    for chosen, after in ((steps[: n // 2], square), (steps[n // 2 :], total)):
        for step, block in zip(chosen, attend(blocks, chosen, [after], n, width)):
            returned[step] = give_back(block, step, n)
    given = base(
        gain.reshape(1, width), y, early_places, total, heads, [returned[step] for step in early]
    )
    return mix(given, late_places, [returned[step] for step in late])


def solution(mesh):
    in_specs = (
        P("cam", "head"),
        P("cam", "head"),
        P("cam", "head"),
        P("cam", "head"),
        P("head", None, None),
        P("head", None, None),
        P("head", None, None),
        P("head"),
        P("cam", None),
    )
    out_specs = P("cam", "head")
    return jax.shard_map(
        per_device, mesh=mesh, in_specs=in_specs, out_specs=out_specs, check_vma=False
    )
```

```python
import functools

import jax
import jax.numpy as jnp
from jax import lax
from jax.experimental import pallas as pl
from jax.experimental.pallas import tpu as pltpu
from jax.sharding import PartitionSpec as P

PATCHES = 32
EPSILON = 1e-06
LANES = 128
TILE = 512
LIMIT = 24
COST = 1
FIRST_COST = pl.CostEstimate(flops=10**12, bytes_accessed=1024, transcendentals=0)
MIB = 1024 * 1024
F32 = jnp.float32
BF16 = jnp.bfloat16
TOKEN = jax.ShapeDtypeStruct((8, LANES), F32)


def dot(a, b):
    return lax.dot_general(a, b, (((1,), (0,)), ((), ())), preferred_element_type=F32)


def dot_bt(a, b):
    return lax.dot_general(a, b, (((1,), (1,)), ((), ())), preferred_element_type=F32)


def dot_at(a, b):
    return lax.dot_general(a, b, (((0,), (0,)), ((), ())), preferred_element_type=F32)


def params(limit=LIMIT):
    return pltpu.CompilerParams(vmem_limit_bytes=int(limit * MIB))


def full(count):
    return [pl.BlockSpec(memory_space=pltpu.VMEM)] * count


def cost(flops, moved, exps=0):
    return pl.CostEstimate(
        flops=int(flops) // COST,
        bytes_accessed=int(moved) // COST,
        transcendentals=int(exps) // COST,
    )


def power_of_two(n):
    return n & (n - 1) == 0


def crossed(step):
    return (step & ~6) | ((step & 2) << 1) | ((step & 4) >> 1)


def peer(me, step, n):
    if power_of_two(n):
        if n < 8:
            return me ^ step
        odd = me & 1
        return me ^ (step * (1 - odd) + crossed(step) * odd)
    ahead = me + step
    wrap = ahead - n
    return wrap * (wrap >= 0) + ahead * (wrap < 0)


def routes(step, n):
    return [(at, int(peer(at, step, n))) for at in range(n)]


def column(row):
    return jnp.broadcast_to(row, (LANES, LANES)).T


def far_first(n):
    return sorted(range(n), key=lambda step: (-(step >> 1).bit_count(), -step))


def fetch(pairs, sems):
    copies = []
    for at, (source, target) in enumerate(pairs):
        copies.append(pltpu.make_async_copy(source, target, sems.at[at]))
        copies[-1].start()
    return copies


def mark_kernel(n, steps, order_ref, *rest):
    outs, token = rest[:-1], rest[-1]
    token[...] = jnp.zeros_like(token)
    me = lax.axis_index("cam")
    count = order_ref.shape[1]
    rows = count // n
    order = order_ref[...]
    slot = lax.broadcasted_iota(jnp.int32, (rows, count), 0)
    for group, out in zip(steps, outs):
        for at, step in enumerate(group):
            hit = slot + peer(me, step, n) * rows == order
            out[at * rows : (at + 1) * rows, :] = hit.astype(F32).astype(BF16)


def mark(order, n, steps):
    count = order.shape[1]
    rows = count // n
    return pl.pallas_call(
        functools.partial(mark_kernel, n, steps),
        out_shape=[jax.ShapeDtypeStruct((len(group) * rows, count), BF16) for group in steps]
        + [TOKEN],
        in_specs=full(1),
        out_specs=full(len(steps) + 1),
        compiler_params=params(),
        cost_estimate=FIRST_COST,
        name="mark",
    )(order)


def sort_kernel(size, onehot, q_ref, k_ref, v_ref, *rest):
    outs, token = rest[-1 - size : -1], rest[-1]
    token[...] = jnp.zeros_like(token)
    rows, width = outs[0].shape[0], q_ref.shape[1]
    group = max(1, min(len(outs), TILE // rows))
    while len(outs) % group:
        group -= 1
    for first in range(0, len(outs), group):
        marks = onehot[first * rows : (first + group) * rows, :]
        for which, ref in enumerate((q_ref, k_ref, v_ref)):
            picked = dot(marks, ref[...]).astype(BF16)
            for at in range(group):
                outs[first + at][:, which * width : (which + 1) * width] = picked[
                    at * rows : (at + 1) * rows
                ]


def sort_tokens(onehot, q, k, v, after, n):
    count, width = q.shape
    rows = count // n
    size = onehot.shape[0] // rows
    return pl.pallas_call(
        functools.partial(sort_kernel, size),
        out_shape=[jax.ShapeDtypeStruct((rows, 3 * width), BF16)] * size + [TOKEN],
        in_specs=full(4) + [pl.BlockSpec(memory_space=pl.ANY)] * len(after),
        out_specs=full(size + 1),
        compiler_params=params(),
        cost_estimate=cost(6 * size * rows * count * width, 6 * count * width),
        name="sort_tokens",
    )(onehot, q, k, v, *after)


def attend_kernel(n, scale, *refs):
    ins, outs = refs[:n], refs[-3 - n : -3]
    q_all, k_all, v_all = refs[-3:]
    rows = ins[0].shape[0]
    width = outs[0].shape[1]
    group = n * PATCHES
    block = min(group, 256)
    for stamp in range(rows // PATCHES):
        here = slice(stamp * PATCHES, (stamp + 1) * PATCHES)
        for cam in range(n):
            there = slice(cam * PATCHES, (cam + 1) * PATCHES)
            q_all[there, :] = ins[cam][here, 0:width]
            k_all[there, :] = ins[cam][here, width : 2 * width]
            v_all[there, :] = ins[cam][here, 2 * width : 3 * width]
        for low in range(0, group, block):
            scores = dot_bt(q_all[low : low + block, :], k_all[...]) * scale
            scores = scores - jnp.max(scores, axis=-1, keepdims=True)
            expo = jnp.exp(scores)
            probs = (expo / jnp.sum(expo, axis=-1, keepdims=True)).astype(BF16)
            result = dot(probs, v_all[...]).astype(BF16)
            for cam in range(low // PATCHES, (low + block) // PATCHES):
                at = cam * PATCHES - low
                outs[cam][here, :] = result[at : at + PATCHES]


def attend(blocks, after, n, width):
    rows = blocks[0].shape[0]
    group = n * PATCHES
    return pl.pallas_call(
        functools.partial(attend_kernel, n, width**-0.5),
        out_shape=[jax.ShapeDtypeStruct((rows, width), BF16)] * n,
        in_specs=full(n) + [pl.BlockSpec(memory_space=pl.ANY)] * len(after),
        out_specs=full(n),
        scratch_shapes=[pltpu.VMEM((group, width), BF16)] * 3,
        compiler_params=params(),
        cost_estimate=cost(
            4 * n * rows * group * width, 8 * n * rows * width, n * rows * group
        ),
        name="attend",
    )(*blocks, *after)


def grads_kernel(n, split, k_ref, v_ref, rate_ref, one_ref, three_ref, two_ref, *rest):
    outs, total = rest[1:-1], rest[-1]
    count, width = k_ref.shape
    hid = one_ref.shape[1]
    one, three, two = one_ref[0], three_ref[0], two_ref[0]
    tile = min(count, TILE)
    for start in range(0, count, tile):
        k = k_ref[start : start + tile, :]
        h_one = dot_bt(k, one)
        h_three = dot_bt(k, three)
        sigma = jax.nn.sigmoid(h_one)
        gated = h_one * sigma
        active = (gated * h_three).astype(BF16)
        pieces = []
        for low in range(start, start + tile, LANES):
            rate = column(rate_ref[:, low : low + LANES])
            rate = jnp.concatenate([rate] * (width // LANES), axis=1)
            pieces.append((-rate * v_ref[low : low + LANES, :].astype(F32)).astype(BF16))
        error = jnp.concatenate(pieces, axis=0)
        back = dot(error, two)
        back_one = (back * h_three * sigma * (1.0 + h_one * (1.0 - sigma))).astype(BF16)
        back_three = (back * gated).astype(BF16)
        sums = (dot_at(back_one, k), dot_at(back_three, k), dot_at(error, active))
        for which, term in enumerate(sums):
            here = slice(which * hid, (which + 1) * hid)
            total[here, :] = term if start == 0 else total[here, :] + term
    if split:
        half = total.shape[0] // 2
        core = lax.axis_index("cam") & 1
        outs[0][...] = total[pl.ds(pl.multiple_of(core * half, half), half), :]
        other = total[pl.ds(pl.multiple_of((1 - core) * half, half), half), :]
        outs[1][...] = other.astype(BF16)
    else:
        outs[0][...] = total[...]


def gradients(k, v, rate, one, three, two, after, n):
    count, width = k.shape
    hid = one.shape[1]
    split = n > 1 and power_of_two(n)
    assert hid == width
    rows = 3 * hid
    parts = 2 if split else 1
    return pl.pallas_call(
        functools.partial(grads_kernel, n, split),
        out_shape=[
            jax.ShapeDtypeStruct((rows // parts, width), kind) for kind in (F32, BF16)[:parts]
        ],
        in_specs=full(6) + [pl.BlockSpec(memory_space=pl.ANY)],
        out_specs=full(parts),
        scratch_shapes=[pltpu.VMEM((rows, width), F32)],
        compiler_params=params(),
        cost_estimate=cost(12 * count * width * hid, 8 * count * width, count * hid),
        name="gradients",
    )(k, v, rate, one, three, two, after)


def merge_kernel(keep_ref, got_ref, *rest):
    rest[-1][...] = keep_ref[...] + got_ref[...].astype(F32)


def merge(keep, got, after):
    return pl.pallas_call(
        merge_kernel,
        out_shape=jax.ShapeDtypeStruct(keep.shape, F32),
        in_specs=full(2) + [pl.BlockSpec(memory_space=pl.ANY)] * len(after),
        out_specs=pl.BlockSpec(memory_space=pltpu.VMEM),
        compiler_params=params(),
        cost_estimate=cost(keep.size, 12 * keep.size),
        name="merge",
    )(keep, got, *after)


def core_step(parts, after, n):
    if len(parts) == 1:
        return parts[0]
    pair = [(at, at ^ 1) for at in range(n)]
    return merge(parts[0], lax.ppermute(parts[1], "cam", pair), after)


def sum_over_chips(mine, split, after, n):
    if not split:
        return [lax.psum(mine, "cam")]
    span = n.bit_length() - 2
    for step in range(span):
        pairs = []
        for at in range(n):
            bit = 1 + (step + (at & 1)) % span
            pairs.append((at, at ^ (1 << bit)))
        got = lax.ppermute(mine.astype(BF16), "cam", pairs)
        if step < len(after):
            mine = merge(mine, got, after[step])
        else:
            mine = mine + got.astype(F32)
    return [mine, lax.ppermute(mine, "cam", [(at, at ^ 1) for at in range(n)])]


def readout_kernel(parts, q_ref, one_ref, three_ref, two_ref, *rest):
    grads, (y_ref, sq_ref, total, fresh) = rest[:parts], rest[-4:]
    hid, width = one_ref.shape[1:]
    if parts == 2:
        half = total.shape[0] // 2
        core = lax.axis_index("cam") & 1
        total[pl.ds(pl.multiple_of(core * half, half), half), :] = grads[0][...]
        total[pl.ds(pl.multiple_of((1 - core) * half, half), half), :] = grads[1][...]
    else:
        total[...] = grads[0][...]
    entries = hid * width
    for which, ref in enumerate((one_ref, three_ref, two_ref)):
        grad = total[which * hid : (which + 1) * hid, :]
        weight = ref[0].astype(F32)
        row_sq = jnp.sum(weight * weight, axis=1, keepdims=True)
        weight_sq = jnp.sum(row_sq, axis=0, keepdims=True)
        grad_sq = jnp.sum(jnp.sum(grad * grad, axis=1, keepdims=True), axis=0, keepdims=True)
        scale = jnp.sqrt(weight_sq / entries) / jnp.sqrt(grad_sq / entries + EPSILON)
        moved = weight - scale * grad
        ratio = jnp.sqrt(row_sq) / jnp.sqrt(
            jnp.sum(moved * moved, axis=1, keepdims=True) + EPSILON
        )
        fresh[which * hid : (which + 1) * hid, :] = (moved * ratio).astype(BF16)
    count = q_ref.shape[0]
    tile = min(count, TILE)
    ones = jnp.ones((8, width), BF16)
    for start in range(0, count, tile):
        here = slice(start, start + tile)
        q = q_ref[here, :]
        h_one = dot_bt(q, fresh[0:hid, :])
        h_three = dot_bt(q, fresh[hid : 2 * hid, :])
        active = (h_one * jax.nn.sigmoid(h_one) * h_three).astype(BF16)
        y = dot_bt(active, fresh[2 * hid :, :])
        y_ref[here, :] = y
        square = y * y
        high = square.astype(BF16)
        low = (square - high.astype(F32)).astype(BF16)
        sq_ref[:, here] = (dot_bt(ones, high) + dot_bt(ones, low))[0:1, :]


def read_out(q, one, three, two, grads, after):
    count, width = q.shape
    hid = one.shape[1]
    parts = len(grads)
    return pl.pallas_call(
        functools.partial(readout_kernel, parts),
        out_shape=[
            jax.ShapeDtypeStruct((count, width), F32),
            jax.ShapeDtypeStruct((1, count), F32),
        ],
        in_specs=full(4 + parts) + [pl.BlockSpec(memory_space=pl.ANY)] * len(after),
        out_specs=full(2),
        scratch_shapes=[pltpu.VMEM((3 * hid, width), F32), pltpu.VMEM((3 * hid, width), BF16)],
        compiler_params=params(),
        cost_estimate=cost(6 * count * width * hid, 8 * count * width, count * hid),
        name="read_out",
    )(q, one, three, two, *grads, *after)


def place_kernel(n, steps, order_ref, *outs):
    me = lax.axis_index("cam")
    count = order_ref.shape[1]
    rows = count // n
    size = len(steps) * rows
    at = lax.broadcasted_iota(jnp.int32, (8, size), 1)
    slots = at * 0
    for which, step in enumerate(steps):
        inside = jnp.logical_and(at >= which * rows, at < (which + 1) * rows)
        slots = jnp.where(inside, peer(me, step, n) * rows + at - which * rows, slots)
    slots = slots[0:1, :].astype(F32)
    split = outs[0].shape[1]
    for low in range(0, count, LANES):
        wanted = column(order_ref[:, low : low + LANES].astype(F32))
        for lane in range(0, size, LANES):
            hit = wanted == slots[:, lane : lane + LANES]
            out = outs[0] if lane < split else outs[1]
            start = lane if lane < split else lane - split
            out[low : low + LANES, start : start + LANES] = hit.astype(F32).astype(BF16)


def place(order, n, early, late):
    count = order.shape[1]
    rows = count // n
    shapes = [jax.ShapeDtypeStruct((count, len(each) * rows), BF16) for each in (early, late)]
    return pl.pallas_call(
        functools.partial(place_kernel, n, (*early, *late)),
        out_shape=shapes,
        in_specs=full(1),
        out_specs=full(2),
        compiler_params=params(),
        cost_estimate=cost(count * count, 2 * count * count),
        name="place",
    )(order)


def gathered(onehot, here, blocks):
    rows = blocks[0].shape[0]
    total = None
    for at, block in enumerate(blocks):
        part = dot(onehot[here, at * rows : (at + 1) * rows], block[...])
        total = part if total is None else total + part
    return total


def base_kernel(heads, gain_ref, y_ref, onehot, total_ref, *rest):
    blocks, out_ref = rest[:-1], rest[-1]
    count, width = y_ref.shape
    inverse = 1.0 / jnp.sqrt(total_ref[...] / (width * heads) + EPSILON)
    gain = gain_ref[...]
    tile = min(count, TILE)
    for low in range(0, count, tile):
        part = gathered(onehot, slice(low, low + tile), blocks)
        for at in range(0, tile, LANES):
            here = slice(low + at, low + at + LANES)
            norm = column(inverse[:, here])
            norm = jnp.concatenate([norm] * (width // LANES), axis=1)
            out_ref[here, :] = y_ref[here, :] * norm * gain + part[at : at + LANES]


def base(gain, y, onehot, total, heads, blocks):
    count, width = y.shape
    moved = len(blocks) * blocks[0].shape[0]
    return pl.pallas_call(
        functools.partial(base_kernel, heads),
        out_shape=jax.ShapeDtypeStruct((count, width), F32),
        in_specs=full(4 + len(blocks)),
        out_specs=pl.BlockSpec(memory_space=pltpu.VMEM),
        compiler_params=params(),
        cost_estimate=cost(2 * count * moved * width, 8 * count * width),
        name="base",
    )(gain, y, onehot, total, *blocks)


def mix_kernel(base_ref, onehot, *rest):
    blocks, (out_ref, held, sems) = rest[:-3], rest[-3:]
    count = base_ref.shape[0]
    tile = min(count, TILE)
    copies = []
    for at in range(count // tile):
        here = slice(at * tile, (at + 1) * tile)
        held[here, :] = (base_ref[here, :] + gathered(onehot, here, blocks)).astype(BF16)
        copies += fetch([(held.at[here], out_ref.at[here])], sems.at[at : at + 1])
    for copy in copies:
        copy.wait()


def mix(given, onehot, blocks):
    count, width = given.shape
    moved = len(blocks) * blocks[0].shape[0]
    tile = min(count, TILE)
    return pl.pallas_call(
        mix_kernel,
        out_shape=jax.ShapeDtypeStruct((count, width), BF16),
        in_specs=full(2 + len(blocks)),
        out_specs=pl.BlockSpec(memory_space=pltpu.HBM),
        scratch_shapes=[
            pltpu.VMEM((count, width), BF16),
            pltpu.SemaphoreType.DMA((count // tile,)),
        ],
        compiler_params=params(),
        cost_estimate=cost(2 * count * moved * width, 8 * count * width),
        name="mix",
    )(given, onehot, *blocks)


def head_steps(heads):
    return heads.bit_length() - 1 if power_of_two(heads) else 0


def head_sum(square, heads, low, high):
    if head_steps(heads) == 0:
        return square if low else lax.psum(square, "head")
    for step in range(low, high):
        pairs = [(at, at ^ (1 << step)) for at in range(heads)]
        got = lax.ppermute(square, "head", pairs)
        square = square + got
    return square


def pass_on_kernel(size, *refs):
    for source, target in zip(refs[:size], refs[size + 1 :]):
        target[...] = source[...]


def pass_on(blocks, after):
    size = len(blocks)
    return pl.pallas_call(
        functools.partial(pass_on_kernel, size),
        out_shape=[jax.ShapeDtypeStruct(block.shape, block.dtype) for block in blocks],
        in_specs=full(size) + [pl.BlockSpec(memory_space=pl.ANY)],
        out_specs=full(size),
        compiler_params=params(),
        cost_estimate=cost(0, 4 * size * blocks[0].size),
        name="pass_on",
    )(*blocks, after)


def exchange(block, step, n):
    return lax.ppermute(block, "cam", routes(step, n)) if step else block


def give_back(block, step, n):
    pairs = [(target, at) for at, target in routes(step, n)]
    return lax.ppermute(block, "cam", pairs) if step else block


def per_device(queries, keys, values, rates, w_one, w_three, w_two, gain, order):
    count, width = queries.shape
    n = lax.axis_size("cam")
    heads = lax.axis_size("head")
    steps = far_first(n)
    few = max(1, n // 4)
    weights = (w_one, w_three, w_two)
    groups = (tuple(steps[:few]), tuple(steps[few : 2 * few]), tuple(steps[2 * few :]))
    marks = mark(order, n, groups)
    arrived = {}
    tokens = []
    for group, onehot in zip(groups, marks):
        blocks = sort_tokens(onehot, queries, keys, values, [], n)
        tokens.append(blocks[-1])
        for step, block in zip(group, blocks):
            arrived[step] = exchange(block, step, n)
    came = [arrived[step] for step in steps]
    parts = gradients(keys, values, rates.reshape(1, count), *weights, tokens[0], n)
    early = steps[: 2 * few] + steps[n - few :]
    late = steps[2 * few : n - few]
    early_places, late_places = place(order, n, early, late)
    mine = core_step(parts, [came[0]], n)
    summed = sum_over_chips(mine, len(parts) == 2, [tokens[1:2], came[1:3] + tokens[2:] + [late_places]], n)
    y, square = read_out(queries, *weights, summed, came[3:4])
    half = head_steps(heads) // 2
    square = head_sum(square, heads, 0, half)
    total = head_sum(square, heads, half, head_steps(heads))
    blocks = [arrived[step] for step in range(n)]
    attended = attend(blocks, [square], n, width)
    later = pass_on([attended[step] for step in steps[n // 2 :]], total)
    attended = dict(zip(steps, [attended[step] for step in steps[: n // 2]] + list(later)))
    returned = {step: give_back(attended[step], step, n) for step in steps}
    given = base(
        gain.reshape(1, width), y, early_places, total, heads, [returned[step] for step in early]
    )
    return mix(given, late_places, [returned[step] for step in late])


def solution(mesh):
    in_specs = (
        P("cam", "head"),
        P("cam", "head"),
        P("cam", "head"),
        P("cam", "head"),
        P("head", None, None),
        P("head", None, None),
        P("head", None, None),
        P("head"),
        P("cam", None),
    )
    out_specs = P("cam", "head")
    return jax.shard_map(
        per_device, mesh=mesh, in_specs=in_specs, out_specs=out_specs, check_vma=False
    )
```

```python
import functools

import jax
import jax.numpy as jnp
from jax import lax
from jax.experimental import pallas as pl
from jax.experimental.pallas import tpu as pltpu
from jax.sharding import PartitionSpec as P

PATCHES = 32
EPSILON = 1e-06
LANES = 128
TILE = 512
LIMIT = 24
COST = 1
FIRST_COST = pl.CostEstimate(flops=10**12, bytes_accessed=1024, transcendentals=0)
MIB = 1024 * 1024
F32 = jnp.float32
BF16 = jnp.bfloat16
TOKEN = jax.ShapeDtypeStruct((8, LANES), F32)


def dot(a, b):
    return lax.dot_general(a, b, (((1,), (0,)), ((), ())), preferred_element_type=F32)


def dot_bt(a, b):
    return lax.dot_general(a, b, (((1,), (1,)), ((), ())), preferred_element_type=F32)


def dot_at(a, b):
    return lax.dot_general(a, b, (((0,), (0,)), ((), ())), preferred_element_type=F32)


def params(limit=LIMIT):
    return pltpu.CompilerParams(vmem_limit_bytes=int(limit * MIB))


def full(count):
    return [pl.BlockSpec(memory_space=pltpu.VMEM)] * count


def cost(flops, moved, exps=0):
    return pl.CostEstimate(
        flops=int(flops) // COST,
        bytes_accessed=int(moved) // COST,
        transcendentals=int(exps) // COST,
    )


def power_of_two(n):
    return n & (n - 1) == 0


def crossed(step):
    return (step & ~6) | ((step & 2) << 1) | ((step & 4) >> 1)


def peer(me, step, n):
    if power_of_two(n):
        if n < 8:
            return me ^ step
        odd = me & 1
        return me ^ (step * (1 - odd) + crossed(step) * odd)
    ahead = me + step
    wrap = ahead - n
    return wrap * (wrap >= 0) + ahead * (wrap < 0)


def routes(step, n):
    return [(at, int(peer(at, step, n))) for at in range(n)]


def column(row):
    return jnp.broadcast_to(row, (LANES, LANES)).T


def far_first(n):
    return sorted(range(n), key=lambda step: (-(step >> 1).bit_count(), -step))


def fetch(pairs, sems):
    copies = []
    for at, (source, target) in enumerate(pairs):
        copies.append(pltpu.make_async_copy(source, target, sems.at[at]))
        copies[-1].start()
    return copies


def mark_kernel(n, steps, order_ref, *rest):
    outs, token = rest[:-1], rest[-1]
    token[...] = jnp.zeros_like(token)
    me = lax.axis_index("cam")
    count = order_ref.shape[1]
    rows = count // n
    order = order_ref[...]
    slot = lax.broadcasted_iota(jnp.int32, (rows, count), 0)
    for group, out in zip(steps, outs):
        for at, step in enumerate(group):
            hit = slot + peer(me, step, n) * rows == order
            out[at * rows : (at + 1) * rows, :] = hit.astype(F32).astype(BF16)


def mark(order, n, steps):
    count = order.shape[1]
    rows = count // n
    return pl.pallas_call(
        functools.partial(mark_kernel, n, steps),
        out_shape=[jax.ShapeDtypeStruct((len(group) * rows, count), BF16) for group in steps]
        + [TOKEN],
        in_specs=full(1),
        out_specs=full(len(steps) + 1),
        compiler_params=params(),
        cost_estimate=FIRST_COST,
        name="mark",
    )(order)


def sort_kernel(size, onehot, q_ref, k_ref, v_ref, *rest):
    outs, token = rest[-1 - size : -1], rest[-1]
    token[...] = jnp.zeros_like(token)
    rows, width = outs[0].shape[0], q_ref.shape[1]
    group = max(1, min(len(outs), TILE // rows))
    while len(outs) % group:
        group -= 1
    for first in range(0, len(outs), group):
        marks = onehot[first * rows : (first + group) * rows, :]
        for which, ref in enumerate((q_ref, k_ref, v_ref)):
            picked = dot(marks, ref[...]).astype(BF16)
            for at in range(group):
                outs[first + at][:, which * width : (which + 1) * width] = picked[
                    at * rows : (at + 1) * rows
                ]


def sort_tokens(onehot, q, k, v, after, n):
    count, width = q.shape
    rows = count // n
    size = onehot.shape[0] // rows
    return pl.pallas_call(
        functools.partial(sort_kernel, size),
        out_shape=[jax.ShapeDtypeStruct((rows, 3 * width), BF16)] * size + [TOKEN],
        in_specs=full(4) + [pl.BlockSpec(memory_space=pl.ANY)] * len(after),
        out_specs=full(size + 1),
        compiler_params=params(),
        cost_estimate=cost(6 * size * rows * count * width, 6 * count * width),
        name="sort_tokens",
    )(onehot, q, k, v, *after)


def attend_kernel(n, scale, *refs):
    ins, outs = refs[:n], refs[-3 - n : -3]
    q_all, k_all, v_all = refs[-3:]
    rows = ins[0].shape[0]
    width = outs[0].shape[1]
    group = n * PATCHES
    block = min(group, 256)
    for stamp in range(rows // PATCHES):
        here = slice(stamp * PATCHES, (stamp + 1) * PATCHES)
        for cam in range(n):
            there = slice(cam * PATCHES, (cam + 1) * PATCHES)
            q_all[there, :] = ins[cam][here, 0:width]
            k_all[there, :] = ins[cam][here, width : 2 * width]
            v_all[there, :] = ins[cam][here, 2 * width : 3 * width]
        for low in range(0, group, block):
            scores = dot_bt(q_all[low : low + block, :], k_all[...]) * scale
            scores = scores - jnp.max(scores, axis=-1, keepdims=True)
            expo = jnp.exp(scores)
            probs = (expo / jnp.sum(expo, axis=-1, keepdims=True)).astype(BF16)
            result = dot(probs, v_all[...]).astype(BF16)
            for cam in range(low // PATCHES, (low + block) // PATCHES):
                at = cam * PATCHES - low
                outs[cam][here, :] = result[at : at + PATCHES]


def attend(blocks, after, n, width):
    rows = blocks[0].shape[0]
    group = n * PATCHES
    return pl.pallas_call(
        functools.partial(attend_kernel, n, width**-0.5),
        out_shape=[jax.ShapeDtypeStruct((rows, width), BF16)] * n,
        in_specs=full(n) + [pl.BlockSpec(memory_space=pl.ANY)] * len(after),
        out_specs=full(n),
        scratch_shapes=[pltpu.VMEM((group, width), BF16)] * 3,
        compiler_params=params(),
        cost_estimate=cost(
            4 * n * rows * group * width, 8 * n * rows * width, n * rows * group
        ),
        name="attend",
    )(*blocks, *after)


def grads_kernel(n, split, k_ref, v_ref, rate_ref, one_ref, three_ref, two_ref, *rest):
    outs, total = rest[1:-1], rest[-1]
    count, width = k_ref.shape
    hid = one_ref.shape[1]
    one, three, two = one_ref[0], three_ref[0], two_ref[0]
    tile = min(count, TILE)
    for start in range(0, count, tile):
        k = k_ref[start : start + tile, :]
        h_one = dot_bt(k, one)
        h_three = dot_bt(k, three)
        sigma = jax.nn.sigmoid(h_one)
        gated = h_one * sigma
        active = (gated * h_three).astype(BF16)
        pieces = []
        for low in range(start, start + tile, LANES):
            rate = column(rate_ref[:, low : low + LANES])
            rate = jnp.concatenate([rate] * (width // LANES), axis=1)
            pieces.append((-rate * v_ref[low : low + LANES, :].astype(F32)).astype(BF16))
        error = jnp.concatenate(pieces, axis=0)
        back = dot(error, two)
        back_one = (back * h_three * sigma * (1.0 + h_one * (1.0 - sigma))).astype(BF16)
        back_three = (back * gated).astype(BF16)
        sums = (dot_at(back_one, k), dot_at(back_three, k), dot_at(error, active))
        for which, term in enumerate(sums):
            here = slice(which * hid, (which + 1) * hid)
            total[here, :] = term if start == 0 else total[here, :] + term
    if split:
        half = total.shape[0] // 2
        core = lax.axis_index("cam") & 1
        outs[0][...] = total[pl.ds(pl.multiple_of(core * half, half), half), :]
        other = total[pl.ds(pl.multiple_of((1 - core) * half, half), half), :]
        outs[1][...] = other.astype(BF16)
    else:
        outs[0][...] = total[...]


def gradients(k, v, rate, one, three, two, after, n):
    count, width = k.shape
    hid = one.shape[1]
    split = n > 1 and power_of_two(n)
    assert hid == width
    rows = 3 * hid
    parts = 2 if split else 1
    return pl.pallas_call(
        functools.partial(grads_kernel, n, split),
        out_shape=[
            jax.ShapeDtypeStruct((rows // parts, width), kind) for kind in (F32, BF16)[:parts]
        ],
        in_specs=full(6) + [pl.BlockSpec(memory_space=pl.ANY)],
        out_specs=full(parts),
        scratch_shapes=[pltpu.VMEM((rows, width), F32)],
        compiler_params=params(),
        cost_estimate=cost(12 * count * width * hid, 8 * count * width, count * hid),
        name="gradients",
    )(k, v, rate, one, three, two, after)


def merge_kernel(keep_ref, got_ref, *rest):
    rest[-1][...] = keep_ref[...] + got_ref[...].astype(F32)


def merge(keep, got, after):
    return pl.pallas_call(
        merge_kernel,
        out_shape=jax.ShapeDtypeStruct(keep.shape, F32),
        in_specs=full(2) + [pl.BlockSpec(memory_space=pl.ANY)] * len(after),
        out_specs=pl.BlockSpec(memory_space=pltpu.VMEM),
        compiler_params=params(),
        cost_estimate=cost(keep.size, 12 * keep.size),
        name="merge",
    )(keep, got, *after)


def core_step(parts, after, n):
    if len(parts) == 1:
        return parts[0]
    pair = [(at, at ^ 1) for at in range(n)]
    return merge(parts[0], lax.ppermute(parts[1], "cam", pair), after)


def sum_over_chips(mine, split, after, n):
    if not split:
        return [lax.psum(mine, "cam")]
    span = n.bit_length() - 2
    for step in range(span):
        pairs = []
        for at in range(n):
            bit = 1 + (step + (at & 1)) % span
            pairs.append((at, at ^ (1 << bit)))
        got = lax.ppermute(mine.astype(BF16), "cam", pairs)
        if step < len(after):
            mine = merge(mine, got, after[step])
        else:
            mine = mine + got.astype(F32)
    return [mine, lax.ppermute(mine, "cam", [(at, at ^ 1) for at in range(n)])]


def readout_kernel(parts, q_ref, one_ref, three_ref, two_ref, *rest):
    grads, (y_ref, sq_ref, total, fresh) = rest[:parts], rest[-4:]
    hid, width = one_ref.shape[1:]
    if parts == 2:
        half = total.shape[0] // 2
        core = lax.axis_index("cam") & 1
        total[pl.ds(pl.multiple_of(core * half, half), half), :] = grads[0][...]
        total[pl.ds(pl.multiple_of((1 - core) * half, half), half), :] = grads[1][...]
    else:
        total[...] = grads[0][...]
    entries = hid * width
    for which, ref in enumerate((one_ref, three_ref, two_ref)):
        grad = total[which * hid : (which + 1) * hid, :]
        weight = ref[0].astype(F32)
        row_sq = jnp.sum(weight * weight, axis=1, keepdims=True)
        weight_sq = jnp.sum(row_sq, axis=0, keepdims=True)
        grad_sq = jnp.sum(jnp.sum(grad * grad, axis=1, keepdims=True), axis=0, keepdims=True)
        scale = jnp.sqrt(weight_sq / entries) / jnp.sqrt(grad_sq / entries + EPSILON)
        moved = weight - scale * grad
        ratio = jnp.sqrt(row_sq) / jnp.sqrt(
            jnp.sum(moved * moved, axis=1, keepdims=True) + EPSILON
        )
        fresh[which * hid : (which + 1) * hid, :] = (moved * ratio).astype(BF16)
    count = q_ref.shape[0]
    tile = min(count, TILE)
    ones = jnp.ones((8, width), BF16)
    for start in range(0, count, tile):
        here = slice(start, start + tile)
        q = q_ref[here, :]
        h_one = dot_bt(q, fresh[0:hid, :])
        h_three = dot_bt(q, fresh[hid : 2 * hid, :])
        active = (h_one * jax.nn.sigmoid(h_one) * h_three).astype(BF16)
        y = dot_bt(active, fresh[2 * hid :, :])
        y_ref[here, :] = y
        square = y * y
        high = square.astype(BF16)
        low = (square - high.astype(F32)).astype(BF16)
        sq_ref[:, here] = (dot_bt(ones, high) + dot_bt(ones, low))[0:1, :]


def read_out(q, one, three, two, grads, after):
    count, width = q.shape
    hid = one.shape[1]
    parts = len(grads)
    return pl.pallas_call(
        functools.partial(readout_kernel, parts),
        out_shape=[
            jax.ShapeDtypeStruct((count, width), F32),
            jax.ShapeDtypeStruct((1, count), F32),
        ],
        in_specs=full(4 + parts) + [pl.BlockSpec(memory_space=pl.ANY)] * len(after),
        out_specs=full(2),
        scratch_shapes=[pltpu.VMEM((3 * hid, width), F32), pltpu.VMEM((3 * hid, width), BF16)],
        compiler_params=params(),
        cost_estimate=cost(6 * count * width * hid, 8 * count * width, count * hid),
        name="read_out",
    )(q, one, three, two, *grads, *after)


def place_kernel(n, steps, order_ref, *outs):
    me = lax.axis_index("cam")
    count = order_ref.shape[1]
    rows = count // n
    size = len(steps) * rows
    at = lax.broadcasted_iota(jnp.int32, (8, size), 1)
    slots = at * 0
    for which, step in enumerate(steps):
        inside = jnp.logical_and(at >= which * rows, at < (which + 1) * rows)
        slots = jnp.where(inside, peer(me, step, n) * rows + at - which * rows, slots)
    slots = slots[0:1, :].astype(F32)
    split = outs[0].shape[1]
    for low in range(0, count, LANES):
        wanted = column(order_ref[:, low : low + LANES].astype(F32))
        for lane in range(0, size, LANES):
            hit = wanted == slots[:, lane : lane + LANES]
            out = outs[0] if lane < split else outs[1]
            start = lane if lane < split else lane - split
            out[low : low + LANES, start : start + LANES] = hit.astype(F32).astype(BF16)


def place(order, n, early, late):
    count = order.shape[1]
    rows = count // n
    shapes = [jax.ShapeDtypeStruct((count, len(each) * rows), BF16) for each in (early, late)]
    return pl.pallas_call(
        functools.partial(place_kernel, n, (*early, *late)),
        out_shape=shapes,
        in_specs=full(1),
        out_specs=full(2),
        compiler_params=params(),
        cost_estimate=cost(count * count, 2 * count * count),
        name="place",
    )(order)


def gathered(onehot, here, blocks):
    rows = blocks[0].shape[0]
    total = None
    for at, block in enumerate(blocks):
        part = dot(onehot[here, at * rows : (at + 1) * rows], block[...])
        total = part if total is None else total + part
    return total


def base_kernel(heads, gain_ref, y_ref, onehot, total_ref, *rest):
    blocks, out_ref = rest[:-1], rest[-1]
    count, width = y_ref.shape
    inverse = 1.0 / jnp.sqrt(total_ref[...] / (width * heads) + EPSILON)
    gain = gain_ref[...]
    tile = min(count, TILE)
    for low in range(0, count, tile):
        part = gathered(onehot, slice(low, low + tile), blocks)
        for at in range(0, tile, LANES):
            here = slice(low + at, low + at + LANES)
            norm = column(inverse[:, here])
            norm = jnp.concatenate([norm] * (width // LANES), axis=1)
            out_ref[here, :] = y_ref[here, :] * norm * gain + part[at : at + LANES]


def base(gain, y, onehot, total, heads, blocks):
    count, width = y.shape
    moved = len(blocks) * blocks[0].shape[0]
    return pl.pallas_call(
        functools.partial(base_kernel, heads),
        out_shape=jax.ShapeDtypeStruct((count, width), F32),
        in_specs=full(4 + len(blocks)),
        out_specs=pl.BlockSpec(memory_space=pltpu.VMEM),
        compiler_params=params(),
        cost_estimate=cost(2 * count * moved * width, 8 * count * width),
        name="base",
    )(gain, y, onehot, total, *blocks)


def mix_kernel(base_ref, onehot, *rest):
    blocks, (out_ref, held, sems) = rest[:-3], rest[-3:]
    count = base_ref.shape[0]
    tile = min(count, TILE)
    copies = []
    for at in range(count // tile):
        here = slice(at * tile, (at + 1) * tile)
        held[here, :] = (base_ref[here, :] + gathered(onehot, here, blocks)).astype(BF16)
        copies += fetch([(held.at[here], out_ref.at[here])], sems.at[at : at + 1])
    for copy in copies:
        copy.wait()


def mix(given, onehot, blocks):
    count, width = given.shape
    moved = len(blocks) * blocks[0].shape[0]
    tile = min(count, TILE)
    return pl.pallas_call(
        mix_kernel,
        out_shape=jax.ShapeDtypeStruct((count, width), BF16),
        in_specs=full(2 + len(blocks)),
        out_specs=pl.BlockSpec(memory_space=pltpu.HBM),
        scratch_shapes=[
            pltpu.VMEM((count, width), BF16),
            pltpu.SemaphoreType.DMA((count // tile,)),
        ],
        compiler_params=params(),
        cost_estimate=cost(2 * count * moved * width, 8 * count * width),
        name="mix",
    )(given, onehot, *blocks)


def head_steps(heads):
    return heads.bit_length() - 1 if power_of_two(heads) else 0


def head_sum(square, heads, low, high):
    if head_steps(heads) == 0:
        return square if low else lax.psum(square, "head")
    for step in range(low, high):
        pairs = [(at, at ^ (1 << step)) for at in range(heads)]
        got = lax.ppermute(square, "head", pairs)
        square = square + got
    return square


def pass_on_kernel(size, *refs):
    for source, target in zip(refs[:size], refs[size + 1 :]):
        target[...] = source[...]


def pass_on(blocks, after):
    size = len(blocks)
    return pl.pallas_call(
        functools.partial(pass_on_kernel, size),
        out_shape=[jax.ShapeDtypeStruct(block.shape, block.dtype) for block in blocks],
        in_specs=full(size) + [pl.BlockSpec(memory_space=pl.ANY)],
        out_specs=full(size),
        compiler_params=params(),
        cost_estimate=cost(0, 4 * size * blocks[0].size),
        name="pass_on",
    )(*blocks, after)


def exchange(block, step, n):
    return lax.ppermute(block, "cam", routes(step, n)) if step else block


def give_back(block, step, n):
    pairs = [(target, at) for at, target in routes(step, n)]
    return lax.ppermute(block, "cam", pairs) if step else block


def per_device(queries, keys, values, rates, w_one, w_three, w_two, gain, order):
    count, width = queries.shape
    n = lax.axis_size("cam")
    heads = lax.axis_size("head")
    steps = far_first(n)
    few = max(1, n // 4)
    weights = (w_one, w_three, w_two)
    groups = (tuple(steps[:few]), tuple(steps[few : 2 * few]), tuple(steps[2 * few :]))
    marks = mark(order, n, groups)
    arrived = {}
    tokens = []
    for group, onehot in zip(groups, marks):
        blocks = sort_tokens(onehot, queries, keys, values, [], n)
        tokens.append(blocks[-1])
        for step, block in zip(group, blocks):
            arrived[step] = exchange(block, step, n)
    came = [arrived[step] for step in steps]
    parts = gradients(keys, values, rates.reshape(1, count), *weights, tokens[0], n)
    early = steps[: 2 * few + 1] + steps[-1:]
    late = steps[2 * few + 1 : -1]
    early_places, late_places = place(order, n, early, late)
    mine = core_step(parts, [came[0]], n)
    summed = sum_over_chips(mine, len(parts) == 2, [tokens[1:2], came[1:3] + tokens[2:] + [late_places]], n)
    y, square = read_out(queries, *weights, summed, came[3:4])
    half = head_steps(heads) // 2
    square = head_sum(square, heads, 0, half)
    total = head_sum(square, heads, half, head_steps(heads))
    blocks = [arrived[step] for step in range(n)]
    attended = attend(blocks, [square], n, width)
    later = pass_on([attended[step] for step in steps[n // 2 :]], total)
    attended = dict(zip(steps, [attended[step] for step in steps[: n // 2]] + list(later)))
    returned = {step: give_back(attended[step], step, n) for step in steps}
    given = base(
        gain.reshape(1, width), y, early_places, total, heads, [returned[step] for step in early]
    )
    return mix(given, late_places, [returned[step] for step in late])


def solution(mesh):
    in_specs = (
        P("cam", "head"),
        P("cam", "head"),
        P("cam", "head"),
        P("cam", "head"),
        P("head", None, None),
        P("head", None, None),
        P("head", None, None),
        P("head"),
        P("cam", None),
    )
    out_specs = P("cam", "head")
    return jax.shard_map(
        per_device, mesh=mesh, in_specs=in_specs, out_specs=out_specs, check_vma=False
    )
```

```python
import functools

import jax
import jax.numpy as jnp
from jax import lax
from jax.experimental import pallas as pl
from jax.experimental.pallas import tpu as pltpu
from jax.sharding import PartitionSpec as P

PATCHES = 32
EPSILON = 1e-06
LANES = 128
TILE = 512
LIMIT = 24
COST = 1
FIRST_COST = pl.CostEstimate(flops=10**12, bytes_accessed=1024, transcendentals=0)
MIB = 1024 * 1024
F32 = jnp.float32
BF16 = jnp.bfloat16
TOKEN = jax.ShapeDtypeStruct((8, LANES), F32)


def dot(a, b):
    return lax.dot_general(a, b, (((1,), (0,)), ((), ())), preferred_element_type=F32)


def dot_bt(a, b):
    return lax.dot_general(a, b, (((1,), (1,)), ((), ())), preferred_element_type=F32)


def dot_at(a, b):
    return lax.dot_general(a, b, (((0,), (0,)), ((), ())), preferred_element_type=F32)


def params(limit=LIMIT):
    return pltpu.CompilerParams(vmem_limit_bytes=int(limit * MIB))


def full(count):
    return [pl.BlockSpec(memory_space=pltpu.VMEM)] * count


def cost(flops, moved, exps=0):
    return pl.CostEstimate(
        flops=int(flops) // COST,
        bytes_accessed=int(moved) // COST,
        transcendentals=int(exps) // COST,
    )


def power_of_two(n):
    return n & (n - 1) == 0


def crossed(step):
    return (step & ~6) | ((step & 2) << 1) | ((step & 4) >> 1)


def peer(me, step, n):
    if power_of_two(n):
        if n < 8:
            return me ^ step
        odd = me & 1
        return me ^ (step * (1 - odd) + crossed(step) * odd)
    ahead = me + step
    wrap = ahead - n
    return wrap * (wrap >= 0) + ahead * (wrap < 0)


def routes(step, n):
    return [(at, int(peer(at, step, n))) for at in range(n)]


def column(row):
    return jnp.broadcast_to(row, (LANES, LANES)).T


def far_first(n):
    return sorted(range(n), key=lambda step: (-(step >> 1).bit_count(), -step))


def fetch(pairs, sems):
    copies = []
    for at, (source, target) in enumerate(pairs):
        copies.append(pltpu.make_async_copy(source, target, sems.at[at]))
        copies[-1].start()
    return copies


def mark_kernel(n, steps, order_ref, *rest):
    outs, token = rest[:-1], rest[-1]
    token[...] = jnp.zeros_like(token)
    me = lax.axis_index("cam")
    count = order_ref.shape[1]
    rows = count // n
    order = order_ref[...]
    slot = lax.broadcasted_iota(jnp.int32, (rows, count), 0)
    for group, out in zip(steps, outs):
        for at, step in enumerate(group):
            hit = slot + peer(me, step, n) * rows == order
            out[at * rows : (at + 1) * rows, :] = hit.astype(F32).astype(BF16)


def mark(order, n, steps):
    count = order.shape[1]
    rows = count // n
    return pl.pallas_call(
        functools.partial(mark_kernel, n, steps),
        out_shape=[jax.ShapeDtypeStruct((len(group) * rows, count), BF16) for group in steps]
        + [TOKEN],
        in_specs=full(1),
        out_specs=full(len(steps) + 1),
        compiler_params=params(),
        cost_estimate=FIRST_COST,
        name="mark",
    )(order)


def sort_kernel(size, onehot, q_ref, k_ref, v_ref, *rest):
    outs, token = rest[-1 - size : -1], rest[-1]
    token[...] = jnp.zeros_like(token)
    rows, width = outs[0].shape[0], q_ref.shape[1]
    group = max(1, min(len(outs), TILE // rows))
    while len(outs) % group:
        group -= 1
    for first in range(0, len(outs), group):
        marks = onehot[first * rows : (first + group) * rows, :]
        for which, ref in enumerate((q_ref, k_ref, v_ref)):
            picked = dot(marks, ref[...]).astype(BF16)
            for at in range(group):
                outs[first + at][:, which * width : (which + 1) * width] = picked[
                    at * rows : (at + 1) * rows
                ]


def sort_tokens(onehot, q, k, v, after, n):
    count, width = q.shape
    rows = count // n
    size = onehot.shape[0] // rows
    return pl.pallas_call(
        functools.partial(sort_kernel, size),
        out_shape=[jax.ShapeDtypeStruct((rows, 3 * width), BF16)] * size + [TOKEN],
        in_specs=full(4) + [pl.BlockSpec(memory_space=pl.ANY)] * len(after),
        out_specs=full(size + 1),
        compiler_params=params(),
        cost_estimate=cost(6 * size * rows * count * width, 6 * count * width),
        name="sort_tokens",
    )(onehot, q, k, v, *after)


def attend_kernel(n, scale, *refs):
    ins, outs = refs[:n], refs[-3 - n : -3]
    q_all, k_all, v_all = refs[-3:]
    rows = ins[0].shape[0]
    width = outs[0].shape[1]
    group = n * PATCHES
    block = min(group, 256)
    for stamp in range(rows // PATCHES):
        here = slice(stamp * PATCHES, (stamp + 1) * PATCHES)
        for cam in range(n):
            there = slice(cam * PATCHES, (cam + 1) * PATCHES)
            q_all[there, :] = ins[cam][here, 0:width]
            k_all[there, :] = ins[cam][here, width : 2 * width]
            v_all[there, :] = ins[cam][here, 2 * width : 3 * width]
        for low in range(0, group, block):
            scores = dot_bt(q_all[low : low + block, :], k_all[...]) * scale
            scores = scores - jnp.max(scores, axis=-1, keepdims=True)
            expo = jnp.exp(scores)
            probs = (expo / jnp.sum(expo, axis=-1, keepdims=True)).astype(BF16)
            result = dot(probs, v_all[...]).astype(BF16)
            for cam in range(low // PATCHES, (low + block) // PATCHES):
                at = cam * PATCHES - low
                outs[cam][here, :] = result[at : at + PATCHES]


def attend(blocks, after, n, width):
    rows = blocks[0].shape[0]
    group = n * PATCHES
    return pl.pallas_call(
        functools.partial(attend_kernel, n, width**-0.5),
        out_shape=[jax.ShapeDtypeStruct((rows, width), BF16)] * n,
        in_specs=full(n) + [pl.BlockSpec(memory_space=pl.ANY)] * len(after),
        out_specs=full(n),
        scratch_shapes=[pltpu.VMEM((group, width), BF16)] * 3,
        compiler_params=params(),
        cost_estimate=cost(
            4 * n * rows * group * width, 8 * n * rows * width, n * rows * group
        ),
        name="attend",
    )(*blocks, *after)


def grads_kernel(n, split, k_ref, v_ref, rate_ref, one_ref, three_ref, two_ref, *rest):
    outs, total = rest[1:-1], rest[-1]
    count, width = k_ref.shape
    hid = one_ref.shape[1]
    one, three, two = one_ref[0], three_ref[0], two_ref[0]
    tile = min(count, TILE)
    for start in range(0, count, tile):
        k = k_ref[start : start + tile, :]
        h_one = dot_bt(k, one)
        h_three = dot_bt(k, three)
        sigma = jax.nn.sigmoid(h_one)
        gated = h_one * sigma
        active = (gated * h_three).astype(BF16)
        pieces = []
        for low in range(start, start + tile, LANES):
            rate = column(rate_ref[:, low : low + LANES])
            rate = jnp.concatenate([rate] * (width // LANES), axis=1)
            pieces.append((-rate * v_ref[low : low + LANES, :].astype(F32)).astype(BF16))
        error = jnp.concatenate(pieces, axis=0)
        back = dot(error, two)
        back_one = (back * h_three * sigma * (1.0 + h_one * (1.0 - sigma))).astype(BF16)
        back_three = (back * gated).astype(BF16)
        sums = (dot_at(back_one, k), dot_at(back_three, k), dot_at(error, active))
        for which, term in enumerate(sums):
            here = slice(which * hid, (which + 1) * hid)
            total[here, :] = term if start == 0 else total[here, :] + term
    if split:
        half = total.shape[0] // 2
        core = lax.axis_index("cam") & 1
        outs[0][...] = total[pl.ds(pl.multiple_of(core * half, half), half), :]
        other = total[pl.ds(pl.multiple_of((1 - core) * half, half), half), :]
        outs[1][...] = other.astype(BF16)
    else:
        outs[0][...] = total[...]


def gradients(k, v, rate, one, three, two, after, n):
    count, width = k.shape
    hid = one.shape[1]
    split = n > 1 and power_of_two(n)
    assert hid == width
    rows = 3 * hid
    parts = 2 if split else 1
    return pl.pallas_call(
        functools.partial(grads_kernel, n, split),
        out_shape=[
            jax.ShapeDtypeStruct((rows // parts, width), kind) for kind in (F32, BF16)[:parts]
        ],
        in_specs=full(6) + [pl.BlockSpec(memory_space=pl.ANY)],
        out_specs=full(parts),
        scratch_shapes=[pltpu.VMEM((rows, width), F32)],
        compiler_params=params(),
        cost_estimate=cost(12 * count * width * hid, 8 * count * width, count * hid),
        name="gradients",
    )(k, v, rate, one, three, two, after)


def merge_kernel(keep_ref, got_ref, *rest):
    rest[-1][...] = keep_ref[...] + got_ref[...].astype(F32)


def merge(keep, got, after):
    return pl.pallas_call(
        merge_kernel,
        out_shape=jax.ShapeDtypeStruct(keep.shape, F32),
        in_specs=full(2) + [pl.BlockSpec(memory_space=pl.ANY)] * len(after),
        out_specs=pl.BlockSpec(memory_space=pltpu.VMEM),
        compiler_params=params(),
        cost_estimate=cost(keep.size, 12 * keep.size),
        name="merge",
    )(keep, got, *after)


def core_step(parts, after, n):
    if len(parts) == 1:
        return parts[0]
    pair = [(at, at ^ 1) for at in range(n)]
    return merge(parts[0], lax.ppermute(parts[1], "cam", pair), after)


def sum_over_chips(mine, split, after, n):
    if not split:
        return [lax.psum(mine, "cam")]
    span = n.bit_length() - 2
    for step in range(span):
        pairs = []
        for at in range(n):
            bit = 1 + (step + (at & 1)) % span
            pairs.append((at, at ^ (1 << bit)))
        got = lax.ppermute(mine.astype(BF16), "cam", pairs)
        if step < len(after):
            mine = merge(mine, got, after[step])
        else:
            mine = mine + got.astype(F32)
    return [mine, lax.ppermute(mine.astype(BF16), "cam", [(at, at ^ 1) for at in range(n)])]


def readout_kernel(parts, q_ref, one_ref, three_ref, two_ref, *rest):
    grads, (y_ref, sq_ref, total, fresh) = rest[:parts], rest[-4:]
    hid, width = one_ref.shape[1:]
    if parts == 2:
        half = total.shape[0] // 2
        core = lax.axis_index("cam") & 1
        total[pl.ds(pl.multiple_of(core * half, half), half), :] = grads[0][...]
        total[pl.ds(pl.multiple_of((1 - core) * half, half), half), :] = grads[1][...].astype(F32)
    else:
        total[...] = grads[0][...]
    entries = hid * width
    for which, ref in enumerate((one_ref, three_ref, two_ref)):
        grad = total[which * hid : (which + 1) * hid, :]
        weight = ref[0].astype(F32)
        row_sq = jnp.sum(weight * weight, axis=1, keepdims=True)
        weight_sq = jnp.sum(row_sq, axis=0, keepdims=True)
        grad_sq = jnp.sum(jnp.sum(grad * grad, axis=1, keepdims=True), axis=0, keepdims=True)
        scale = jnp.sqrt(weight_sq / entries) / jnp.sqrt(grad_sq / entries + EPSILON)
        moved = weight - scale * grad
        ratio = jnp.sqrt(row_sq) / jnp.sqrt(
            jnp.sum(moved * moved, axis=1, keepdims=True) + EPSILON
        )
        fresh[which * hid : (which + 1) * hid, :] = (moved * ratio).astype(BF16)
    count = q_ref.shape[0]
    tile = min(count, TILE)
    ones = jnp.ones((8, width), BF16)
    for start in range(0, count, tile):
        here = slice(start, start + tile)
        q = q_ref[here, :]
        h_one = dot_bt(q, fresh[0:hid, :])
        h_three = dot_bt(q, fresh[hid : 2 * hid, :])
        active = (h_one * jax.nn.sigmoid(h_one) * h_three).astype(BF16)
        y = dot_bt(active, fresh[2 * hid :, :])
        y_ref[here, :] = y
        square = y * y
        high = square.astype(BF16)
        low = (square - high.astype(F32)).astype(BF16)
        sq_ref[:, here] = (dot_bt(ones, high) + dot_bt(ones, low))[0:1, :]


def read_out(q, one, three, two, grads, after):
    count, width = q.shape
    hid = one.shape[1]
    parts = len(grads)
    return pl.pallas_call(
        functools.partial(readout_kernel, parts),
        out_shape=[
            jax.ShapeDtypeStruct((count, width), F32),
            jax.ShapeDtypeStruct((1, count), F32),
        ],
        in_specs=full(4 + parts) + [pl.BlockSpec(memory_space=pl.ANY)] * len(after),
        out_specs=full(2),
        scratch_shapes=[pltpu.VMEM((3 * hid, width), F32), pltpu.VMEM((3 * hid, width), BF16)],
        compiler_params=params(),
        cost_estimate=cost(6 * count * width * hid, 8 * count * width, count * hid),
        name="read_out",
    )(q, one, three, two, *grads, *after)


def place_kernel(n, steps, order_ref, *outs):
    me = lax.axis_index("cam")
    count = order_ref.shape[1]
    rows = count // n
    size = len(steps) * rows
    at = lax.broadcasted_iota(jnp.int32, (8, size), 1)
    slots = at * 0
    for which, step in enumerate(steps):
        inside = jnp.logical_and(at >= which * rows, at < (which + 1) * rows)
        slots = jnp.where(inside, peer(me, step, n) * rows + at - which * rows, slots)
    slots = slots[0:1, :].astype(F32)
    split = outs[0].shape[1]
    for low in range(0, count, LANES):
        wanted = column(order_ref[:, low : low + LANES].astype(F32))
        for lane in range(0, size, LANES):
            hit = wanted == slots[:, lane : lane + LANES]
            out = outs[0] if lane < split else outs[1]
            start = lane if lane < split else lane - split
            out[low : low + LANES, start : start + LANES] = hit.astype(F32).astype(BF16)


def place(order, n, early, late):
    count = order.shape[1]
    rows = count // n
    shapes = [jax.ShapeDtypeStruct((count, len(each) * rows), BF16) for each in (early, late)]
    return pl.pallas_call(
        functools.partial(place_kernel, n, (*early, *late)),
        out_shape=shapes,
        in_specs=full(1),
        out_specs=full(2),
        compiler_params=params(),
        cost_estimate=cost(count * count, 2 * count * count),
        name="place",
    )(order)


def gathered(onehot, here, blocks):
    rows = blocks[0].shape[0]
    total = None
    for at, block in enumerate(blocks):
        part = dot(onehot[here, at * rows : (at + 1) * rows], block[...])
        total = part if total is None else total + part
    return total


def base_kernel(heads, gain_ref, y_ref, onehot, total_ref, *rest):
    blocks, out_ref = rest[:-1], rest[-1]
    count, width = y_ref.shape
    inverse = 1.0 / jnp.sqrt(total_ref[...] / (width * heads) + EPSILON)
    gain = gain_ref[...]
    tile = min(count, TILE)
    for low in range(0, count, tile):
        part = gathered(onehot, slice(low, low + tile), blocks)
        for at in range(0, tile, LANES):
            here = slice(low + at, low + at + LANES)
            norm = column(inverse[:, here])
            norm = jnp.concatenate([norm] * (width // LANES), axis=1)
            out_ref[here, :] = y_ref[here, :] * norm * gain + part[at : at + LANES]


def base(gain, y, onehot, total, heads, blocks):
    count, width = y.shape
    moved = len(blocks) * blocks[0].shape[0]
    return pl.pallas_call(
        functools.partial(base_kernel, heads),
        out_shape=jax.ShapeDtypeStruct((count, width), F32),
        in_specs=full(4 + len(blocks)),
        out_specs=pl.BlockSpec(memory_space=pltpu.VMEM),
        compiler_params=params(),
        cost_estimate=cost(2 * count * moved * width, 8 * count * width),
        name="base",
    )(gain, y, onehot, total, *blocks)


def mix_kernel(base_ref, onehot, *rest):
    blocks, (out_ref, held, sems) = rest[:-3], rest[-3:]
    count = base_ref.shape[0]
    tile = min(count, TILE)
    copies = []
    for at in range(count // tile):
        here = slice(at * tile, (at + 1) * tile)
        held[here, :] = (base_ref[here, :] + gathered(onehot, here, blocks)).astype(BF16)
        copies += fetch([(held.at[here], out_ref.at[here])], sems.at[at : at + 1])
    for copy in copies:
        copy.wait()


def mix(given, onehot, blocks):
    count, width = given.shape
    moved = len(blocks) * blocks[0].shape[0]
    tile = min(count, TILE)
    return pl.pallas_call(
        mix_kernel,
        out_shape=jax.ShapeDtypeStruct((count, width), BF16),
        in_specs=full(2 + len(blocks)),
        out_specs=pl.BlockSpec(memory_space=pltpu.HBM),
        scratch_shapes=[
            pltpu.VMEM((count, width), BF16),
            pltpu.SemaphoreType.DMA((count // tile,)),
        ],
        compiler_params=params(),
        cost_estimate=cost(2 * count * moved * width, 8 * count * width),
        name="mix",
    )(given, onehot, *blocks)


def head_steps(heads):
    return heads.bit_length() - 1 if power_of_two(heads) else 0


def head_sum(square, heads, low, high):
    if head_steps(heads) == 0:
        return square if low else lax.psum(square, "head")
    for step in range(low, high):
        pairs = [(at, at ^ (1 << step)) for at in range(heads)]
        got = lax.ppermute(square, "head", pairs)
        square = square + got
    return square


def pass_on_kernel(size, *refs):
    for source, target in zip(refs[:size], refs[size + 1 :]):
        target[...] = source[...]


def pass_on(blocks, after):
    size = len(blocks)
    return pl.pallas_call(
        functools.partial(pass_on_kernel, size),
        out_shape=[jax.ShapeDtypeStruct(block.shape, block.dtype) for block in blocks],
        in_specs=full(size) + [pl.BlockSpec(memory_space=pl.ANY)],
        out_specs=full(size),
        compiler_params=params(),
        cost_estimate=cost(0, 4 * size * blocks[0].size),
        name="pass_on",
    )(*blocks, after)


def exchange(block, step, n):
    return lax.ppermute(block, "cam", routes(step, n)) if step else block


def give_back(block, step, n):
    pairs = [(target, at) for at, target in routes(step, n)]
    return lax.ppermute(block, "cam", pairs) if step else block


def per_device(queries, keys, values, rates, w_one, w_three, w_two, gain, order):
    count, width = queries.shape
    n = lax.axis_size("cam")
    heads = lax.axis_size("head")
    steps = far_first(n)
    few = max(1, n // 4)
    weights = (w_one, w_three, w_two)
    groups = (tuple(steps[:few]), tuple(steps[few : 2 * few]), tuple(steps[2 * few :]))
    marks = mark(order, n, groups)
    arrived = {}
    tokens = []
    for group, onehot in zip(groups, marks):
        blocks = sort_tokens(onehot, queries, keys, values, [], n)
        tokens.append(blocks[-1])
        for step, block in zip(group, blocks):
            arrived[step] = exchange(block, step, n)
    came = [arrived[step] for step in steps]
    parts = gradients(keys, values, rates.reshape(1, count), *weights, tokens[0], n)
    early = steps[: 2 * few] + steps[n - few :]
    late = steps[2 * few : n - few]
    early_places, late_places = place(order, n, early, late)
    mine = core_step(parts, [came[0]], n)
    summed = sum_over_chips(mine, len(parts) == 2, [tokens[1:2], came[1:3] + tokens[2:] + [late_places]], n)
    y, square = read_out(queries, *weights, summed, came[3:4])
    half = head_steps(heads) // 2
    square = head_sum(square, heads, 0, half)
    total = head_sum(square, heads, half, head_steps(heads))
    blocks = [arrived[step] for step in range(n)]
    attended = attend(blocks, [square], n, width)
    later = pass_on([attended[step] for step in steps[n // 2 :]], total)
    attended = dict(zip(steps, [attended[step] for step in steps[: n // 2]] + list(later)))
    returned = {step: give_back(attended[step], step, n) for step in steps}
    given = base(
        gain.reshape(1, width), y, early_places, total, heads, [returned[step] for step in early]
    )
    return mix(given, late_places, [returned[step] for step in late])


def solution(mesh):
    in_specs = (
        P("cam", "head"),
        P("cam", "head"),
        P("cam", "head"),
        P("cam", "head"),
        P("head", None, None),
        P("head", None, None),
        P("head", None, None),
        P("head"),
        P("cam", None),
    )
    out_specs = P("cam", "head")
    return jax.shard_map(
        per_device, mesh=mesh, in_specs=in_specs, out_specs=out_specs, check_vma=False
    )
```
